256 devices in a mesh: seq: 32 (over y_lo, z, core), tp: 8 (over y_hi, x).
Axes of the slice: x: 4, y: 4 (y_hi: 2, y_lo: 2; y = y_hi * 2 + y_lo), z: 8, core: 2. Of those that a mesh axis runs over, the one named last changes fastest.
Arguments:
- layer_input: bfloat16 [16384, 1792], P('seq'), may hold values from -6 to 6
- grad_output: bfloat16 [16384, 1792], P('seq'), may hold values from -6 to 6
- tile_image: int32 [128], replicated, may hold values from 0 to 127, as said below
- qkv_weight: bfloat16 [1792, 3, 1792], P('seq', None, 'tp'), may hold values from -0.125 to 0.125
- out_weight: bfloat16 [1792, 1792], P('seq', 'tp'), may hold values from -0.125 to 0.125
Outputs:
- grad_input: bfloat16 [16384, 1792], P('seq')
- qkv_grad: float32 [1792, 3, 1792], P('seq', None, 'tp')
- out_grad: float32 [1792, 1792], P('seq', 'tp')
The draws below stay inside these ranges and needn't reach their ends.
Inputs may be any that keep to these rules, and one draw needn't show every extreme that they name: `tile_image`: each image covers 1 to 4 consecutive whole tiles, and one covers exactly 4; an image's number is the index of its first tile, so numbers never fall along the tiles and the last tile is an image of its own; every boundary between the tiles of two consecutive seq shards lies inside an image, which covers 1 or 2 tiles on each side of it.
All inputs are finite; a program needn't handle non-finite values.
Results may differ from the reference program's by a relative error of at most 0.025.
Values may be sent and summed in bfloat16 or wider, within the bound.
A program may use at most 64 MiB of HBM per device.

```python
import jax
import jax.numpy as jnp
from jax import lax

D = 1792
HEADS = 16
HD = 112
TILE = 128
MOST = 4
RIM = 384
TOK_DEV = 512
TOKENS = 16384
NTILES = 128


def draw_tile_image(key, part):
    per_shard = TOK_DEV // TILE
    shards = NTILES // per_shard
    key_before, key_after, key_extra = jax.random.split(key, 3)
    before = jax.random.randint(key_before, (shards + 1,), 1, 3, dtype=jnp.int32)
    after = jax.random.randint(key_after, (shards,), 1, 3, dtype=jnp.int32)
    before = before.at[1].set(2).at[shards].set(0)
    after = after.at[1].set(2).at[0].set(0)
    tiles = jnp.arange(NTILES, dtype=jnp.int32)
    shard_of = tiles // per_shard
    position = tiles % per_shard
    lower = after[shard_of]
    upper = per_shard - before[shard_of + 1]
    extra = jax.random.randint(key_extra, (NTILES,), 0, 3, dtype=jnp.int32) == 0
    in_gap = (position >= lower) & (position < upper)
    starts = (position == lower) | (position == upper) | in_gap & (((position - lower) % MOST == 0) | extra)
    starts = starts | (tiles == NTILES - 1)
    firsts = jnp.where(starts, tiles, jnp.zeros_like(tiles))
    return lax.cummax(firsts, axis=0).astype(jnp.int32)


def spiked(values, rng, source, target, shards_of, factor):
    def block_of(axis_at):
        return (jnp.arange(values.shape[axis_at]) // (values.shape[axis_at] // shards_of)).reshape((-1,) + (1,) * (values.ndim - 1 - axis_at))

    one_side = jax.random.permutation(rng, shards_of)[block_of(target)]
    other_side = (block_of(target) + shards_of // 2) % shards_of
    return jnp.where((block_of(source) == one_side) | (block_of(source) == other_side), factor * values, values)


def block_levels(stream_key, extent, pieces, least, largest):
    loudness = 1.0
    for axis_at, blocks in pieces:
        steps = jax.random.uniform(jax.random.fold_in(jax.random.fold_in(stream_key, 6), axis_at), (blocks,), jnp.float32, least / len(pieces), largest / len(pieces))
        loudness = loudness * jnp.repeat(jnp.exp(steps), extent[axis_at] // blocks).reshape((-1,) + (1,) * (len(extent) - 1 - axis_at))
    return loudness


def bell_draw(own_key, shape, spread, most, pieces=(), kind=jnp.bfloat16):
    array = jax.random.normal(own_key, shape, jnp.float32) * spread
    if len(pieces) > 0:
        array = block_levels(own_key, shape, pieces, -0.22, 0.18) * array
    return jnp.clip(array, min=-most, max=most).astype(kind)


def bell_draw_with(rng, extent, width, bound, cuts, heavy, kind=jnp.bfloat16):
    array = width * jax.random.normal(rng, extent, jnp.float32)
    if cuts:
        array = array * block_levels(rng, extent, cuts, -0.22, 0.18)
    return jnp.clip(spiked(array, jax.random.fold_in(rng, 3), *heavy), -bound, bound).astype(kind)


def setup_inputs(seed: int = 0) -> dict:
    seeds = jax.random.split(jax.random.key(seed), 6)
    return {
        "layer_input": bell_draw(seeds[0], (TOKENS, D), 1.0, 6.0, ((0, 32),)),
        "grad_output": bell_draw_with(seeds[1], (TOKENS, D), 1.0, 6.0, ((0, 32),), (0, 1, 32, 2.75)),
        "tile_image": draw_tile_image(jax.random.fold_in(seeds[5], 71), 0),
        "qkv_weight": bell_draw(seeds[3], (D, 3, D), D ** -0.5, 0.125, ((0, 32), (2, 8))),
        "out_weight": bell_draw(seeds[4], (D, D), D ** -0.5, 0.125, ((0, 32), (1, 8))),
    }


def attend_block(queries, key_rows, value_rows, upstream, query_ids, key_ids, factor):
    scores = jnp.einsum('qhd,khd->hqk', queries.astype(jnp.float32), key_rows.astype(jnp.float32)) * factor
    allowed = query_ids[:, None] == key_ids[None, :]
    exponent = jnp.where(allowed, jnp.exp(scores), 0.0)
    attn_prob = exponent / lax.optimization_barrier(jnp.sum(exponent, axis=-1, keepdims=True))
    prob_low = attn_prob.astype(jnp.bfloat16)
    attended = jnp.einsum('hqk,khd->qhd', prob_low.astype(jnp.float32), value_rows.astype(jnp.float32))
    up_float = upstream.astype(jnp.float32)
    dprob = jnp.einsum('qhd,khd->hqk', up_float, value_rows.astype(jnp.float32))
    row_delta = jnp.einsum('qhd,qhd->hq', up_float, attended)[:, :, None]
    dscore = (attn_prob * (dprob - row_delta) * factor).astype(jnp.bfloat16)
    dscore_f = dscore.astype(jnp.float32)
    dquery = jnp.einsum('hqk,khd->qhd', dscore_f, key_rows.astype(jnp.float32)).astype(jnp.bfloat16)
    dkey = jnp.einsum('hqk,qhd->khd', dscore_f, queries.astype(jnp.float32))
    dvalue = jnp.einsum('hqk,qhd->khd', prob_low.astype(jnp.float32), up_float)
    return (attended.astype(jnp.bfloat16), dquery, dkey, dvalue)

def reference(layer_input, grad_output, tile_image, qkv_weight, out_weight):
    widened = layer_input.astype(jnp.float32)
    center = widened - lax.optimization_barrier(jnp.mean(widened, axis=-1, keepdims=True))
    inv_std = lax.rsqrt(lax.optimization_barrier(jnp.mean(center * center, axis=-1, keepdims=True)) + 1e-06)
    normed = center * inv_std
    normed_low = normed.astype(jnp.bfloat16)
    projected = jnp.einsum('td,dce->cte', normed_low.astype(jnp.float32), qkv_weight.astype(jnp.float32)).astype(jnp.bfloat16)
    upstream = jnp.dot(grad_output, out_weight, preferred_element_type=jnp.float32).astype(jnp.bfloat16)
    query_heads = projected[0].reshape(TOKENS, HEADS, HD)
    key_pad = jnp.pad(projected[1].reshape(TOKENS, HEADS, HD), ((RIM, RIM), (0, 0), (0, 0)))
    value_pad = jnp.pad(projected[2].reshape(TOKENS, HEADS, HD), ((RIM, RIM), (0, 0), (0, 0)))
    up_heads = upstream.reshape(TOKENS, HEADS, HD)
    all_ids = jnp.repeat(jnp.pad(tile_image, (MOST - 1, MOST - 1), constant_values=-1), TILE)
    block_rows = min(TOK_DEV, 512)
    reach = block_rows + 2 * RIM
    factor = float(HD) ** (-0.5)

    def step(carry, block):
        grad_keys, grad_values = carry
        first = (block * block_rows).astype(jnp.int32)
        queries = lax.dynamic_slice_in_dim(query_heads, first, block_rows, 0)
        key_rows = lax.dynamic_slice_in_dim(key_pad, first, reach, 0)
        value_rows = lax.dynamic_slice_in_dim(value_pad, first, reach, 0)
        up_rows = lax.dynamic_slice_in_dim(up_heads, first, block_rows, 0)
        query_ids = lax.dynamic_slice_in_dim(all_ids, first + RIM, block_rows, 0)
        key_ids = lax.dynamic_slice_in_dim(all_ids, first, reach, 0)
        attended, dquery, dkey, dvalue = attend_block(queries, key_rows, value_rows, up_rows, query_ids, key_ids, factor)
        old_keys = lax.dynamic_slice_in_dim(grad_keys, first, reach, 0)
        old_values = lax.dynamic_slice_in_dim(grad_values, first, reach, 0)
        grad_keys = lax.dynamic_update_slice_in_dim(grad_keys, old_keys + dkey, first, 0)
        grad_values = lax.dynamic_update_slice_in_dim(grad_values, old_values + dvalue, first, 0)
        return ((grad_keys, grad_values), (attended, dquery))
    start_keys = jnp.zeros((TOKENS + 2 * RIM, HEADS, HD), jnp.float32)
    start_values = jnp.zeros((TOKENS + 2 * RIM, HEADS, HD), jnp.float32)
    (grad_keys, grad_values), (attended_all, dquery_all) = lax.scan(step, (start_keys, start_values), jnp.arange(TOKENS // block_rows, dtype=jnp.int32))
    attended_low = attended_all.reshape(TOKENS, D)
    dquery_low = dquery_all.reshape(TOKENS, D)
    dkey_low = grad_keys[RIM:RIM + TOKENS].reshape(TOKENS, D).astype(jnp.bfloat16)
    dvalue_low = grad_values[RIM:RIM + TOKENS].reshape(TOKENS, D).astype(jnp.bfloat16)
    grad_proj = jnp.stack([dquery_low, dkey_low, dvalue_low], axis=1)
    grad_float = grad_proj.astype(jnp.float32)
    qkv_grad = jnp.einsum('td,tce->dce', normed_low.astype(jnp.float32), grad_float)
    out_grad = jnp.dot(grad_output.T, attended_low, preferred_element_type=jnp.float32)
    grad_norm = jnp.einsum('tce,dce->td', grad_float, qkv_weight.astype(jnp.float32))
    grad_input = inv_std * (grad_norm - lax.optimization_barrier(jnp.mean(grad_norm, axis=-1, keepdims=True)) - normed * lax.optimization_barrier(jnp.mean(grad_norm * normed, axis=-1, keepdims=True)))
    return (grad_input.astype(jnp.bfloat16), qkv_grad, out_grad)
```

```python
import functools

import jax
import jax.numpy as jnp
from jax import lax
from jax.experimental import pallas as pl
from jax.experimental.pallas import tpu as pltpu
from jax.sharding import PartitionSpec as P

HD = 112
TILE = 128
LANES = 256
TOK = 512
D = 1792
CHIP_ROWS = 112
HALO = 256
PAD_TOK = TOK + 2 * HALO
WINDOW = 768
BLOCK = 64
FACTOR = float(HD) ** (-0.5)
F32 = jnp.float32
BF16 = jnp.bfloat16
MESH = pl.DeviceIdType.MESH
N_COPIES = 160

NT = (((1,), (1,)), ((), ()))


def dot(a, b):
    return jnp.dot(a, b, preferred_element_type=F32)


def dot_nt(a, b):
    return lax.dot_general(a, b, NT, preferred_element_type=F32)


class Sender:
    def __init__(self, send_sems, recv_sems):
        self.send_sems, self.recv_sems = send_sems, recv_sems
        self.copies = []

    def __call__(self, src, dst, device):
        index = len(self.copies)
        copy = pltpu.make_async_remote_copy(
            src_ref=src,
            dst_ref=dst,
            send_sem=self.send_sems.at[index],
            recv_sem=self.recv_sems.at[index],
            device_id=device,
            device_id_type=MESH,
        )
        copy.start()
        self.copies.append(copy)
        return copy

    def drain(self):
        for copy in self.copies:
            copy.wait_send()


def kernel(
    x_hbm,
    go_hbm,
    own_ref,
    ids_ref,
    gi_ref,
    og_ref,
    x_ref,
    go_ref,
    sib_ref,
    w_ref,
    xn_ref,
    stat_ref,
    xt_ref,
    got_ref,
    kp_ref,
    vp_ref,
    q_ref,
    u_ref,
    dk_ref,
    dv_ref,
    hs_ref,
    hr_ref,
    gp_ref,
    part_ref,
    ps_ref,
    rb_ref,
    ys_ref,
    yr_ref,
    fin_ref,
    fs_ref,
    fr_ref,
    gn_ref,
    tr_ref,
    send_sems,
    recv_sems,
    load_sems,
):
    seq = lax.axis_index("seq")
    tp = lax.axis_index("tp")
    core = lax.rem(seq, 2)
    z = lax.rem(seq // 2, 8)
    yl = seq // 16
    other = 1 - yl

    def at_z(offset):
        return lax.rem(z + 8 + offset, 8)

    def device(yl_, z_, core_):
        return (yl_ * 16 + z_ * 2 + core_, tp)

    sibling = device(yl, z, 1 - core)
    z_next = {1: device(yl, at_z(1), core), -1: device(yl, at_z(-1), core)}
    y_pair = device(other, z, core)
    following = (lax.rem(seq + 1, 32), tp)
    previous = (lax.rem(seq + 31, 32), tp)

    def tp_peer(d):
        return jnp.bitwise_xor(tp, d)

    load_x = pltpu.make_async_copy(x_hbm, x_ref, load_sems.at[0])
    load_go = pltpu.make_async_copy(go_hbm, go_ref, load_sems.at[1])
    load_x.start()
    load_go.start()

    barrier = pltpu.get_barrier_semaphore()
    peers = [sibling, z_next[1], z_next[-1], y_pair, following, previous]
    peers += [(seq, tp_peer(d)) for d in range(1, 8)]
    for peer in peers:
        pl.semaphore_signal(barrier, inc=1, device_id=peer, device_id_type=MESH)
    pl.semaphore_wait(barrier, len(peers))

    send = Sender(send_sems, recv_sems)
    groups = (core, 2 + core)

    to_sibling = send(own_ref, sib_ref, sibling)
    load_x.wait()

    def norm_rows(start, count):
        def body(i, _):
            rows = pl.ds(pl.multiple_of(start + i * 32, 32), 32)
            wide = x_ref[rows].astype(F32)
            mean = jnp.mean(wide, axis=-1, keepdims=True)
            center = wide - mean
            inv_std = lax.rsqrt(jnp.mean(center * center, axis=-1, keepdims=True) + 1e-06)
            xn_ref[rows] = (center * inv_std).astype(BF16)
            return 0

        lax.fori_loop(0, count // 32, body, 0)

    def transpose_rows(src, dst, start, count):
        for i in range(0, count, 128):
            dst[:, start + i : start + i + 128] = src[start + i : start + i + 128, :].T

    to_sibling.wait_recv()
    for g in range(4):
        mine = own_ref[g].astype(F32)
        theirs = sib_ref[g].astype(F32)
        low = jnp.where(core == 0, mine, theirs)
        high = jnp.where(core == 0, theirs, mine)
        w_ref[g, yl, z] = jnp.concatenate([low, high], axis=0).astype(BF16)

    ring = {}
    pair = {}
    for i in (0, 1):
        g = groups[i]
        block = w_ref.at[g, yl, z]
        for sign in (1, -1):
            ring[sign, 1, i, 0] = send(block, block, z_next[sign])
        pair[i] = send(block, block, y_pair)
    norm_rows(0, 256)
    beside = []
    for i in (0, 1):
        block = w_ref.at[groups[i], other, z]
        pair[i].wait_recv()
        for sign in (1, -1):
            ring[sign, 1, i, 1] = send(block, block, z_next[sign])
        beside.append(send(block, block, sibling))

    load_go.wait()
    between = {
        1: lambda: norm_rows(256, 256),
        2: lambda: transpose_rows(xn_ref, xt_ref, 0, 512),
        3: lambda: transpose_rows(go_ref, got_ref, 0, 512),
    }
    for t in (1, 2, 3, 4):
        for i in (0, 1):
            for side in (0, 1):
                for sign in (1, -1):
                    if (sign, t, i, side) not in ring:
                        continue
                    ring[sign, t, i, side].wait_recv()
                    block = w_ref.at[groups[i], (yl, other)[side], at_z(-sign * t)]
                    if t < 3 or (t == 3 and side == (0 if sign == 1 else 1)):
                        ring[sign, t + 1, i, side] = send(block, block, z_next[sign])
                    beside.append(send(block, block, sibling))
        if t in between:
            between[t]()
    for copy in beside:
        copy.wait_recv()

    def weights(g):
        return w_ref[g].reshape(D, LANES)

    halo = []
    for g, ref in ((0, kp_ref), (1, vp_ref)):
        ref[HALO : HALO + TOK] = dot(xn_ref[...], weights(g)).astype(BF16)
        halo.append(send(ref.at[pl.ds(HALO, HALO)], ref.at[pl.ds(HALO + TOK, HALO)], previous))
        halo.append(send(ref.at[pl.ds(TOK, HALO)], ref.at[pl.ds(0, HALO)], following))
    q_ref[...] = dot(xn_ref[...], weights(2)).astype(BF16)
    u_ref[...] = dot(go_ref[...], weights(3)).astype(BF16)

    def tile_id(tile):
        inside = jnp.logical_and(tile >= 0, tile < 128)
        value = ids_ref[jnp.clip(tile, 0, 127)]
        return jnp.where(inside, value, -1)

    key_ids = [tile_id(4 * seq - 2 + k) for k in range(8)]
    lane = lax.broadcasted_iota(jnp.int32, (1, 256), 1)
    for copy in halo:
        copy.wait_recv()

    for h in (0, 1):
        lanes = slice(128 * h, 128 * h + 128)
        key_t = kp_ref[:, lanes].T
        value_t = vp_ref[:, lanes].T
        for half in (0, 1):
            keys = slice(256 * half, 256 * half + WINDOW)
            rows = slice(256 * half, 256 * half + 256)
            query = q_ref[rows, lanes]
            up = u_ref[rows, lanes]
            key = kp_ref[keys, lanes]
            value = vp_ref[keys, lanes]
            scores = dot_nt(key, query) * FACTOR
            query_id = jnp.where(lane < 128, key_ids[2 + 2 * half], key_ids[3 + 2 * half])
            parts = []
            for k in range(6):
                allowed = query_id == key_ids[2 * half + k]
                parts.append(jnp.where(allowed, jnp.exp(scores[128 * k : 128 * k + 128]), 0.0))
            exponent = jnp.concatenate(parts, axis=0)
            prob = exponent * (1.0 / jnp.sum(exponent, axis=0, keepdims=True))
            prob_low = prob.astype(BF16)
            attended = dot(value_t[:, keys], prob_low)
            delta = jnp.sum(up.astype(F32).T * attended, axis=0, keepdims=True)
            dprob = dot_nt(value, up)
            dscore = (prob * (dprob - delta) * FACTOR).astype(BF16)
            dquery = dot(key_t[:, keys], dscore)
            gp_ref[2, rows, lanes] = dquery.T.astype(BF16)
            gp_ref[3, rows, lanes] = attended.T.astype(BF16)
            dkey = dot(dscore, query)
            dvalue = dot(prob_low, up)
            for ref, grad in ((dk_ref, dkey), (dv_ref, dvalue)):
                if half == 0:
                    ref[0:WINDOW, lanes] = grad
                else:
                    ref[256:WINDOW, lanes] += grad[: WINDOW - 256]
                    ref[WINDOW:PAD_TOK, lanes] = grad[WINDOW - 256 :]

    back = []
    for j, ref in ((0, dk_ref), (1, dv_ref)):
        hs_ref[j, 0] = ref[0:HALO].astype(BF16)
        hs_ref[j, 1] = ref[HALO + TOK : PAD_TOK].astype(BF16)
        back.append(send(hs_ref.at[j, 0], hr_ref.at[j, 0], previous))
        back.append(send(hs_ref.at[j, 1], hr_ref.at[j, 1], following))

    def weight_grad(g):
        src = got_ref if g == 3 else xt_ref

        def body(i, _):
            rows = pl.ds(pl.multiple_of(i * 896, 128), 896)
            part_ref[g, i] = dot(src[rows], gp_ref[g]).astype(BF16).reshape(8, CHIP_ROWS, LANES)
            return 0

        lax.fori_loop(0, 2, body, 0)

    weight_grad(2)
    weight_grad(3)
    swap = {1: send(part_ref.at[3 - core], ps_ref.at[1], sibling)}
    for copy in back:
        copy.wait_recv()
    for j, ref in ((0, dk_ref), (1, dv_ref)):
        gp_ref[j, 0:HALO] = (ref[HALO : 2 * HALO] + hr_ref[j, 1].astype(F32)).astype(BF16)
        gp_ref[j, HALO:TOK] = (ref[2 * HALO : 3 * HALO] + hr_ref[j, 0].astype(F32)).astype(BF16)

    for half in (0, 1):
        rows = slice(256 * half, 256 * half + 256)
        for y in (0, 1):
            total = dot_nt(gp_ref[0, rows], w_ref[0, y].reshape(896, LANES))
            total += dot_nt(gp_ref[1, rows], w_ref[1, y].reshape(896, LANES))
            total += dot_nt(gp_ref[2, rows], w_ref[2, y].reshape(896, LANES))
            gn_ref[rows, 896 * y : 896 * y + 896] = total.astype(BF16)
    scatter = []
    for d in range(1, 8):
        peer = tp_peer(d)
        block = gn_ref.at[pl.ds(pl.multiple_of(peer * BLOCK, BLOCK), BLOCK)]
        scatter.append(send(block, tr_ref.at[d - 1], (seq, peer)))

    weight_grad(0)
    weight_grad(1)
    swap[0] = send(part_ref.at[1 - core], ps_ref.at[0], sibling)

    for i in (1, 0):
        swap[i].wait_recv()
    chain = {}

    def ring_step(t):
        for i in (0, 1):
            g = groups[i]
            for side in (0, 1):
                y = (yl, other)[side]
                for sign in (1, -1):
                    if t == 4 and side != (0 if sign == 1 else 1):
                        continue
                    zz = at_z(sign * t)
                    total = part_ref[g, y, zz].astype(F32) + ps_ref[i, y, zz].astype(F32)
                    if (sign, t + 1, i, side) in chain:
                        chain[sign, t + 1, i, side].wait_recv()
                        total += rb_ref[(sign + 1) // 2, t, i, side].astype(F32)
                    part_ref[g, y, zz] = total.astype(BF16)
                    chain[sign, t, i, side] = send(
                        part_ref.at[g, y, zz],
                        rb_ref.at[(sign + 1) // 2, t - 1, i, side],
                        z_next[sign],
                    )

    ring_step(4)
    ring_step(3)
    ring_step(2)

    for copy in scatter:
        copy.wait_recv()
    mine = pl.ds(pl.multiple_of(tp * BLOCK, BLOCK), BLOCK)

    def norm_back(i, _):
        rows = pl.ds(pl.multiple_of(tp * BLOCK + i * 16, 16), 16)
        part = pl.ds(pl.multiple_of(i * 16, 16), 16)
        total = gn_ref[rows].astype(F32)
        for d in range(7):
            total += tr_ref[d, part].astype(F32)
        wide = x_ref[rows].astype(F32)
        center = wide - jnp.mean(wide, axis=-1, keepdims=True)
        inv_std = lax.rsqrt(jnp.mean(center * center, axis=-1, keepdims=True) + 1e-06)
        normed = center * inv_std
        grad = inv_std * (
            total
            - jnp.mean(total, axis=-1, keepdims=True)
            - normed * jnp.mean(total * normed, axis=-1, keepdims=True)
        )
        gi_ref[rows] = grad.astype(BF16)
        return 0

    lax.fori_loop(0, BLOCK // 16, norm_back, 0)
    gather = [send(gi_ref.at[mine], gi_ref.at[mine], (seq, tp_peer(d))) for d in range(1, 8)]

    ring_step(1)
    y_copies = []
    for i in (0, 1):
        g = groups[i]
        for side in (1, 0):
            y = (yl, other)[side]
            total = part_ref[g, y, z].astype(F32) + ps_ref[i, y, z].astype(F32)
            for sign in (1, -1):
                chain[sign, 1, i, side].wait_recv()
                total += rb_ref[(sign + 1) // 2, 0, i, side].astype(F32)
            if side == 1:
                ys_ref[i] = total.astype(BF16)
                y_copies.append(send(ys_ref.at[i], yr_ref.at[i], y_pair))
            else:
                fin_ref[i] = total
    own_rows = pl.ds(pl.multiple_of(56 * core, 8), 56)
    sib_rows = pl.ds(pl.multiple_of(56 * (1 - core), 8), 56)
    for i in (0, 1):
        y_copies[i].wait_recv()
        fin_ref[i] += yr_ref[i].astype(F32)
        fs_ref[i] = fin_ref[i, sib_rows]
        og_ref[groups[i]] = fin_ref[i, own_rows]
    last = send(fs_ref, fr_ref, sibling)
    last.wait_recv()
    og_ref[1 - core] = fr_ref[0]
    og_ref[3 - core] = fr_ref[1]

    for copy in gather:
        copy.wait_recv()
    send.drain()


def per_device(layer_input, grad_output, tile_image, qkv_weight, out_weight):
    rows = qkv_weight.shape[0]
    both = jnp.concatenate([qkv_weight, out_weight[:, None]], axis=1).reshape(rows, 4, 2, HD)
    both = jnp.pad(both, ((0, 0), (0, 0), (0, 0), (0, 128 - HD))).reshape(rows, 4, LANES)
    own = jnp.stack([both[:, 1], both[:, 2], both[:, 0], both[:, 3]])
    vmem = pltpu.VMEM
    grad_input, grads = pl.pallas_call(
        kernel,
        out_shape=(
            jax.ShapeDtypeStruct((TOK, D), BF16),
            jax.ShapeDtypeStruct((4, 56, LANES), F32),
        ),
        in_specs=[
            pl.BlockSpec(memory_space=pl.ANY),
            pl.BlockSpec(memory_space=pl.ANY),
            pl.BlockSpec(memory_space=pltpu.VMEM),
            pl.BlockSpec(memory_space=pltpu.SMEM),
        ],
        out_specs=(
            pl.BlockSpec(memory_space=pltpu.VMEM),
            pl.BlockSpec(memory_space=pltpu.VMEM),
        ),
        scratch_shapes=[
            vmem((TOK, D), BF16),
            vmem((TOK, D), BF16),
            vmem((4, 56, LANES), BF16),
            vmem((4, 2, 8, CHIP_ROWS, LANES), BF16),
            vmem((TOK, D), BF16),
            vmem((8, 128), F32),
            vmem((D, TOK), BF16),
            vmem((D, TOK), BF16),
            vmem((PAD_TOK, LANES), BF16),
            vmem((PAD_TOK, LANES), BF16),
            vmem((TOK, LANES), BF16),
            vmem((TOK, LANES), BF16),
            vmem((PAD_TOK, LANES), F32),
            vmem((PAD_TOK, LANES), F32),
            vmem((2, 2, HALO, LANES), BF16),
            vmem((2, 2, HALO, LANES), BF16),
            vmem((4, TOK, LANES), BF16),
            vmem((4, 2, 8, CHIP_ROWS, LANES), BF16),
            vmem((2, 2, 8, CHIP_ROWS, LANES), BF16),
            vmem((2, 4, 2, 2, CHIP_ROWS, LANES), BF16),
            vmem((2, CHIP_ROWS, LANES), BF16),
            vmem((2, CHIP_ROWS, LANES), BF16),
            vmem((2, CHIP_ROWS, LANES), F32),
            vmem((2, 56, LANES), F32),
            vmem((2, 56, LANES), F32),
            vmem((TOK, D), BF16),
            vmem((7, BLOCK, D), BF16),
            pltpu.SemaphoreType.DMA((N_COPIES,)),
            pltpu.SemaphoreType.DMA((N_COPIES,)),
            pltpu.SemaphoreType.DMA((2,)),
        ],
        compiler_params=pltpu.CompilerParams(
            collective_id=0, has_side_effects=True, vmem_limit_bytes=56 << 20
        ),
        name="attention_backward",
    )(layer_input, grad_output, own, tile_image)
    grads = grads.reshape(4, rows, 2, 128)[..., :HD].reshape(4, rows, 2 * HD)
    qkv_grad = jnp.stack([grads[2], grads[0], grads[1]], axis=1)
    return (grad_input, qkv_grad, grads[3])


def solution(mesh):
    placed = (P("seq", None), P("seq", None), P(), P("seq", None, "tp"), P("seq", "tp"))
    return jax.shard_map(
        per_device,
        mesh=mesh,
        in_specs=placed,
        out_specs=(P("seq", None), P("seq", None, "tp"), P("seq", "tp")),
        check_vma=False,
    )
```

```python
import functools

import jax
import jax.numpy as jnp
from jax import lax
from jax.experimental import pallas as pl
from jax.experimental.pallas import tpu as pltpu
from jax.sharding import PartitionSpec as P

HD = 112
TILE = 128
LANES = 256
TOK = 512
D = 1792
CHIP_ROWS = 112
HALO = 256
PAD_TOK = TOK + 2 * HALO
WINDOW = 768
BLOCK = 64
CUT = 768
FACTOR = float(HD) ** (-0.5)
F32 = jnp.float32
BF16 = jnp.bfloat16
MESH = pl.DeviceIdType.MESH
N_COPIES = 160

NT = (((1,), (1,)), ((), ()))


def dot(a, b):
    return jnp.dot(a, b, preferred_element_type=F32)


def dot_nt(a, b):
    return lax.dot_general(a, b, NT, preferred_element_type=F32)


class Sender:
    def __init__(self, send_sems, recv_sems):
        self.send_sems, self.recv_sems = send_sems, recv_sems
        self.copies = []

    def __call__(self, src, dst, device):
        index = len(self.copies)
        copy = pltpu.make_async_remote_copy(
            src_ref=src,
            dst_ref=dst,
            send_sem=self.send_sems.at[index],
            recv_sem=self.recv_sems.at[index],
            device_id=device,
            device_id_type=MESH,
        )
        copy.start()
        self.copies.append(copy)
        return copy

    def drain(self):
        for copy in self.copies:
            copy.wait_send()


def kernel(
    x_hbm,
    go_hbm,
    own_ref,
    ids_ref,
    gi_ref,
    og_ref,
    x_ref,
    go_ref,
    sib_ref,
    w_ref,
    xn_ref,
    xt_ref,
    got_ref,
    kp_ref,
    vp_ref,
    q_ref,
    u_ref,
    dk_ref,
    dv_ref,
    hs_ref,
    hr_ref,
    gp_ref,
    part_ref,
    ps_ref,
    rb_ref,
    ys_ref,
    yr_ref,
    fin_ref,
    fs_ref,
    fr_ref,
    ga_ref,
    gb_ref,
    ra1_ref,
    rb1_ref,
    sa2_ref,
    ra2_ref,
    sb2_ref,
    rb2_ref,
    suma_ref,
    send_sems,
    recv_sems,
    load_sems,
):
    seq = lax.axis_index("seq")
    tp = lax.axis_index("tp")
    core = lax.rem(seq, 2)
    z = lax.rem(seq // 2, 8)
    yl = seq // 16
    other = 1 - yl

    def at_z(offset):
        return lax.rem(z + 8 + offset, 8)

    def device(yl_, z_, core_):
        return (yl_ * 16 + z_ * 2 + core_, tp)

    sibling = device(yl, z, 1 - core)
    z_next = {1: device(yl, at_z(1), core), -1: device(yl, at_z(-1), core)}
    y_pair = device(other, z, core)
    following = (lax.rem(seq + 1, 32), tp)
    previous = (lax.rem(seq + 31, 32), tp)

    def tp_peer(d):
        return jnp.bitwise_xor(tp, d)

    load_x = pltpu.make_async_copy(x_hbm, x_ref, load_sems.at[0])
    load_go = pltpu.make_async_copy(go_hbm, go_ref, load_sems.at[1])
    load_x.start()
    load_go.start()

    barrier = pltpu.get_barrier_semaphore()
    peers = [sibling, z_next[1], z_next[-1], y_pair, following, previous]
    peers += [(seq, tp_peer(d)) for d in range(1, 8)]
    for peer in peers:
        pl.semaphore_signal(barrier, inc=1, device_id=peer, device_id_type=MESH)
    pl.semaphore_wait(barrier, len(peers))

    send = Sender(send_sems, recv_sems)
    groups = (core, 2 + core)

    to_sibling = send(own_ref, sib_ref, sibling)
    load_x.wait()

    def norm_rows(start):
        rows = slice(start, start + 32)
        wide = x_ref[rows].astype(F32)
        mean = jnp.mean(wide, axis=-1, keepdims=True)
        center = wide - mean
        inv_std = lax.rsqrt(jnp.mean(center * center, axis=-1, keepdims=True) + 1e-06)
        xn_ref[rows] = (center * inv_std).astype(BF16)

    def transpose_block(src, dst, row, column):
        dst[column : column + 896, row : row + 128] = src[row : row + 128, column : column + 896].T

    work = [functools.partial(norm_rows, 32 * i) for i in range(16)]
    for source, target in ((go_ref, got_ref), (xn_ref, xt_ref)):
        for row in range(0, TOK, 128):
            for column in (0, 896):
                work.append(functools.partial(transpose_block, source, target, row, column))
    work.reverse()

    def do_some(count):
        for _ in range(min(count, len(work))):
            work.pop()()

    to_sibling.wait_recv()
    for g in range(4):
        mine = own_ref[g].astype(F32)
        theirs = sib_ref[g].astype(F32)
        low = jnp.where(core == 0, mine, theirs)
        high = jnp.where(core == 0, theirs, mine)
        w_ref[g, yl, z] = jnp.concatenate([low, high], axis=0).astype(BF16)

    ring = {}
    pair = {}
    for i in (0, 1):
        g = groups[i]
        block = w_ref.at[g, yl, z]
        for sign in (1, -1):
            ring[sign, 1, i, 0] = send(block, block, z_next[sign])
        pair[i] = send(block, block, y_pair)
    beside = []
    do_some(2)
    for i in (0, 1):
        block = w_ref.at[groups[i], other, z]
        pair[i].wait_recv()
        for sign in (1, -1):
            ring[sign, 1, i, 1] = send(block, block, z_next[sign])
        beside.append(send(block, block, sibling))

    load_go.wait()
    for t in (1, 2, 3, 4):
        for i in (0, 1):
            for side in (0, 1):
                for sign in (1, -1):
                    if (sign, t, i, side) not in ring:
                        continue
                    ring[sign, t, i, side].wait_recv()
                    block = w_ref.at[groups[i], (yl, other)[side], at_z(-sign * t)]
                    if t < 3 or (t == 3 and side == (0 if sign == 1 else 1)):
                        ring[sign, t + 1, i, side] = send(block, block, z_next[sign])
                    beside.append(send(block, block, sibling))
                do_some(2)
    do_some(len(work))
    for copy in beside:
        copy.wait_recv()

    def weights(g):
        return w_ref[g].reshape(D, LANES)

    halo = []
    for g, ref in ((0, kp_ref), (1, vp_ref)):
        ref[HALO : HALO + TOK] = dot(xn_ref[...], weights(g)).astype(BF16)
        halo.append(send(ref.at[pl.ds(HALO, HALO)], ref.at[pl.ds(HALO + TOK, HALO)], previous))
        halo.append(send(ref.at[pl.ds(TOK, HALO)], ref.at[pl.ds(0, HALO)], following))
    q_ref[...] = dot(xn_ref[...], weights(2)).astype(BF16)
    u_ref[...] = dot(go_ref[...], weights(3)).astype(BF16)

    def tile_id(tile):
        inside = jnp.logical_and(tile >= 0, tile < 128)
        value = ids_ref[jnp.clip(tile, 0, 127)]
        return jnp.where(inside, value, -1)

    key_ids = [tile_id(4 * seq - 2 + k) for k in range(8)]
    lane = lax.broadcasted_iota(jnp.int32, (1, 256), 1)
    for copy in halo:
        copy.wait_recv()

    back = []
    for h in (0, 1):
        lanes = slice(128 * h, 128 * h + 128)
        key_t = kp_ref[:, lanes].T
        value_t = vp_ref[:, lanes].T
        for half in (0, 1):
            keys = slice(256 * half, 256 * half + WINDOW)
            rows = slice(256 * half, 256 * half + 256)
            query = q_ref[rows, lanes]
            up = u_ref[rows, lanes]
            key = kp_ref[keys, lanes]
            value = vp_ref[keys, lanes]
            scores = dot_nt(key, query) * FACTOR
            query_id = jnp.where(lane < 128, key_ids[2 + 2 * half], key_ids[3 + 2 * half])
            parts = []
            for k in range(6):
                allowed = query_id == key_ids[2 * half + k]
                parts.append(jnp.where(allowed, jnp.exp(scores[128 * k : 128 * k + 128]), 0.0))
            exponent = jnp.concatenate(parts, axis=0)
            prob = exponent * (1.0 / jnp.sum(exponent, axis=0, keepdims=True))
            prob_low = prob.astype(BF16)
            attended = dot(value_t[:, keys], prob_low)
            delta = jnp.sum(up.astype(F32).T * attended, axis=0, keepdims=True)
            dprob = dot_nt(value, up)
            dscore = (prob * (dprob - delta) * FACTOR).astype(BF16)
            dquery = dot(key_t[:, keys], dscore)
            gp_ref[2, rows, lanes] = dquery.T.astype(BF16)
            gp_ref[3, rows, lanes] = attended.T.astype(BF16)
            dkey = dot(dscore, query)
            dvalue = dot(prob_low, up)
            for ref, grad in ((dk_ref, dkey), (dv_ref, dvalue)):
                if half == 0:
                    ref[0:WINDOW, lanes] = grad
                else:
                    ref[256:WINDOW, lanes] += grad[: WINDOW - 256]
                    ref[WINDOW:PAD_TOK, lanes] = grad[WINDOW - 256 :]
        for j, ref in ((0, dk_ref), (1, dv_ref)):
            hs_ref[h, j, 0] = ref[0:HALO, lanes].astype(BF16)
            hs_ref[h, j, 1] = ref[HALO + TOK : PAD_TOK, lanes].astype(BF16)
            back.append(send(hs_ref.at[h, j, 0], hr_ref.at[h, j, 0], previous))
            back.append(send(hs_ref.at[h, j, 1], hr_ref.at[h, j, 1], following))

    def weight_grad(g):
        src = got_ref if g == 3 else xt_ref

        def body(i, _):
            rows = pl.ds(pl.multiple_of(i * 896, 128), 896)
            part_ref[g, i] = dot(src[rows], gp_ref[g]).astype(BF16).reshape(8, CHIP_ROWS, LANES)
            return 0

        lax.fori_loop(0, 2, body, 0)

    weight_grad(2)
    weight_grad(3)
    swap = {1: send(part_ref.at[3 - core], ps_ref.at[1], sibling)}
    for copy in back:
        copy.wait_recv()
    for h in (0, 1):
        lanes = slice(128 * h, 128 * h + 128)
        for j, ref in ((0, dk_ref), (1, dv_ref)):
            low = ref[HALO : 2 * HALO, lanes] + hr_ref[h, j, 1].astype(F32)
            high = ref[2 * HALO : 3 * HALO, lanes] + hr_ref[h, j, 0].astype(F32)
            gp_ref[j, 0:HALO, lanes] = low.astype(BF16)
            gp_ref[j, HALO:TOK, lanes] = high.astype(BF16)

    yh, xx = tp // 4, lax.rem(tp, 4)
    y_other = (seq, (1 - yh) * 4 + xx)

    def x_at(e):
        return lax.rem(xx + e, 4)

    def x_peer(e):
        return (seq, yh * 4 + x_at(e))

    def block_at(e):
        return pl.ds(pl.multiple_of(x_at(e) * BLOCK, BLOCK), BLOCK)

    def partial_norm(half, start, stop):
        rows = pl.ds(pl.multiple_of(half * 256, 256), 256)
        total = dot_nt(gp_ref[0, rows], weights(0)[start:stop])
        total += dot_nt(gp_ref[1, rows], weights(1)[start:stop])
        total += dot_nt(gp_ref[2, rows], weights(2)[start:stop])
        return total.astype(BF16)

    gb_ref[1 - yh] = partial_norm(1 - yh, CUT, D)
    y_first = {}
    for e in (1, 3, 2, 0):
        y_first[e] = send(gb_ref.at[1 - yh, block_at(e)], rb1_ref.at[e], y_other)
    for half in (0, 1):
        ga_ref[half] = partial_norm(half, 0, CUT)
    x_first = [send(ga_ref.at[:, block_at(e)], ra1_ref.at[e - 1], x_peer(e)) for e in (1, 3, 2)]
    gb_ref[yh] = partial_norm(yh, CUT, D)

    weight_grad(0)
    weight_grad(1)
    swap[0] = send(part_ref.at[1 - core], ps_ref.at[0], sibling)

    for i in (1, 0):
        swap[i].wait_recv()
    chain = {}

    def ring_step(t):
        for i in (0, 1):
            g = groups[i]
            for side in (0, 1):
                y = (yl, other)[side]
                for sign in (1, -1):
                    if t == 4 and side != (0 if sign == 1 else 1):
                        continue
                    zz = at_z(sign * t)
                    total = part_ref[g, y, zz].astype(F32) + ps_ref[i, y, zz].astype(F32)
                    if (sign, t + 1, i, side) in chain:
                        chain[sign, t + 1, i, side].wait_recv()
                        total += rb_ref[(sign + 1) // 2, t, i, side].astype(F32)
                    part_ref[g, y, zz] = total.astype(BF16)
                    chain[sign, t, i, side] = send(
                        part_ref.at[g, y, zz],
                        rb_ref.at[(sign + 1) // 2, t - 1, i, side],
                        z_next[sign],
                    )

    ring_step(4)

    x_second = []
    for e in (1, 3, 2):
        y_first[e].wait_recv()
        total = gb_ref[yh, block_at(e)].astype(F32) + rb1_ref[e].astype(F32)
        sb2_ref[e - 1] = total.astype(BF16)
        x_second.append(send(sb2_ref.at[e - 1], rb2_ref.at[e - 1], x_peer(e)))

    for copy in x_first:
        copy.wait_recv()
    sums = []
    for half in (1 - yh, yh):
        total = ga_ref[half, block_at(0)].astype(F32)
        for e in (1, 2, 3):
            total += ra1_ref[e - 1, half].astype(F32)
        sums.append(total)
        if len(sums) == 1:
            sa2_ref[...] = total.astype(BF16)
            y_second = send(sa2_ref, ra2_ref, y_other)
    suma_ref[...] = sums[1]
    ring_step(3)

    y_second.wait_recv()
    y_first[0].wait_recv()
    for copy in x_second:
        copy.wait_recv()

    def norm_back(i, _):
        rows = pl.ds(pl.multiple_of(tp * BLOCK + i * 16, 16), 16)
        part = pl.ds(pl.multiple_of(i * 16, 16), 16)
        own_part = pl.ds(pl.multiple_of(xx * BLOCK + i * 16, 16), 16)
        first = suma_ref[part] + ra2_ref[part].astype(F32)
        second = gb_ref[yh, own_part].astype(F32) + rb1_ref[0, part].astype(F32)
        for e in range(3):
            second += rb2_ref[e, part].astype(F32)
        total = jnp.concatenate([first, second], axis=1)
        wide = x_ref[rows].astype(F32)
        center = wide - jnp.mean(wide, axis=-1, keepdims=True)
        inv_std = lax.rsqrt(jnp.mean(center * center, axis=-1, keepdims=True) + 1e-06)
        normed = center * inv_std
        grad = inv_std * (
            total
            - jnp.mean(total, axis=-1, keepdims=True)
            - normed * jnp.mean(total * normed, axis=-1, keepdims=True)
        )
        gi_ref[rows] = grad.astype(BF16)
        return 0

    lax.fori_loop(0, BLOCK // 16, norm_back, 0)

    def rows_of(y, x):
        return pl.ds(pl.multiple_of((y * 4 + x) * BLOCK, BLOCK), BLOCK)

    def share(y, x, columns, to):
        piece = gi_ref.at[rows_of(y, x), columns]
        return send(piece, piece, to)

    first, second = pl.ds(0, CUT), pl.ds(CUT, D - CUT)
    y_gather = [share(yh, xx, first, y_other)]
    x_gather = {e: share(yh, xx, second, x_peer(e)) for e in (1, 3, 2)}
    y_gather.append(share(yh, xx, second, y_other))
    gather = [share(yh, xx, first, x_peer(e)) for e in (1, 3, 2)]
    gather.append(y_gather[1])
    ring_step(2)
    y_gather[0].wait_recv()
    for e in (1, 3, 2):
        gather.append(share(1 - yh, xx, first, x_peer(e)))
    for e in (1, 3, 2):
        x_gather[e].wait_recv()
        gather.append(share(yh, x_at(-e + 4), second, y_other))

    ring_step(1)
    y_copies = []
    for i in (0, 1):
        g = groups[i]
        for side in (1, 0):
            y = (yl, other)[side]
            total = part_ref[g, y, z].astype(F32) + ps_ref[i, y, z].astype(F32)
            for sign in (1, -1):
                chain[sign, 1, i, side].wait_recv()
                total += rb_ref[(sign + 1) // 2, 0, i, side].astype(F32)
            if side == 1:
                ys_ref[i] = total.astype(BF16)
                y_copies.append(send(ys_ref.at[i], yr_ref.at[i], y_pair))
            else:
                fin_ref[i] = total
    own_rows = pl.ds(pl.multiple_of(56 * core, 8), 56)
    sib_rows = pl.ds(pl.multiple_of(56 * (1 - core), 8), 56)
    for i in (0, 1):
        y_copies[i].wait_recv()
        fin_ref[i] += yr_ref[i].astype(F32)
        fs_ref[i] = fin_ref[i, sib_rows]
        og_ref[groups[i]] = fin_ref[i, own_rows]
    last = send(fs_ref, fr_ref, sibling)
    last.wait_recv()
    og_ref[1 - core] = fr_ref[0]
    og_ref[3 - core] = fr_ref[1]

    for copy in gather:
        copy.wait_recv()
    send.drain()


def per_device(layer_input, grad_output, tile_image, qkv_weight, out_weight):
    rows = qkv_weight.shape[0]
    both = jnp.concatenate([qkv_weight, out_weight[:, None]], axis=1).reshape(rows, 4, 2, HD)
    both = jnp.pad(both, ((0, 0), (0, 0), (0, 0), (0, 128 - HD))).reshape(rows, 4, LANES)
    own = jnp.stack([both[:, 1], both[:, 2], both[:, 0], both[:, 3]])
    vmem = pltpu.VMEM
    grad_input, grads = pl.pallas_call(
        kernel,
        out_shape=(
            jax.ShapeDtypeStruct((TOK, D), BF16),
            jax.ShapeDtypeStruct((4, 56, LANES), F32),
        ),
        in_specs=[
            pl.BlockSpec(memory_space=pl.ANY),
            pl.BlockSpec(memory_space=pl.ANY),
            pl.BlockSpec(memory_space=pltpu.VMEM),
            pl.BlockSpec(memory_space=pltpu.SMEM),
        ],
        out_specs=(
            pl.BlockSpec(memory_space=pltpu.VMEM),
            pl.BlockSpec(memory_space=pltpu.VMEM),
        ),
        scratch_shapes=[
            vmem((TOK, D), BF16),
            vmem((TOK, D), BF16),
            vmem((4, 56, LANES), BF16),
            vmem((4, 2, 8, CHIP_ROWS, LANES), BF16),
            vmem((TOK, D), BF16),
            vmem((D, TOK), BF16),
            vmem((D, TOK), BF16),
            vmem((PAD_TOK, LANES), BF16),
            vmem((PAD_TOK, LANES), BF16),
            vmem((TOK, LANES), BF16),
            vmem((TOK, LANES), BF16),
            vmem((PAD_TOK, LANES), F32),
            vmem((PAD_TOK, LANES), F32),
            vmem((2, 2, 2, HALO, 128), BF16),
            vmem((2, 2, 2, HALO, 128), BF16),
            vmem((4, TOK, LANES), BF16),
            vmem((4, 2, 8, CHIP_ROWS, LANES), BF16),
            vmem((2, 2, 8, CHIP_ROWS, LANES), BF16),
            vmem((2, 4, 2, 2, CHIP_ROWS, LANES), BF16),
            vmem((2, CHIP_ROWS, LANES), BF16),
            vmem((2, CHIP_ROWS, LANES), BF16),
            vmem((2, CHIP_ROWS, LANES), F32),
            vmem((2, 56, LANES), F32),
            vmem((2, 56, LANES), F32),
            vmem((2, 256, CUT), BF16),
            vmem((2, 256, D - CUT), BF16),
            vmem((3, 2, BLOCK, CUT), BF16),
            vmem((4, BLOCK, D - CUT), BF16),
            vmem((BLOCK, CUT), BF16),
            vmem((BLOCK, CUT), BF16),
            vmem((3, BLOCK, D - CUT), BF16),
            vmem((3, BLOCK, D - CUT), BF16),
            vmem((BLOCK, CUT), F32),
            pltpu.SemaphoreType.DMA((N_COPIES,)),
            pltpu.SemaphoreType.DMA((N_COPIES,)),
            pltpu.SemaphoreType.DMA((2,)),
        ],
        compiler_params=pltpu.CompilerParams(
            collective_id=0, has_side_effects=True, vmem_limit_bytes=56 << 20
        ),
        name="attention_backward",
    )(layer_input, grad_output, own, tile_image)
    grads = grads.reshape(4, rows, 2, 128)[..., :HD].reshape(4, rows, 2 * HD)
    qkv_grad = jnp.stack([grads[2], grads[0], grads[1]], axis=1)
    return (grad_input, qkv_grad, grads[3])


def solution(mesh):
    placed = (P("seq", None), P("seq", None), P(), P("seq", None, "tp"), P("seq", "tp"))
    return jax.shard_map(
        per_device,
        mesh=mesh,
        in_specs=placed,
        out_specs=(P("seq", None), P("seq", None, "tp"), P("seq", "tp")),
        check_vma=False,
    )
```

```python
import functools

import jax
import jax.numpy as jnp
from jax import lax
from jax.experimental import pallas as pl
from jax.experimental.pallas import tpu as pltpu
from jax.sharding import PartitionSpec as P

HD = 112
TILE = 128
LANES = 256
TOK = 512
D = 1792
CHIP_ROWS = 112
HALO = 256
PAD_TOK = TOK + 2 * HALO
WINDOW = 768
BLOCK = 64
CUT = 768
FACTOR = float(HD) ** (-0.5)
F32 = jnp.float32
BF16 = jnp.bfloat16
MESH = pl.DeviceIdType.MESH
N_COPIES = 160

NT = (((1,), (1,)), ((), ()))


def dot(a, b):
    return jnp.dot(a, b, preferred_element_type=F32)


def dot_nt(a, b):
    return lax.dot_general(a, b, NT, preferred_element_type=F32)


class Sender:
    def __init__(self, send_sems, recv_sems):
        self.send_sems, self.recv_sems = send_sems, recv_sems
        self.copies = []

    def __call__(self, src, dst, device):
        index = len(self.copies)
        copy = pltpu.make_async_remote_copy(
            src_ref=src,
            dst_ref=dst,
            send_sem=self.send_sems.at[index],
            recv_sem=self.recv_sems.at[index],
            device_id=device,
            device_id_type=MESH,
        )
        copy.start()
        self.copies.append(copy)
        return copy

    def drain(self):
        for copy in self.copies:
            copy.wait_send()


def kernel(
    x_hbm,
    go_hbm,
    qkv_ref,
    out_ref,
    ids_ref,
    gi_ref,
    qkv_grad_ref,
    out_grad_ref,
    own_ref,
    og_ref,
    x_ref,
    go_ref,
    sib_ref,
    w_ref,
    xb_ref,
    gob_ref,
    acc_ref,
    xt_ref,
    got_ref,
    kp_ref,
    vp_ref,
    q_ref,
    u_ref,
    dk_ref,
    dv_ref,
    hs_ref,
    hr_ref,
    gp_ref,
    part_ref,
    ps_ref,
    rb_ref,
    ys_ref,
    yr_ref,
    fin_ref,
    fs_ref,
    fr_ref,
    ga_ref,
    gb_ref,
    ra1_ref,
    rb1_ref,
    sa2_ref,
    ra2_ref,
    sb2_ref,
    rb2_ref,
    suma_ref,
    send_sems,
    recv_sems,
    load_sems,
):
    seq = lax.axis_index("seq")
    tp = lax.axis_index("tp")
    core = lax.rem(seq, 2)
    z = lax.rem(seq // 2, 8)
    yl = seq // 16
    other = 1 - yl

    def at_z(offset):
        return lax.rem(z + 8 + offset, 8)

    def device(yl_, z_, core_):
        return (yl_ * 16 + z_ * 2 + core_, tp)

    sibling = device(yl, z, 1 - core)
    z_next = {1: device(yl, at_z(1), core), -1: device(yl, at_z(-1), core)}
    y_pair = device(other, z, core)
    following = (lax.rem(seq + 1, 32), tp)
    previous = (lax.rem(seq + 31, 32), tp)

    def tp_peer(d):
        return jnp.bitwise_xor(tp, d)

    load_x = pltpu.make_async_copy(x_hbm, x_ref, load_sems.at[0])
    load_go = pltpu.make_async_copy(go_hbm, go_ref, load_sems.at[1])
    load_x.start()
    load_go.start()

    barrier = pltpu.get_barrier_semaphore()
    peers = [sibling, z_next[1], z_next[-1], y_pair, following, previous]
    peers += [(seq, tp_peer(d)) for d in range(1, 8)]

    def spread(rows):
        wide = rows.astype(F32)
        gap = jnp.zeros((wide.shape[0], 128 - HD), F32)
        return jnp.concatenate([wide[:, :HD], gap, wide[:, HD:], gap], axis=1).astype(BF16)

    def close_up(wide):
        return jnp.concatenate([wide[:, :HD], wide[:, 128 : 128 + HD]], axis=1)

    own_ref[0] = spread(qkv_ref[1])
    own_ref[1] = spread(qkv_ref[2])
    own_ref[2] = spread(qkv_ref[0])
    own_ref[3] = spread(out_ref[...])
    for peer in peers:
        pl.semaphore_signal(barrier, inc=1, device_id=peer, device_id_type=MESH)
    pl.semaphore_wait(barrier, len(peers))

    send = Sender(send_sems, recv_sems)
    groups = (core, 2 + core)

    to_sibling = send(own_ref, sib_ref, sibling)
    load_x.wait()

    def split_columns(dst, rows, wide):
        for k in range(8):
            low = wide[:, CHIP_ROWS * k : CHIP_ROWS * (k + 1)]
            high = wide[:, 896 + CHIP_ROWS * k : 896 + CHIP_ROWS * (k + 1)]
            dst[k, rows, 0 : 2 * CHIP_ROWS] = jnp.concatenate([low, high], axis=1).astype(BF16)

    def split_rows(start):
        rows = slice(start, start + 32)
        split_columns(gob_ref, rows, go_ref[rows].astype(F32))

    def norm_rows(start):
        rows = slice(start, start + 32)
        wide = x_ref[rows].astype(F32)
        mean = jnp.mean(wide, axis=-1, keepdims=True)
        center = wide - mean
        inv_std = lax.rsqrt(jnp.mean(center * center, axis=-1, keepdims=True) + 1e-06)
        split_columns(xb_ref, rows, center * inv_std)

    def transpose_block(src, dst, k):
        dst[k] = src[k].T[: 2 * CHIP_ROWS]

    work = [functools.partial(norm_rows, 32 * i) for i in range(16)]
    work += [functools.partial(split_rows, 32 * i) for i in range(16)]
    later = []
    for source, target in ((gob_ref, got_ref), (xb_ref, xt_ref)):
        for k in range(8):
            later.append(functools.partial(transpose_block, source, target, k))
    work.reverse()
    later.reverse()

    def do_some(count):
        for _ in range(count):
            if work or later:
                (work or later).pop()()

    def project(blocks, first=False):
        for g, src in ((0, xb_ref), (1, xb_ref), (2, xb_ref), (3, gob_ref)):
            total = 0.0 if first else acc_ref[g]
            for k in blocks:
                block = w_ref[g, k].reshape(2 * CHIP_ROWS, LANES)
                total += dot(src[k, :, 0 : 2 * CHIP_ROWS], block)
            acc_ref[g] = total

    to_sibling.wait_recv()
    for g in range(4):
        mine = own_ref[g].astype(F32)
        theirs = sib_ref[g].astype(F32)
        low = jnp.where(core == 0, mine, theirs)
        high = jnp.where(core == 0, theirs, mine)
        w_ref[g, z, yl] = jnp.concatenate([low, high], axis=0).astype(BF16)

    ring = {}
    pair = {}
    for i in (0, 1):
        g = groups[i]
        block = w_ref.at[g, z, yl]
        for sign in (1, -1):
            ring[sign, 1, i, 0] = send(block, block, z_next[sign])
        pair[i] = send(block, block, y_pair)
    beside = []
    do_some(4)
    for i in (0, 1):
        block = w_ref.at[groups[i], z, other]
        pair[i].wait_recv()
        for sign in (1, -1):
            ring[sign, 1, i, 1] = send(block, block, z_next[sign])
        beside.append(send(block, block, sibling))

    load_go.wait()
    do_some(6)
    for t in (1, 2, 3, 4):
        before = list(beside)
        beside = []
        for i in (0, 1):
            for side in (0, 1):
                for sign in (1, -1):
                    if (sign, t, i, side) not in ring:
                        continue
                    ring[sign, t, i, side].wait_recv()
                    block = w_ref.at[groups[i], at_z(-sign * t), (yl, other)[side]]
                    if t < 3 or (t == 3 and side == (0 if sign == 1 else 1)):
                        ring[sign, t + 1, i, side] = send(block, block, z_next[sign])
                    beside.append(send(block, block, sibling))
                do_some(2)
        if t == 1:
            do_some(len(work))
        for copy in before:
            copy.wait_recv()
        project([at_z(1 - t), at_z(t - 1)] if t > 1 else [z], t == 1)
    do_some(len(later))
    for copy in beside:
        copy.wait_recv()
    project([at_z(4)])

    def weights(g):
        return jnp.concatenate([w_ref[g, :, y].reshape(896, LANES) for y in (0, 1)], axis=0)

    halo = []
    for g, ref in ((0, kp_ref), (1, vp_ref)):
        ref[HALO : HALO + TOK] = acc_ref[g].astype(BF16)
        halo.append(send(ref.at[pl.ds(HALO, HALO)], ref.at[pl.ds(HALO + TOK, HALO)], previous))
        halo.append(send(ref.at[pl.ds(TOK, HALO)], ref.at[pl.ds(0, HALO)], following))
    q_ref[...] = acc_ref[2].astype(BF16)
    u_ref[...] = acc_ref[3].astype(BF16)

    def tile_id(tile):
        inside = jnp.logical_and(tile >= 0, tile < 128)
        value = ids_ref[jnp.clip(tile, 0, 127)]
        return jnp.where(inside, value, -1)

    key_ids = [tile_id(4 * seq - 2 + k) for k in range(8)]
    lane = lax.broadcasted_iota(jnp.int32, (1, 256), 1)
    for copy in halo:
        copy.wait_recv()

    back = []
    for h in (0, 1):
        lanes = slice(128 * h, 128 * h + 128)
        key_t = kp_ref[:, lanes].T
        value_t = vp_ref[:, lanes].T
        for half in (0, 1):
            keys = slice(256 * half, 256 * half + WINDOW)
            rows = slice(256 * half, 256 * half + 256)
            query = q_ref[rows, lanes]
            up = u_ref[rows, lanes]
            key = kp_ref[keys, lanes]
            value = vp_ref[keys, lanes]
            scores = dot_nt(key, query) * FACTOR
            query_id = jnp.where(lane < 128, key_ids[2 + 2 * half], key_ids[3 + 2 * half])
            parts = []
            for k in range(6):
                allowed = query_id == key_ids[2 * half + k]
                parts.append(jnp.where(allowed, jnp.exp(scores[128 * k : 128 * k + 128]), 0.0))
            exponent = jnp.concatenate(parts, axis=0)
            prob = exponent * (1.0 / jnp.sum(exponent, axis=0, keepdims=True))
            prob_low = prob.astype(BF16)
            attended = dot(value_t[:, keys], prob_low)
            delta = jnp.sum(up.astype(F32).T * attended, axis=0, keepdims=True)
            dprob = dot_nt(value, up)
            dscore = (prob * (dprob - delta) * FACTOR).astype(BF16)
            dquery = dot(key_t[:, keys], dscore)
            gp_ref[2, rows, lanes] = dquery.T.astype(BF16)
            gp_ref[3, rows, lanes] = attended.T.astype(BF16)
            dkey = dot(dscore, query)
            dvalue = dot(prob_low, up)
            for ref, grad in ((dk_ref, dkey), (dv_ref, dvalue)):
                if half == 0:
                    ref[0:WINDOW, lanes] = grad
                else:
                    ref[256:WINDOW, lanes] += grad[: WINDOW - 256]
                    ref[WINDOW:PAD_TOK, lanes] = grad[WINDOW - 256 :]
        for j, ref in ((0, dk_ref), (1, dv_ref)):
            hs_ref[h, j, 0] = ref[0:HALO, lanes].astype(BF16)
            hs_ref[h, j, 1] = ref[HALO + TOK : PAD_TOK, lanes].astype(BF16)
            back.append(send(hs_ref.at[h, j, 0], hr_ref.at[h, j, 0], previous))
            back.append(send(hs_ref.at[h, j, 1], hr_ref.at[h, j, 1], following))

    def weight_grad(g):
        src = got_ref if g == 3 else xt_ref

        def body(i, _):
            blocks = pl.ds(i * 4, 4)
            grad = dot(src[blocks].reshape(896, TOK), gp_ref[g]).astype(BF16)
            part_ref[g, blocks] = grad.reshape(4, 2, CHIP_ROWS, LANES)
            return 0

        lax.fori_loop(0, 2, body, 0)

    weight_grad(2)
    weight_grad(3)
    swap = {1: send(part_ref.at[3 - core], ps_ref.at[1], sibling)}
    for copy in back:
        copy.wait_recv()
    for h in (0, 1):
        lanes = slice(128 * h, 128 * h + 128)
        for j, ref in ((0, dk_ref), (1, dv_ref)):
            low = ref[HALO : 2 * HALO, lanes] + hr_ref[h, j, 1].astype(F32)
            high = ref[2 * HALO : 3 * HALO, lanes] + hr_ref[h, j, 0].astype(F32)
            gp_ref[j, 0:HALO, lanes] = low.astype(BF16)
            gp_ref[j, HALO:TOK, lanes] = high.astype(BF16)

    yh, xx = tp // 4, lax.rem(tp, 4)
    y_other = (seq, (1 - yh) * 4 + xx)

    def x_at(e):
        return lax.rem(xx + e, 4)

    def x_peer(e):
        return (seq, yh * 4 + x_at(e))

    def block_at(e):
        return pl.ds(pl.multiple_of(x_at(e) * BLOCK, BLOCK), BLOCK)

    def partial_norm(half, start, stop):
        rows = pl.ds(pl.multiple_of(half * 256, 256), 256)
        total = dot_nt(gp_ref[0, rows], weights(0)[start:stop])
        total += dot_nt(gp_ref[1, rows], weights(1)[start:stop])
        total += dot_nt(gp_ref[2, rows], weights(2)[start:stop])
        return total.astype(BF16)

    gb_ref[1 - yh] = partial_norm(1 - yh, CUT, D)
    y_first = {}
    for e in (1, 3, 2, 0):
        y_first[e] = send(gb_ref.at[1 - yh, block_at(e)], rb1_ref.at[e], y_other)
    for half in (0, 1):
        ga_ref[half] = partial_norm(half, 0, CUT)
    x_first = [send(ga_ref.at[:, block_at(e)], ra1_ref.at[e - 1], x_peer(e)) for e in (1, 3, 2)]
    gb_ref[yh] = partial_norm(yh, CUT, D)

    weight_grad(0)
    weight_grad(1)
    swap[0] = send(part_ref.at[1 - core], ps_ref.at[0], sibling)

    for i in (1, 0):
        swap[i].wait_recv()
    chain = {}

    def ring_step(t):
        for i in (0, 1):
            g = groups[i]
            for side in (0, 1):
                y = (yl, other)[side]
                for sign in (1, -1):
                    if t == 4 and side != (0 if sign == 1 else 1):
                        continue
                    zz = at_z(sign * t)
                    total = part_ref[g, zz, y].astype(F32) + ps_ref[i, zz, y].astype(F32)
                    if (sign, t + 1, i, side) in chain:
                        chain[sign, t + 1, i, side].wait_recv()
                        total += rb_ref[(sign + 1) // 2, t, i, side].astype(F32)
                    part_ref[g, zz, y] = total.astype(BF16)
                    chain[sign, t, i, side] = send(
                        part_ref.at[g, zz, y],
                        rb_ref.at[(sign + 1) // 2, t - 1, i, side],
                        z_next[sign],
                    )

    ring_step(4)

    x_second = []
    for e in (1, 3, 2):
        y_first[e].wait_recv()
        total = gb_ref[yh, block_at(e)].astype(F32) + rb1_ref[e].astype(F32)
        sb2_ref[e - 1] = total.astype(BF16)
        x_second.append(send(sb2_ref.at[e - 1], rb2_ref.at[e - 1], x_peer(e)))

    for copy in x_first:
        copy.wait_recv()
    sums = []
    for half in (1 - yh, yh):
        total = ga_ref[half, block_at(0)].astype(F32)
        for e in (1, 2, 3):
            total += ra1_ref[e - 1, half].astype(F32)
        sums.append(total)
        if len(sums) == 1:
            sa2_ref[...] = total.astype(BF16)
            y_second = send(sa2_ref, ra2_ref, y_other)
    suma_ref[...] = sums[1]
    ring_step(3)

    y_second.wait_recv()
    y_first[0].wait_recv()
    for copy in x_second:
        copy.wait_recv()

    def norm_back(i, _):
        rows = pl.ds(pl.multiple_of(tp * BLOCK + i * 16, 16), 16)
        part = pl.ds(pl.multiple_of(i * 16, 16), 16)
        own_part = pl.ds(pl.multiple_of(xx * BLOCK + i * 16, 16), 16)
        first = suma_ref[part] + ra2_ref[part].astype(F32)
        second = gb_ref[yh, own_part].astype(F32) + rb1_ref[0, part].astype(F32)
        for e in range(3):
            second += rb2_ref[e, part].astype(F32)
        total = jnp.concatenate([first, second], axis=1)
        wide = x_ref[rows].astype(F32)
        center = wide - jnp.mean(wide, axis=-1, keepdims=True)
        inv_std = lax.rsqrt(jnp.mean(center * center, axis=-1, keepdims=True) + 1e-06)
        normed = center * inv_std
        grad = inv_std * (
            total
            - jnp.mean(total, axis=-1, keepdims=True)
            - normed * jnp.mean(total * normed, axis=-1, keepdims=True)
        )
        gi_ref[rows] = grad.astype(BF16)
        return 0

    lax.fori_loop(0, BLOCK // 16, norm_back, 0)

    def rows_of(y, x):
        return pl.ds(pl.multiple_of((y * 4 + x) * BLOCK, BLOCK), BLOCK)

    def share(y, x, columns, to):
        piece = gi_ref.at[rows_of(y, x), columns]
        return send(piece, piece, to)

    first, second = pl.ds(0, CUT), pl.ds(CUT, D - CUT)
    y_gather = [share(yh, xx, first, y_other)]
    x_gather = {e: share(yh, xx, second, x_peer(e)) for e in (1, 3, 2)}
    y_gather.append(share(yh, xx, second, y_other))
    gather = [share(yh, xx, first, x_peer(e)) for e in (1, 3, 2)]
    gather.append(y_gather[1])
    ring_step(2)
    y_gather[0].wait_recv()
    for e in (1, 3, 2):
        gather.append(share(1 - yh, xx, first, x_peer(e)))
    for e in (1, 3, 2):
        x_gather[e].wait_recv()
        gather.append(share(yh, x_at(-e + 4), second, y_other))

    ring_step(1)
    y_copies = []
    for i in (0, 1):
        g = groups[i]
        for side in (1, 0):
            y = (yl, other)[side]
            total = part_ref[g, z, y].astype(F32) + ps_ref[i, z, y].astype(F32)
            for sign in (1, -1):
                chain[sign, 1, i, side].wait_recv()
                total += rb_ref[(sign + 1) // 2, 0, i, side].astype(F32)
            if side == 1:
                ys_ref[i] = total.astype(BF16)
                y_copies.append(send(ys_ref.at[i], yr_ref.at[i], y_pair))
            else:
                fin_ref[i] = total
    own_rows = pl.ds(pl.multiple_of(56 * core, 8), 56)
    sib_rows = pl.ds(pl.multiple_of(56 * (1 - core), 8), 56)
    for i in (0, 1):
        y_copies[i].wait_recv()
        fin_ref[i] += yr_ref[i].astype(F32)
        fs_ref[i] = fin_ref[i, sib_rows]
        og_ref[groups[i]] = fin_ref[i, own_rows]
    last = send(fs_ref, fr_ref, sibling)
    last.wait_recv()
    og_ref[1 - core] = fr_ref[0]
    og_ref[3 - core] = fr_ref[1]
    for c, g in ((0, 2), (1, 0), (2, 1)):
        qkv_grad_ref[c] = close_up(og_ref[g])
    out_grad_ref[...] = close_up(og_ref[3])

    for copy in gather:
        copy.wait_recv()
    send.drain()


def per_device(layer_input, grad_output, tile_image, qkv_weight, out_weight):
    vmem = pltpu.VMEM
    grad_input, qkv_grad, out_grad = pl.pallas_call(
        kernel,
        out_shape=(
            jax.ShapeDtypeStruct((TOK, D), BF16),
            jax.ShapeDtypeStruct((3, 56, 2 * HD), F32),
            jax.ShapeDtypeStruct((56, 2 * HD), F32),
        ),
        in_specs=[
            pl.BlockSpec(memory_space=pl.ANY),
            pl.BlockSpec(memory_space=pl.ANY),
            pl.BlockSpec(memory_space=pltpu.VMEM),
            pl.BlockSpec(memory_space=pltpu.VMEM),
            pl.BlockSpec(memory_space=pltpu.SMEM),
        ],
        out_specs=(
            pl.BlockSpec(memory_space=pltpu.VMEM),
            pl.BlockSpec(memory_space=pltpu.VMEM),
            pl.BlockSpec(memory_space=pltpu.VMEM),
        ),
        scratch_shapes=[
            vmem((4, 56, LANES), BF16),
            vmem((4, 56, LANES), F32),
            vmem((TOK, D), BF16),
            vmem((TOK, D), BF16),
            vmem((4, 56, LANES), BF16),
            vmem((4, 8, 2, CHIP_ROWS, LANES), BF16),
            vmem((8, TOK, LANES), BF16),
            vmem((8, TOK, LANES), BF16),
            vmem((4, TOK, LANES), F32),
            vmem((8, 2 * CHIP_ROWS, TOK), BF16),
            vmem((8, 2 * CHIP_ROWS, TOK), BF16),
            vmem((PAD_TOK, LANES), BF16),
            vmem((PAD_TOK, LANES), BF16),
            vmem((TOK, LANES), BF16),
            vmem((TOK, LANES), BF16),
            vmem((PAD_TOK, LANES), F32),
            vmem((PAD_TOK, LANES), F32),
            vmem((2, 2, 2, HALO, 128), BF16),
            vmem((2, 2, 2, HALO, 128), BF16),
            vmem((4, TOK, LANES), BF16),
            vmem((4, 8, 2, CHIP_ROWS, LANES), BF16),
            vmem((2, 8, 2, CHIP_ROWS, LANES), BF16),
            vmem((2, 4, 2, 2, CHIP_ROWS, LANES), BF16),
            vmem((2, CHIP_ROWS, LANES), BF16),
            vmem((2, CHIP_ROWS, LANES), BF16),
            vmem((2, CHIP_ROWS, LANES), F32),
            vmem((2, 56, LANES), F32),
            vmem((2, 56, LANES), F32),
            vmem((2, 256, CUT), BF16),
            vmem((2, 256, D - CUT), BF16),
            vmem((3, 2, BLOCK, CUT), BF16),
            vmem((4, BLOCK, D - CUT), BF16),
            vmem((BLOCK, CUT), BF16),
            vmem((BLOCK, CUT), BF16),
            vmem((3, BLOCK, D - CUT), BF16),
            vmem((3, BLOCK, D - CUT), BF16),
            vmem((BLOCK, CUT), F32),
            pltpu.SemaphoreType.DMA((N_COPIES,)),
            pltpu.SemaphoreType.DMA((N_COPIES,)),
            pltpu.SemaphoreType.DMA((2,)),
        ],
        compiler_params=pltpu.CompilerParams(
            collective_id=0, has_side_effects=True, vmem_limit_bytes=56 << 20
        ),
        name="attention_backward",
    )(layer_input, grad_output, qkv_weight.transpose(1, 0, 2), out_weight, tile_image)
    return (grad_input, qkv_grad.transpose(1, 0, 2), out_grad)


def solution(mesh):
    placed = (P("seq", None), P("seq", None), P(), P("seq", None, "tp"), P("seq", "tp"))
    return jax.shard_map(
        per_device,
        mesh=mesh,
        in_specs=placed,
        out_specs=(P("seq", None), P("seq", None, "tp"), P("seq", "tp")),
        check_vma=False,
    )
```

```python
import functools

import jax
import jax.numpy as jnp
from jax import lax
from jax.experimental import pallas as pl
from jax.experimental.pallas import tpu as pltpu
from jax.sharding import PartitionSpec as P

HD = 112
TILE = 128
LANES = 256
TOK = 512
D = 1792
CHIP_ROWS = 112
HALO = 256
PAD_TOK = TOK + 2 * HALO
WINDOW = 768
BLOCK = 64
CUT = 768
FACTOR = float(HD) ** (-0.5)
F32 = jnp.float32
BF16 = jnp.bfloat16
MESH = pl.DeviceIdType.MESH
N_COPIES = 160

NT = (((1,), (1,)), ((), ()))


def dot(a, b):
    return jnp.dot(a, b, preferred_element_type=F32)


def dot_nt(a, b):
    return lax.dot_general(a, b, NT, preferred_element_type=F32)


class Sender:
    def __init__(self, send_sems, recv_sems):
        self.send_sems, self.recv_sems = send_sems, recv_sems
        self.copies = []

    def __call__(self, src, dst, device):
        index = len(self.copies)
        copy = pltpu.make_async_remote_copy(
            src_ref=src,
            dst_ref=dst,
            send_sem=self.send_sems.at[index],
            recv_sem=self.recv_sems.at[index],
            device_id=device,
            device_id_type=MESH,
        )
        copy.start()
        self.copies.append(copy)
        return copy

    def drain(self):
        for copy in self.copies:
            copy.wait_send()


def kernel(
    x_hbm,
    go_hbm,
    qkv_ref,
    out_ref,
    ids_ref,
    gi_ref,
    qkv_grad_ref,
    out_grad_ref,
    own_ref,
    og_ref,
    x_ref,
    go_ref,
    sib_ref,
    w_ref,
    xb_ref,
    gob_ref,
    acc_ref,
    xt_ref,
    got_ref,
    kp_ref,
    vp_ref,
    q_ref,
    u_ref,
    dk_ref,
    dv_ref,
    hs_ref,
    hr_ref,
    gp_ref,
    part_ref,
    ps_ref,
    rb_ref,
    ys_ref,
    yr_ref,
    fin_ref,
    fs_ref,
    fr_ref,
    ga_ref,
    gb_ref,
    ra1_ref,
    rb1_ref,
    sa2_ref,
    ra2_ref,
    sb2_ref,
    rb2_ref,
    suma_ref,
    send_sems,
    recv_sems,
    load_sems,
):
    seq = lax.axis_index("seq")
    tp = lax.axis_index("tp")
    core = lax.rem(seq, 2)
    z = lax.rem(seq // 2, 8)
    yl = seq // 16
    other = 1 - yl

    def at_z(offset):
        return lax.rem(z + 8 + offset, 8)

    def device(yl_, z_, core_):
        return (yl_ * 16 + z_ * 2 + core_, tp)

    sibling = device(yl, z, 1 - core)
    z_next = {1: device(yl, at_z(1), core), -1: device(yl, at_z(-1), core)}
    y_pair = device(other, z, core)
    following = (lax.rem(seq + 1, 32), tp)
    previous = (lax.rem(seq + 31, 32), tp)

    def tp_peer(d):
        return jnp.bitwise_xor(tp, d)

    load_x = pltpu.make_async_copy(x_hbm, x_ref, load_sems.at[0])
    load_go = pltpu.make_async_copy(go_hbm, go_ref, load_sems.at[1])
    load_x.start()
    load_go.start()

    barrier = pltpu.get_barrier_semaphore()
    peers = [sibling, z_next[1], z_next[-1], y_pair, following, previous]
    peers += [(seq, tp_peer(d)) for d in range(1, 8)]

    def spread(rows):
        wide = rows.astype(F32)
        gap = jnp.zeros((wide.shape[0], 128 - HD), F32)
        return jnp.concatenate([wide[:, :HD], gap, wide[:, HD:], gap], axis=1).astype(BF16)

    def close_up(wide):
        return jnp.concatenate([wide[:, :HD], wide[:, 128 : 128 + HD]], axis=1)

    own_ref[0] = spread(qkv_ref[1])
    own_ref[1] = spread(qkv_ref[2])
    own_ref[2] = spread(qkv_ref[0])
    own_ref[3] = spread(out_ref[...])
    for peer in peers:
        pl.semaphore_signal(barrier, inc=1, device_id=peer, device_id_type=MESH)
    pl.semaphore_wait(barrier, len(peers))

    send = Sender(send_sems, recv_sems)
    groups = (core, 2 + core)

    to_sibling = send(own_ref, sib_ref, sibling)
    load_x.wait()

    def split_columns(dst, rows, wide):
        for k in range(8):
            low = wide[:, CHIP_ROWS * k : CHIP_ROWS * (k + 1)]
            high = wide[:, 896 + CHIP_ROWS * k : 896 + CHIP_ROWS * (k + 1)]
            dst[k, rows, 0 : 2 * CHIP_ROWS] = jnp.concatenate([low, high], axis=1).astype(BF16)

    def split_rows(start):
        rows = slice(start, start + 32)
        split_columns(gob_ref, rows, go_ref[rows].astype(F32))

    def norm_rows(start):
        rows = slice(start, start + 32)
        wide = x_ref[rows].astype(F32)
        mean = jnp.mean(wide, axis=-1, keepdims=True)
        center = wide - mean
        inv_std = lax.rsqrt(jnp.mean(center * center, axis=-1, keepdims=True) + 1e-06)
        split_columns(xb_ref, rows, center * inv_std)

    def transpose_block(src, dst, k):
        dst[k] = src[k].T[: 2 * CHIP_ROWS]

    work = [functools.partial(norm_rows, 32 * i) for i in range(16)]
    work += [functools.partial(split_rows, 32 * i) for i in range(16)]
    later = []
    for source, target in ((gob_ref, got_ref), (xb_ref, xt_ref)):
        for k in range(8):
            later.append(functools.partial(transpose_block, source, target, k))
    work.reverse()
    later.reverse()

    def do_some(count):
        for _ in range(count):
            if work or later:
                (work or later).pop()()

    def project(blocks, first=False):
        for g, src in ((0, xb_ref), (1, xb_ref), (2, xb_ref), (3, gob_ref)):
            total = 0.0 if first else acc_ref[g]
            for k in blocks:
                block = w_ref[g, k].reshape(2 * CHIP_ROWS, LANES)
                total += dot(src[k, :, 0 : 2 * CHIP_ROWS], block)
            acc_ref[g] = total

    to_sibling.wait_recv()
    for g in range(4):
        mine = own_ref[g].astype(F32)
        theirs = sib_ref[g].astype(F32)
        low = jnp.where(core == 0, mine, theirs)
        high = jnp.where(core == 0, theirs, mine)
        w_ref[g, z, yl] = jnp.concatenate([low, high], axis=0).astype(BF16)

    ring = {}
    pair = {}
    for i in (0, 1):
        g = groups[i]
        block = w_ref.at[g, z, yl]
        for sign in (1, -1):
            ring[sign, 1, i, 0] = send(block, block, z_next[sign])
        pair[i] = send(block, block, y_pair)
    beside = []
    do_some(4)
    for i in (0, 1):
        block = w_ref.at[groups[i], z, other]
        pair[i].wait_recv()
        for sign in (1, -1):
            ring[sign, 1, i, 1] = send(block, block, z_next[sign])
        beside.append(send(block, block, sibling))

    load_go.wait()
    do_some(6)
    for t in (1, 2, 3, 4):
        before = list(beside)
        beside = []
        for i in (0, 1):
            for side in (0, 1):
                for sign in (1, -1):
                    if (sign, t, i, side) not in ring:
                        continue
                    ring[sign, t, i, side].wait_recv()
                    block = w_ref.at[groups[i], at_z(-sign * t), (yl, other)[side]]
                    if t < 3 or (t == 3 and side == (0 if sign == 1 else 1)):
                        ring[sign, t + 1, i, side] = send(block, block, z_next[sign])
                    beside.append(send(block, block, sibling))
                do_some(2)
        if t == 1:
            do_some(len(work))
        for copy in before:
            copy.wait_recv()
        project([at_z(1 - t), at_z(t - 1)] if t > 1 else [z], t == 1)
    do_some(len(later))
    for copy in beside:
        copy.wait_recv()

    def weights(g):
        return jnp.concatenate([w_ref[g, :, y].reshape(896, LANES) for y in (0, 1)], axis=0)

    halo = []
    def finished(g):
        src = gob_ref if g == 3 else xb_ref
        k = at_z(4)
        block = w_ref[g, k].reshape(2 * CHIP_ROWS, LANES)
        return (acc_ref[g] + dot(src[k, :, 0 : 2 * CHIP_ROWS], block)).astype(BF16)

    for g, ref in ((0, kp_ref), (1, vp_ref)):
        ref[HALO : HALO + TOK] = finished(g)
        halo.append(send(ref.at[pl.ds(HALO, HALO)], ref.at[pl.ds(HALO + TOK, HALO)], previous))
        halo.append(send(ref.at[pl.ds(TOK, HALO)], ref.at[pl.ds(0, HALO)], following))
    q_ref[...] = finished(2)
    u_ref[...] = finished(3)

    def tile_id(tile):
        inside = jnp.logical_and(tile >= 0, tile < 128)
        value = ids_ref[jnp.clip(tile, 0, 127)]
        return jnp.where(inside, value, -1)

    key_ids = [tile_id(4 * seq - 2 + k) for k in range(8)]
    lane = lax.broadcasted_iota(jnp.int32, (1, 256), 1)
    for copy in halo:
        copy.wait_recv()

    back = []
    for h in (0, 1):
        lanes = slice(128 * h, 128 * h + 128)
        key_t = kp_ref[:, lanes].T
        value_t = vp_ref[:, lanes].T
        for half in (0, 1):
            keys = slice(256 * half, 256 * half + WINDOW)
            rows = slice(256 * half, 256 * half + 256)
            query = q_ref[rows, lanes]
            up = u_ref[rows, lanes]
            key = kp_ref[keys, lanes]
            value = vp_ref[keys, lanes]
            scores = dot_nt(key, query) * FACTOR
            query_id = jnp.where(lane < 128, key_ids[2 + 2 * half], key_ids[3 + 2 * half])
            parts = []
            for k in range(6):
                allowed = query_id == key_ids[2 * half + k]
                parts.append(jnp.where(allowed, jnp.exp(scores[128 * k : 128 * k + 128]), 0.0))
            exponent = jnp.concatenate(parts, axis=0)
            prob = exponent * (1.0 / jnp.sum(exponent, axis=0, keepdims=True))
            prob_low = prob.astype(BF16)
            attended = dot(value_t[:, keys], prob_low)
            delta = jnp.sum(up.astype(F32).T * attended, axis=0, keepdims=True)
            dprob = dot_nt(value, up)
            dscore = (prob * (dprob - delta) * FACTOR).astype(BF16)
            dquery = dot(key_t[:, keys], dscore)
            gp_ref[2, rows, lanes] = dquery.T.astype(BF16)
            gp_ref[3, rows, lanes] = attended.T.astype(BF16)
            dkey = dot(dscore, query)
            dvalue = dot(prob_low, up)
            for ref, grad in ((dk_ref, dkey), (dv_ref, dvalue)):
                if half == 0:
                    ref[0:WINDOW, lanes] = grad
                else:
                    ref[256:WINDOW, lanes] += grad[: WINDOW - 256]
                    ref[WINDOW:PAD_TOK, lanes] = grad[WINDOW - 256 :]
        for j, ref in ((0, dk_ref), (1, dv_ref)):
            hs_ref[h, j, 0] = ref[0:HALO, lanes].astype(BF16)
            hs_ref[h, j, 1] = ref[HALO + TOK : PAD_TOK, lanes].astype(BF16)
            back.append(send(hs_ref.at[h, j, 0], hr_ref.at[h, j, 0], previous))
            back.append(send(hs_ref.at[h, j, 1], hr_ref.at[h, j, 1], following))

    def weight_grad(g):
        src = got_ref if g == 3 else xt_ref

        def body(i, _):
            blocks = pl.ds(i * 4, 4)
            grad = dot(src[blocks].reshape(896, TOK), gp_ref[g]).astype(BF16)
            part_ref[g, blocks] = grad.reshape(4, 2, CHIP_ROWS, LANES)
            return 0

        lax.fori_loop(0, 2, body, 0)

    weight_grad(2)
    weight_grad(3)
    swap = {1: send(part_ref.at[3 - core], ps_ref.at[1], sibling)}
    for copy in back:
        copy.wait_recv()
    for h in (0, 1):
        lanes = slice(128 * h, 128 * h + 128)
        for j, ref in ((0, dk_ref), (1, dv_ref)):
            low = ref[HALO : 2 * HALO, lanes] + hr_ref[h, j, 1].astype(F32)
            high = ref[2 * HALO : 3 * HALO, lanes] + hr_ref[h, j, 0].astype(F32)
            gp_ref[j, 0:HALO, lanes] = low.astype(BF16)
            gp_ref[j, HALO:TOK, lanes] = high.astype(BF16)

    yh, xx = tp // 4, lax.rem(tp, 4)
    y_other = (seq, (1 - yh) * 4 + xx)

    def x_at(e):
        return lax.rem(xx + e, 4)

    def x_peer(e):
        return (seq, yh * 4 + x_at(e))

    def block_at(e):
        return pl.ds(pl.multiple_of(x_at(e) * BLOCK, BLOCK), BLOCK)

    def partial_norm(half, start, stop):
        rows = pl.ds(pl.multiple_of(half * 256, 256), 256)
        total = dot_nt(gp_ref[0, rows], weights(0)[start:stop])
        total += dot_nt(gp_ref[1, rows], weights(1)[start:stop])
        total += dot_nt(gp_ref[2, rows], weights(2)[start:stop])
        return total.astype(BF16)

    gb_ref[1 - yh] = partial_norm(1 - yh, CUT, D)
    y_first = {}
    for e in (1, 3, 2, 0):
        y_first[e] = send(gb_ref.at[1 - yh, block_at(e)], rb1_ref.at[e], y_other)
    for half in (0, 1):
        ga_ref[half] = partial_norm(half, 0, CUT)
    x_first = [send(ga_ref.at[:, block_at(e)], ra1_ref.at[e - 1], x_peer(e)) for e in (1, 3, 2)]
    gb_ref[yh] = partial_norm(yh, CUT, D)


    chain = {}

    def ring_step(t, i):
        g = groups[i]
        if t == 4:
            swap[i].wait_recv()
        for side in (0, 1):
            y = (yl, other)[side]
            for sign in (1, -1):
                if t == 4 and side != (0 if sign == 1 else 1):
                    continue
                zz = at_z(sign * t)
                total = part_ref[g, zz, y].astype(F32) + ps_ref[i, zz, y].astype(F32)
                if (sign, t + 1, i, side) in chain:
                    chain[sign, t + 1, i, side].wait_recv()
                    total += rb_ref[(sign + 1) // 2, t, i, side].astype(F32)
                part_ref[g, zz, y] = total.astype(BF16)
                chain[sign, t, i, side] = send(
                    part_ref.at[g, zz, y],
                    rb_ref.at[(sign + 1) // 2, t - 1, i, side],
                    z_next[sign],
                )

    y_copies = {}

    def y_stage(i):
        g = groups[i]
        for side in (1, 0):
            y = (yl, other)[side]
            total = part_ref[g, z, y].astype(F32) + ps_ref[i, z, y].astype(F32)
            for sign in (1, -1):
                chain[sign, 1, i, side].wait_recv()
                total += rb_ref[(sign + 1) // 2, 0, i, side].astype(F32)
            if side == 1:
                ys_ref[i] = total.astype(BF16)
                y_copies[i] = send(ys_ref.at[i], yr_ref.at[i], y_pair)
            else:
                fin_ref[i] = total

    ring_step(4, 1)
    weight_grad(0)
    weight_grad(1)
    swap[0] = send(part_ref.at[1 - core], ps_ref.at[0], sibling)
    ring_step(3, 1)

    x_second = []
    for e in (1, 3, 2):
        y_first[e].wait_recv()
        total = gb_ref[yh, block_at(e)].astype(F32) + rb1_ref[e].astype(F32)
        sb2_ref[e - 1] = total.astype(BF16)
        x_second.append(send(sb2_ref.at[e - 1], rb2_ref.at[e - 1], x_peer(e)))
        if e == 3:
            ring_step(4, 0)
    ring_step(2, 1)

    for copy in x_first:
        copy.wait_recv()
    sums = []
    for half in (1 - yh, yh):
        total = ga_ref[half, block_at(0)].astype(F32)
        for e in (1, 2, 3):
            total += ra1_ref[e - 1, half].astype(F32)
        sums.append(total)
        if len(sums) == 1:
            sa2_ref[...] = total.astype(BF16)
            y_second = send(sa2_ref, ra2_ref, y_other)
    suma_ref[...] = sums[1]
    ring_step(3, 0)
    ring_step(1, 1)

    y_second.wait_recv()
    y_first[0].wait_recv()
    for copy in x_second:
        copy.wait_recv()

    def norm_back(i, _):
        rows = pl.ds(pl.multiple_of(tp * BLOCK + i * 16, 16), 16)
        part = pl.ds(pl.multiple_of(i * 16, 16), 16)
        own_part = pl.ds(pl.multiple_of(xx * BLOCK + i * 16, 16), 16)
        first = suma_ref[part] + ra2_ref[part].astype(F32)
        second = gb_ref[yh, own_part].astype(F32) + rb1_ref[0, part].astype(F32)
        for e in range(3):
            second += rb2_ref[e, part].astype(F32)
        total = jnp.concatenate([first, second], axis=1)
        wide = x_ref[rows].astype(F32)
        center = wide - jnp.mean(wide, axis=-1, keepdims=True)
        inv_std = lax.rsqrt(jnp.mean(center * center, axis=-1, keepdims=True) + 1e-06)
        normed = center * inv_std
        grad = inv_std * (
            total
            - jnp.mean(total, axis=-1, keepdims=True)
            - normed * jnp.mean(total * normed, axis=-1, keepdims=True)
        )
        gi_ref[rows] = grad.astype(BF16)
        return 0

    lax.fori_loop(0, BLOCK // 16, norm_back, 0)

    def rows_of(y, x):
        return pl.ds(pl.multiple_of((y * 4 + x) * BLOCK, BLOCK), BLOCK)

    def share(y, x, columns, to):
        piece = gi_ref.at[rows_of(y, x), columns]
        return send(piece, piece, to)

    first, second = pl.ds(0, CUT), pl.ds(CUT, D - CUT)
    y_gather = [share(yh, xx, first, y_other)]
    x_gather = {e: share(yh, xx, second, x_peer(e)) for e in (1, 3, 2)}
    y_gather.append(share(yh, xx, second, y_other))
    gather = [share(yh, xx, first, x_peer(e)) for e in (1, 3, 2)]
    gather.append(y_gather[1])
    ring_step(2, 0)
    y_stage(1)
    y_gather[0].wait_recv()
    for e in (1, 3, 2):
        gather.append(share(1 - yh, xx, first, x_peer(e)))
    for e in (1, 3, 2):
        x_gather[e].wait_recv()
        gather.append(share(yh, x_at(-e + 4), second, y_other))

    ring_step(1, 0)
    y_stage(0)
    own_rows = pl.ds(pl.multiple_of(56 * core, 8), 56)
    sib_rows = pl.ds(pl.multiple_of(56 * (1 - core), 8), 56)
    for i in (0, 1):
        y_copies[i].wait_recv()
        fin_ref[i] += yr_ref[i].astype(F32)
        fs_ref[i] = fin_ref[i, sib_rows]
        og_ref[groups[i]] = fin_ref[i, own_rows]
    last = send(fs_ref, fr_ref, sibling)
    last.wait_recv()
    og_ref[1 - core] = fr_ref[0]
    og_ref[3 - core] = fr_ref[1]
    for c, g in ((0, 2), (1, 0), (2, 1)):
        qkv_grad_ref[c] = close_up(og_ref[g])
    out_grad_ref[...] = close_up(og_ref[3])

    for copy in gather:
        copy.wait_recv()
    send.drain()


def publish(gi, qkv_grad, out_grad, gi_out, qkv_out, out_out, sems):
    copies = []
    for i in range(4):
        rows = pl.ds(i * (TOK // 4), TOK // 4)
        copies.append(pltpu.make_async_copy(gi.at[rows], gi_out.at[rows], sems.at[i]))
    copies.append(pltpu.make_async_copy(qkv_grad, qkv_out, sems.at[4]))
    copies.append(pltpu.make_async_copy(out_grad, out_out, sems.at[5]))
    for copy in copies:
        copy.start()
    for copy in copies:
        copy.wait()


def per_device(layer_input, grad_output, tile_image, qkv_weight, out_weight):
    vmem = pltpu.VMEM
    shapes = (
        jax.ShapeDtypeStruct((TOK, D), BF16),
        jax.ShapeDtypeStruct((3, 56, 2 * HD), F32),
        jax.ShapeDtypeStruct((56, 2 * HD), F32),
    )
    results = pl.pallas_call(
        kernel,
        out_shape=shapes,
        in_specs=[
            pl.BlockSpec(memory_space=pl.ANY),
            pl.BlockSpec(memory_space=pl.ANY),
            pl.BlockSpec(memory_space=pltpu.VMEM),
            pl.BlockSpec(memory_space=pltpu.VMEM),
            pl.BlockSpec(memory_space=pltpu.SMEM),
        ],
        out_specs=(
            pl.BlockSpec(memory_space=pltpu.VMEM),
            pl.BlockSpec(memory_space=pltpu.VMEM),
            pl.BlockSpec(memory_space=pltpu.VMEM),
        ),
        scratch_shapes=[
            vmem((4, 56, LANES), BF16),
            vmem((4, 56, LANES), F32),
            vmem((TOK, D), BF16),
            vmem((TOK, D), BF16),
            vmem((4, 56, LANES), BF16),
            vmem((4, 8, 2, CHIP_ROWS, LANES), BF16),
            vmem((8, TOK, LANES), BF16),
            vmem((8, TOK, LANES), BF16),
            vmem((4, TOK, LANES), F32),
            vmem((8, 2 * CHIP_ROWS, TOK), BF16),
            vmem((8, 2 * CHIP_ROWS, TOK), BF16),
            vmem((PAD_TOK, LANES), BF16),
            vmem((PAD_TOK, LANES), BF16),
            vmem((TOK, LANES), BF16),
            vmem((TOK, LANES), BF16),
            vmem((PAD_TOK, LANES), F32),
            vmem((PAD_TOK, LANES), F32),
            vmem((2, 2, 2, HALO, 128), BF16),
            vmem((2, 2, 2, HALO, 128), BF16),
            vmem((4, TOK, LANES), BF16),
            vmem((4, 8, 2, CHIP_ROWS, LANES), BF16),
            vmem((2, 8, 2, CHIP_ROWS, LANES), BF16),
            vmem((2, 4, 2, 2, CHIP_ROWS, LANES), BF16),
            vmem((2, CHIP_ROWS, LANES), BF16),
            vmem((2, CHIP_ROWS, LANES), BF16),
            vmem((2, CHIP_ROWS, LANES), F32),
            vmem((2, 56, LANES), F32),
            vmem((2, 56, LANES), F32),
            vmem((2, 256, CUT), BF16),
            vmem((2, 256, D - CUT), BF16),
            vmem((3, 2, BLOCK, CUT), BF16),
            vmem((4, BLOCK, D - CUT), BF16),
            vmem((BLOCK, CUT), BF16),
            vmem((BLOCK, CUT), BF16),
            vmem((3, BLOCK, D - CUT), BF16),
            vmem((3, BLOCK, D - CUT), BF16),
            vmem((BLOCK, CUT), F32),
            pltpu.SemaphoreType.DMA((N_COPIES,)),
            pltpu.SemaphoreType.DMA((N_COPIES,)),
            pltpu.SemaphoreType.DMA((2,)),
        ],
        compiler_params=pltpu.CompilerParams(
            collective_id=0, has_side_effects=True, vmem_limit_bytes=56 << 20
        ),
        name="attention_backward",
    )(layer_input, grad_output, qkv_weight.transpose(1, 0, 2), out_weight, tile_image)
    grad_input, qkv_grad, out_grad = pl.pallas_call(
        publish,
        out_shape=shapes,
        in_specs=[pl.BlockSpec(memory_space=pl.ANY)] * 3,
        out_specs=[pl.BlockSpec(memory_space=pl.ANY)] * 3,
        scratch_shapes=[pltpu.SemaphoreType.DMA((6,))],
        name="publish",
    )(*results)
    return (grad_input, qkv_grad.transpose(1, 0, 2), out_grad)


def solution(mesh):
    placed = (P("seq", None), P("seq", None), P(), P("seq", None, "tp"), P("seq", "tp"))
    return jax.shard_map(
        per_device,
        mesh=mesh,
        in_specs=placed,
        out_specs=(P("seq", None), P("seq", None, "tp"), P("seq", "tp")),
        check_vma=False,
    )
```

```python
import functools

import jax
import jax.numpy as jnp
from jax import lax
from jax.experimental import pallas as pl
from jax.experimental.pallas import tpu as pltpu
from jax.sharding import PartitionSpec as P

HD = 112
TILE = 128
LANES = 256
TOK = 512
D = 1792
CHIP_ROWS = 112
HALO = 256
PAD_TOK = TOK + 2 * HALO
WINDOW = 768
BLOCK = 64
CUT = 768
PACK = 512
FACTOR = float(HD) ** (-0.5)
F32 = jnp.float32
BF16 = jnp.bfloat16
MESH = pl.DeviceIdType.MESH
N_COPIES = 160

NT = (((1,), (1,)), ((), ()))


def dot(a, b):
    return jnp.dot(a, b, preferred_element_type=F32)


def dot_nt(a, b):
    return lax.dot_general(a, b, NT, preferred_element_type=F32)


class Sender:
    def __init__(self, send_sems, recv_sems):
        self.send_sems, self.recv_sems = send_sems, recv_sems
        self.copies = []

    def __call__(self, src, dst, device):
        index = len(self.copies)
        copy = pltpu.make_async_remote_copy(
            src_ref=src,
            dst_ref=dst,
            send_sem=self.send_sems.at[index],
            recv_sem=self.recv_sems.at[index],
            device_id=device,
            device_id_type=MESH,
        )
        copy.start()
        self.copies.append(copy)
        return copy

    def drain(self):
        for copy in self.copies:
            copy.wait_send()


def kernel(
    x_hbm,
    go_hbm,
    qkv_ref,
    out_ref,
    ids_ref,
    gi_ref,
    qkv_grad_ref,
    out_grad_ref,
    og_ref,
    x_ref,
    go_ref,
    wp_ref,
    wq_ref,
    w_ref,
    xb_ref,
    gob_ref,
    acc_ref,
    xt_ref,
    got_ref,
    kp_ref,
    vp_ref,
    q_ref,
    u_ref,
    dk_ref,
    dv_ref,
    hs_ref,
    hr_ref,
    gp_ref,
    part_ref,
    ps_ref,
    rb_ref,
    ys_ref,
    yr_ref,
    fin_ref,
    fs_ref,
    fr_ref,
    ga_ref,
    gb_ref,
    ra1_ref,
    rb1_ref,
    sa2_ref,
    ra2_ref,
    sb2_ref,
    rb2_ref,
    suma_ref,
    send_sems,
    recv_sems,
    load_sems,
):
    seq = lax.axis_index("seq")
    tp = lax.axis_index("tp")
    core = lax.rem(seq, 2)
    z = lax.rem(seq // 2, 8)
    yl = seq // 16
    other = 1 - yl

    def at_z(offset):
        return lax.rem(z + 8 + offset, 8)

    def device(yl_, z_, core_):
        return (yl_ * 16 + z_ * 2 + core_, tp)

    sibling = device(yl, z, 1 - core)
    z_next = {1: device(yl, at_z(1), core), -1: device(yl, at_z(-1), core)}
    y_pair = device(other, z, core)
    following = (lax.rem(seq + 1, 32), tp)
    previous = (lax.rem(seq + 31, 32), tp)

    def tp_peer(d):
        return jnp.bitwise_xor(tp, d)

    load_x = pltpu.make_async_copy(x_hbm, x_ref, load_sems.at[0])
    load_go = pltpu.make_async_copy(go_hbm, go_ref, load_sems.at[1])
    load_x.start()
    load_go.start()

    barrier = pltpu.get_barrier_semaphore()
    peers = [sibling, z_next[1], z_next[-1], y_pair, following, previous]
    peers += [(seq, tp_peer(d)) for d in range(1, 8)]

    def close_up(wide):
        return jnp.concatenate([wide[:, :HD], wide[:, 128 : 128 + HD]], axis=1)

    own = [qkv_ref[1], qkv_ref[2], qkv_ref[0], out_ref[...]]
    own = jnp.concatenate([rows.astype(F32) for rows in own], axis=1).astype(BF16)
    wp_ref[z, yl, core] = own[:, :PACK]
    wq_ref[z, yl, core] = own[:, PACK:]
    for peer in peers:
        pl.semaphore_signal(barrier, inc=1, device_id=peer, device_id_type=MESH)
    pl.semaphore_wait(barrier, len(peers))

    send = Sender(send_sems, recv_sems)
    groups = (core, 2 + core)

    first_own = wp_ref.at[z, yl, core]
    second_own = wq_ref.at[z, yl, core]
    ring, cross, relay, beside = {}, {}, {}, {t: [] for t in range(6)}
    for sign in (1, -1):
        ring[sign, 1, 0] = send(first_own, first_own, z_next[sign])
    cross = send(first_own, first_own, y_pair)
    for sign in (1, -1):
        ring[sign, 1, 2] = send(second_own, second_own, z_next[sign])
    relay[0] = [send(second_own, second_own, y_pair)]
    beside[0].append(send(first_own, first_own, sibling))
    beside[0].append(send(second_own, second_own, sibling))
    load_x.wait()

    def split_columns(dst, rows, wide):
        for k in range(8):
            low = wide[:, CHIP_ROWS * k : CHIP_ROWS * (k + 1)]
            high = wide[:, 896 + CHIP_ROWS * k : 896 + CHIP_ROWS * (k + 1)]
            dst[k, rows, 0 : 2 * CHIP_ROWS] = jnp.concatenate([low, high], axis=1).astype(BF16)

    def split_rows(start):
        rows = slice(start, start + 32)
        split_columns(gob_ref, rows, go_ref[rows].astype(F32))

    def norm_rows(start):
        rows = slice(start, start + 32)
        wide = x_ref[rows].astype(F32)
        mean = jnp.mean(wide, axis=-1, keepdims=True)
        center = wide - mean
        inv_std = lax.rsqrt(jnp.mean(center * center, axis=-1, keepdims=True) + 1e-06)
        split_columns(xb_ref, rows, center * inv_std)

    def transpose_block(src, dst, k):
        dst[k] = src[k].T[: 2 * CHIP_ROWS]

    work = [functools.partial(norm_rows, 32 * i) for i in range(16)]
    work += [functools.partial(split_rows, 32 * i) for i in range(16)]
    later = []
    for source, target in ((gob_ref, got_ref), (xb_ref, xt_ref)):
        for k in range(8):
            later.append(functools.partial(transpose_block, source, target, k))
    work.reverse()
    later.reverse()

    def do_some(count):
        for _ in range(count):
            if work or later:
                (work or later).pop()()

    def unpack(k):
        first = wp_ref[k].astype(F32).reshape(2 * CHIP_ROWS, PACK)
        second = wq_ref[k].astype(F32).reshape(2 * CHIP_ROWS, 8 * HD - PACK)
        packed = jnp.concatenate([first, second], axis=1)
        gap = jnp.zeros((2 * CHIP_ROWS, 128 - HD), F32)
        for g in range(4):
            low = packed[:, 2 * HD * g : 2 * HD * g + HD]
            high = packed[:, 2 * HD * g + HD : 2 * HD * (g + 1)]
            wide = jnp.concatenate([low, gap, high, gap], axis=1).astype(BF16)
            w_ref[g, k] = wide.reshape(2, CHIP_ROWS, LANES)

    def project(blocks, first=False):
        for k in blocks:
            unpack(k)
        for g, src in ((0, xb_ref), (1, xb_ref), (2, xb_ref), (3, gob_ref)):
            total = 0.0 if first else acc_ref[g]
            for k in blocks:
                block = w_ref[g, k].reshape(2 * CHIP_ROWS, LANES)
                total += dot(src[k, :, 0 : 2 * CHIP_ROWS], block)
            acc_ref[g] = total

    block = wp_ref.at[z, other, core]
    cross.wait_recv()
    for sign in (1, -1):
        ring[sign, 1, 1] = send(block, block, z_next[sign])
    beside[0].append(send(block, block, sibling))
    load_go.wait()
    do_some(4)

    def piece(kind, k):
        ref = wq_ref if kind == 2 else wp_ref
        return ref.at[k, other if kind == 1 else yl, core]

    turn = 1 - 2 * core
    turned = device(yl, at_z(turn), core)
    for t in (1, 2, 3, 4):
        relay[t] = []
        for kind in (0, 2, 1):
            for sign in (1, -1):
                if (sign, t, kind) not in ring:
                    continue
                ring[sign, t, kind].wait_recv()
                block = piece(kind, at_z(-sign * t))
                if t < 3 or (t == 3 and kind < 2 and sign == (1, -1)[kind]):
                    ring[sign, t + 1, kind] = send(block, block, z_next[sign])
                if t == 3 and kind == 2 and sign == -1:
                    farthest = piece(kind, at_z(-turn * t))
                    ring[1, 4, 2] = send(farthest, farthest, turned)
                if kind == 2:
                    relay[t].append(send(block, block, y_pair))
                beside[t].append(send(block, block, sibling))
            do_some(3)
        spots = [z] if t == 1 else [at_z(1 - t), at_z(t - 1)]
        for copy, k in zip(relay[t - 1], spots):
            copy.wait_recv()
            block = wq_ref.at[k, other, core]
            beside[t - 1].append(send(block, block, sibling))
        if t == 2:
            do_some(len(work))
            for copy in beside[0]:
                copy.wait_recv()
            project([z], True)
        if t > 2:
            for copy in beside[t - 2]:
                copy.wait_recv()
            project([at_z(2 - t), at_z(t - 2)])
    relay[4][0].wait_recv()
    block = wq_ref.at[at_z(4), other, core]
    beside[4].append(send(block, block, sibling))
    for copy in beside[3]:
        copy.wait_recv()
    project([at_z(-3), at_z(3)])
    do_some(len(later))
    for copy in beside[4]:
        copy.wait_recv()
    unpack(at_z(4))

    def weights(g):
        return jnp.concatenate([w_ref[g, :, y].reshape(896, LANES) for y in (0, 1)], axis=0)

    halo = []
    def finished(g):
        src = gob_ref if g == 3 else xb_ref
        k = at_z(4)
        block = w_ref[g, k].reshape(2 * CHIP_ROWS, LANES)
        return (acc_ref[g] + dot(src[k, :, 0 : 2 * CHIP_ROWS], block)).astype(BF16)

    for g, ref in ((0, kp_ref), (1, vp_ref)):
        ref[HALO : HALO + TOK] = finished(g)
        halo.append(send(ref.at[pl.ds(HALO, HALO)], ref.at[pl.ds(HALO + TOK, HALO)], previous))
        halo.append(send(ref.at[pl.ds(TOK, HALO)], ref.at[pl.ds(0, HALO)], following))
    q_ref[...] = finished(2)
    u_ref[...] = finished(3)

    def tile_id(tile):
        inside = jnp.logical_and(tile >= 0, tile < 128)
        value = ids_ref[jnp.clip(tile, 0, 127)]
        return jnp.where(inside, value, -1)

    key_ids = [tile_id(4 * seq - 2 + k) for k in range(8)]
    lane = lax.broadcasted_iota(jnp.int32, (1, 256), 1)
    for copy in halo:
        copy.wait_recv()

    back = []
    for h in (0, 1):
        lanes = slice(128 * h, 128 * h + 128)
        key_t = kp_ref[:, lanes].T
        value_t = vp_ref[:, lanes].T
        for half in (0, 1):
            keys = slice(256 * half, 256 * half + WINDOW)
            rows = slice(256 * half, 256 * half + 256)
            query = q_ref[rows, lanes]
            up = u_ref[rows, lanes]
            key = kp_ref[keys, lanes]
            value = vp_ref[keys, lanes]
            scores = dot_nt(key, query) * FACTOR
            query_id = jnp.where(lane < 128, key_ids[2 + 2 * half], key_ids[3 + 2 * half])
            parts = []
            for k in range(6):
                allowed = query_id == key_ids[2 * half + k]
                parts.append(jnp.where(allowed, jnp.exp(scores[128 * k : 128 * k + 128]), 0.0))
            exponent = jnp.concatenate(parts, axis=0)
            prob = exponent * (1.0 / jnp.sum(exponent, axis=0, keepdims=True))
            prob_low = prob.astype(BF16)
            attended = dot(value_t[:, keys], prob_low)
            delta = jnp.sum(up.astype(F32).T * attended, axis=0, keepdims=True)
            dprob = dot_nt(value, up)
            dscore = (prob * (dprob - delta) * FACTOR).astype(BF16)
            dquery = dot(key_t[:, keys], dscore)
            gp_ref[2, rows, lanes] = dquery.T.astype(BF16)
            gp_ref[3, rows, lanes] = attended.T.astype(BF16)
            dkey = dot(dscore, query)
            dvalue = dot(prob_low, up)
            for ref, grad in ((dk_ref, dkey), (dv_ref, dvalue)):
                if half == 0:
                    ref[0:WINDOW, lanes] = grad
                else:
                    ref[256:WINDOW, lanes] += grad[: WINDOW - 256]
                    ref[WINDOW:PAD_TOK, lanes] = grad[WINDOW - 256 :]
        for j, ref in ((0, dk_ref), (1, dv_ref)):
            hs_ref[h, j, 0] = ref[0:HALO, lanes].astype(BF16)
            hs_ref[h, j, 1] = ref[HALO + TOK : PAD_TOK, lanes].astype(BF16)
            back.append(send(hs_ref.at[h, j, 0], hr_ref.at[h, j, 0], previous))
            back.append(send(hs_ref.at[h, j, 1], hr_ref.at[h, j, 1], following))

    def weight_grad(g):
        src = got_ref if g == 3 else xt_ref

        def body(i, _):
            blocks = pl.ds(i * 4, 4)
            grad = dot(src[blocks].reshape(896, TOK), gp_ref[g]).astype(BF16)
            part_ref[g, blocks] = grad.reshape(4, 2, CHIP_ROWS, LANES)
            return 0

        lax.fori_loop(0, 2, body, 0)

    weight_grad(2)
    weight_grad(3)
    swap = {1: send(part_ref.at[3 - core], ps_ref.at[1], sibling)}
    for copy in back:
        copy.wait_recv()
    for h in (0, 1):
        lanes = slice(128 * h, 128 * h + 128)
        for j, ref in ((0, dk_ref), (1, dv_ref)):
            low = ref[HALO : 2 * HALO, lanes] + hr_ref[h, j, 1].astype(F32)
            high = ref[2 * HALO : 3 * HALO, lanes] + hr_ref[h, j, 0].astype(F32)
            gp_ref[j, 0:HALO, lanes] = low.astype(BF16)
            gp_ref[j, HALO:TOK, lanes] = high.astype(BF16)

    yh, xx = tp // 4, lax.rem(tp, 4)
    y_other = (seq, (1 - yh) * 4 + xx)

    def x_at(e):
        return lax.rem(xx + e, 4)

    def x_peer(e):
        return (seq, yh * 4 + x_at(e))

    def block_at(e):
        return pl.ds(pl.multiple_of(x_at(e) * BLOCK, BLOCK), BLOCK)

    def partial_norm(half, start, stop):
        rows = pl.ds(pl.multiple_of(half * 256, 256), 256)
        total = dot_nt(gp_ref[0, rows], weights(0)[start:stop])
        total += dot_nt(gp_ref[1, rows], weights(1)[start:stop])
        total += dot_nt(gp_ref[2, rows], weights(2)[start:stop])
        return total.astype(BF16)

    gb_ref[1 - yh] = partial_norm(1 - yh, CUT, D)
    y_first = {}
    for e in (1, 3, 2, 0):
        y_first[e] = send(gb_ref.at[1 - yh, block_at(e)], rb1_ref.at[e], y_other)
    for half in (0, 1):
        ga_ref[half] = partial_norm(half, 0, CUT)
    x_first = [send(ga_ref.at[:, block_at(e)], ra1_ref.at[e - 1], x_peer(e)) for e in (1, 3, 2)]
    gb_ref[yh] = partial_norm(yh, CUT, D)


    chain = {}

    def ring_step(t, i):
        g = groups[i]
        if t == 4:
            swap[i].wait_recv()
        for side in (0, 1):
            y = (yl, other)[side]
            for sign in (1, -1):
                if t == 4 and side != (0 if sign == 1 else 1):
                    continue
                zz = at_z(sign * t)
                total = part_ref[g, zz, y].astype(F32) + ps_ref[i, zz, y].astype(F32)
                if (sign, t + 1, i, side) in chain:
                    chain[sign, t + 1, i, side].wait_recv()
                    total += rb_ref[(sign + 1) // 2, t, i, side].astype(F32)
                part_ref[g, zz, y] = total.astype(BF16)
                chain[sign, t, i, side] = send(
                    part_ref.at[g, zz, y],
                    rb_ref.at[(sign + 1) // 2, t - 1, i, side],
                    z_next[sign],
                )

    y_copies = {}

    def y_stage(i):
        g = groups[i]
        for side in (1, 0):
            y = (yl, other)[side]
            total = part_ref[g, z, y].astype(F32) + ps_ref[i, z, y].astype(F32)
            for sign in (1, -1):
                chain[sign, 1, i, side].wait_recv()
                total += rb_ref[(sign + 1) // 2, 0, i, side].astype(F32)
            if side == 1:
                ys_ref[i] = total.astype(BF16)
                y_copies[i] = send(ys_ref.at[i], yr_ref.at[i], y_pair)
            else:
                fin_ref[i] = total

    ring_step(4, 1)
    weight_grad(0)
    weight_grad(1)
    swap[0] = send(part_ref.at[1 - core], ps_ref.at[0], sibling)
    ring_step(3, 1)

    x_second = []
    for e in (1, 3, 2):
        y_first[e].wait_recv()
        total = gb_ref[yh, block_at(e)].astype(F32) + rb1_ref[e].astype(F32)
        sb2_ref[e - 1] = total.astype(BF16)
        x_second.append(send(sb2_ref.at[e - 1], rb2_ref.at[e - 1], x_peer(e)))
        if e == 3:
            ring_step(4, 0)
    ring_step(2, 1)

    for copy in x_first:
        copy.wait_recv()
    sums = []
    for half in (1 - yh, yh):
        total = ga_ref[half, block_at(0)].astype(F32)
        for e in (1, 2, 3):
            total += ra1_ref[e - 1, half].astype(F32)
        sums.append(total)
        if len(sums) == 1:
            sa2_ref[...] = total.astype(BF16)
            y_second = send(sa2_ref, ra2_ref, y_other)
    suma_ref[...] = sums[1]
    ring_step(3, 0)
    ring_step(1, 1)

    y_second.wait_recv()
    y_first[0].wait_recv()
    for copy in x_second:
        copy.wait_recv()

    def norm_back(i, _):
        rows = pl.ds(pl.multiple_of(tp * BLOCK + i * 16, 16), 16)
        part = pl.ds(pl.multiple_of(i * 16, 16), 16)
        own_part = pl.ds(pl.multiple_of(xx * BLOCK + i * 16, 16), 16)
        first = suma_ref[part] + ra2_ref[part].astype(F32)
        second = gb_ref[yh, own_part].astype(F32) + rb1_ref[0, part].astype(F32)
        for e in range(3):
            second += rb2_ref[e, part].astype(F32)
        total = jnp.concatenate([first, second], axis=1)
        wide = x_ref[rows].astype(F32)
        center = wide - jnp.mean(wide, axis=-1, keepdims=True)
        inv_std = lax.rsqrt(jnp.mean(center * center, axis=-1, keepdims=True) + 1e-06)
        normed = center * inv_std
        grad = inv_std * (
            total
            - jnp.mean(total, axis=-1, keepdims=True)
            - normed * jnp.mean(total * normed, axis=-1, keepdims=True)
        )
        gi_ref[rows] = grad.astype(BF16)
        return 0

    lax.fori_loop(0, BLOCK // 16, norm_back, 0)

    def rows_of(y, x):
        return pl.ds(pl.multiple_of((y * 4 + x) * BLOCK, BLOCK), BLOCK)

    def share(y, x, columns, to):
        piece = gi_ref.at[rows_of(y, x), columns]
        return send(piece, piece, to)

    first, second = pl.ds(0, CUT), pl.ds(CUT, D - CUT)
    y_gather = [share(yh, xx, first, y_other)]
    x_gather = {e: share(yh, xx, second, x_peer(e)) for e in (1, 3, 2)}
    y_gather.append(share(yh, xx, second, y_other))
    gather = [share(yh, xx, first, x_peer(e)) for e in (1, 3, 2)]
    gather.append(y_gather[1])
    ring_step(2, 0)
    y_stage(1)
    y_gather[0].wait_recv()
    for e in (1, 3, 2):
        gather.append(share(1 - yh, xx, first, x_peer(e)))
    for e in (1, 3, 2):
        x_gather[e].wait_recv()
        gather.append(share(yh, x_at(-e + 4), second, y_other))

    ring_step(1, 0)
    y_stage(0)
    own_rows = pl.ds(pl.multiple_of(56 * core, 8), 56)
    sib_rows = pl.ds(pl.multiple_of(56 * (1 - core), 8), 56)
    for i in (0, 1):
        y_copies[i].wait_recv()
        fin_ref[i] += yr_ref[i].astype(F32)
        fs_ref[i] = fin_ref[i, sib_rows]
        og_ref[groups[i]] = fin_ref[i, own_rows]
    last = send(fs_ref, fr_ref, sibling)
    last.wait_recv()
    og_ref[1 - core] = fr_ref[0]
    og_ref[3 - core] = fr_ref[1]
    for c, g in ((0, 2), (1, 0), (2, 1)):
        qkv_grad_ref[c] = close_up(og_ref[g])
    out_grad_ref[...] = close_up(og_ref[3])

    for copy in gather:
        copy.wait_recv()
    send.drain()


def publish(gi, qkv_grad, out_grad, gi_out, qkv_out, out_out, gi_buf, qkv_buf, out_buf, sems):
    moves = []
    for i in range(4):
        rows = pl.ds(i * (TOK // 4), TOK // 4)
        moves.append((gi.at[rows], gi_buf.at[rows], gi_out.at[rows]))
    moves.append((qkv_grad, qkv_buf, qkv_out))
    moves.append((out_grad, out_buf, out_out))
    loads, stores = [], []
    for i, (src, buf, dst) in enumerate(moves):
        loads.append(pltpu.make_async_copy(src, buf, sems.at[0, i]))
        stores.append(pltpu.make_async_copy(buf, dst, sems.at[1, i]))
        loads[-1].start()
    for load, store in zip(loads, stores):
        load.wait()
        store.start()
    for store in stores:
        store.wait()


def per_device(layer_input, grad_output, tile_image, qkv_weight, out_weight):
    vmem = pltpu.VMEM
    shapes = (
        jax.ShapeDtypeStruct((TOK, D), BF16),
        jax.ShapeDtypeStruct((3, 56, 2 * HD), F32),
        jax.ShapeDtypeStruct((56, 2 * HD), F32),
    )
    results = pl.pallas_call(
        kernel,
        out_shape=shapes,
        in_specs=[
            pl.BlockSpec(memory_space=pl.ANY),
            pl.BlockSpec(memory_space=pl.ANY),
            pl.BlockSpec(memory_space=pltpu.VMEM),
            pl.BlockSpec(memory_space=pltpu.VMEM),
            pl.BlockSpec(memory_space=pltpu.SMEM),
        ],
        out_specs=(
            pl.BlockSpec(memory_space=pltpu.VMEM),
            pl.BlockSpec(memory_space=pltpu.VMEM),
            pl.BlockSpec(memory_space=pltpu.VMEM),
        ),
        scratch_shapes=[
            vmem((4, 56, LANES), F32),
            vmem((TOK, D), BF16),
            vmem((TOK, D), BF16),
            vmem((8, 2, 2, 56, PACK), BF16),
            vmem((8, 2, 2, 56, 8 * HD - PACK), BF16),
            vmem((4, 8, 2, CHIP_ROWS, LANES), BF16),
            vmem((8, TOK, LANES), BF16),
            vmem((8, TOK, LANES), BF16),
            vmem((4, TOK, LANES), F32),
            vmem((8, 2 * CHIP_ROWS, TOK), BF16),
            vmem((8, 2 * CHIP_ROWS, TOK), BF16),
            vmem((PAD_TOK, LANES), BF16),
            vmem((PAD_TOK, LANES), BF16),
            vmem((TOK, LANES), BF16),
            vmem((TOK, LANES), BF16),
            vmem((PAD_TOK, LANES), F32),
            vmem((PAD_TOK, LANES), F32),
            vmem((2, 2, 2, HALO, 128), BF16),
            vmem((2, 2, 2, HALO, 128), BF16),
            vmem((4, TOK, LANES), BF16),
            vmem((4, 8, 2, CHIP_ROWS, LANES), BF16),
            vmem((2, 8, 2, CHIP_ROWS, LANES), BF16),
            vmem((2, 4, 2, 2, CHIP_ROWS, LANES), BF16),
            vmem((2, CHIP_ROWS, LANES), BF16),
            vmem((2, CHIP_ROWS, LANES), BF16),
            vmem((2, CHIP_ROWS, LANES), F32),
            vmem((2, 56, LANES), F32),
            vmem((2, 56, LANES), F32),
            vmem((2, 256, CUT), BF16),
            vmem((2, 256, D - CUT), BF16),
            vmem((3, 2, BLOCK, CUT), BF16),
            vmem((4, BLOCK, D - CUT), BF16),
            vmem((BLOCK, CUT), BF16),
            vmem((BLOCK, CUT), BF16),
            vmem((3, BLOCK, D - CUT), BF16),
            vmem((3, BLOCK, D - CUT), BF16),
            vmem((BLOCK, CUT), F32),
            pltpu.SemaphoreType.DMA((N_COPIES,)),
            pltpu.SemaphoreType.DMA((N_COPIES,)),
            pltpu.SemaphoreType.DMA((2,)),
        ],
        compiler_params=pltpu.CompilerParams(
            collective_id=0, has_side_effects=True, vmem_limit_bytes=56 << 20
        ),
        name="attention_backward",
    )(layer_input, grad_output, qkv_weight.transpose(1, 0, 2), out_weight, tile_image)
    grad_input, qkv_grad, out_grad = pl.pallas_call(
        publish,
        out_shape=shapes,
        in_specs=[pl.BlockSpec(memory_space=pl.ANY)] * 3,
        out_specs=[pl.BlockSpec(memory_space=pl.ANY)] * 3,
        scratch_shapes=[
            vmem((TOK, D), BF16),
            vmem((3, 56, 2 * HD), F32),
            vmem((56, 2 * HD), F32),
            pltpu.SemaphoreType.DMA((2, 6)),
        ],
        name="publish",
    )(*results)
    return (grad_input, qkv_grad.transpose(1, 0, 2), out_grad)


def solution(mesh):
    placed = (P("seq", None), P("seq", None), P(), P("seq", None, "tp"), P("seq", "tp"))
    return jax.shard_map(
        per_device,
        mesh=mesh,
        in_specs=placed,
        out_specs=(P("seq", None), P("seq", None, "tp"), P("seq", "tp")),
        check_vma=False,
    )
```

```python
import functools

import jax
import jax.numpy as jnp
from jax import lax
from jax.experimental import pallas as pl
from jax.experimental.pallas import tpu as pltpu
from jax.sharding import PartitionSpec as P

HD = 112
TILE = 128
LANES = 256
TOK = 512
D = 1792
CHIP_ROWS = 112
HALO = 256
PAD_TOK = TOK + 2 * HALO
WINDOW = 768
BLOCK = 64
PART = 32
CUT = 768
PACK = 512
FACTOR = float(HD) ** (-0.5)
F32 = jnp.float32
BF16 = jnp.bfloat16
MESH = pl.DeviceIdType.MESH
N_COPIES = 176

NT = (((1,), (1,)), ((), ()))


def dot(a, b):
    return jnp.dot(a, b, preferred_element_type=F32)


def dot_nt(a, b):
    return lax.dot_general(a, b, NT, preferred_element_type=F32)


class Sender:
    def __init__(self, send_sems, recv_sems):
        self.send_sems, self.recv_sems = send_sems, recv_sems
        self.copies = []

    def __call__(self, src, dst, device):
        index = len(self.copies)
        copy = pltpu.make_async_remote_copy(
            src_ref=src,
            dst_ref=dst,
            send_sem=self.send_sems.at[index],
            recv_sem=self.recv_sems.at[index],
            device_id=device,
            device_id_type=MESH,
        )
        copy.start()
        self.copies.append(copy)
        return copy

    def drain(self):
        for copy in self.copies:
            copy.wait_send()


def kernel(
    x_hbm,
    go_hbm,
    qkv_ref,
    out_ref,
    ids_ref,
    gi_ref,
    qkv_grad_ref,
    out_grad_ref,
    og_ref,
    x_ref,
    go_ref,
    wp_ref,
    wq_ref,
    w_ref,
    xb_ref,
    gob_ref,
    acc_ref,
    xt_ref,
    got_ref,
    kp_ref,
    vp_ref,
    q_ref,
    u_ref,
    dk_ref,
    dv_ref,
    hs_ref,
    hr_ref,
    gp_ref,
    part_ref,
    ps_ref,
    rb_ref,
    ys_ref,
    yr_ref,
    fin_ref,
    fs_ref,
    fr_ref,
    ga_ref,
    gb_ref,
    ra1_ref,
    rb1_ref,
    sa2_ref,
    ra2_ref,
    sb2_ref,
    rb2_ref,
    suma_ref,
    send_sems,
    recv_sems,
    load_sems,
):
    seq = lax.axis_index("seq")
    tp = lax.axis_index("tp")
    core = lax.rem(seq, 2)
    z = lax.rem(seq // 2, 8)
    yl = seq // 16
    other = 1 - yl

    def at_z(offset):
        return lax.rem(z + 8 + offset, 8)

    def device(yl_, z_, core_):
        return (yl_ * 16 + z_ * 2 + core_, tp)

    sibling = device(yl, z, 1 - core)
    z_next = {1: device(yl, at_z(1), core), -1: device(yl, at_z(-1), core)}
    y_pair = device(other, z, core)
    following = (lax.rem(seq + 1, 32), tp)
    previous = (lax.rem(seq + 31, 32), tp)

    def tp_peer(d):
        return jnp.bitwise_xor(tp, d)

    load_x = pltpu.make_async_copy(x_hbm, x_ref, load_sems.at[0])
    load_go = pltpu.make_async_copy(go_hbm, go_ref, load_sems.at[1])
    load_x.start()
    load_go.start()

    barrier = pltpu.get_barrier_semaphore()
    peers = [sibling, z_next[1], z_next[-1], y_pair, following, previous]
    peers += [(seq, tp_peer(d)) for d in range(1, 8)]

    def close_up(wide):
        return jnp.concatenate([wide[:, :HD], wide[:, 128 : 128 + HD]], axis=1)

    own = [qkv_ref[1], qkv_ref[2], qkv_ref[0], out_ref[...]]
    own = jnp.concatenate([rows.astype(F32) for rows in own], axis=1).astype(BF16)
    wp_ref[z, yl, core] = own[:, :PACK]
    wq_ref[z, yl, core] = own[:, PACK:]
    for peer in peers:
        pl.semaphore_signal(barrier, inc=1, device_id=peer, device_id_type=MESH)
    pl.semaphore_wait(barrier, len(peers))

    send = Sender(send_sems, recv_sems)
    groups = (core, 2 + core)

    first_own = wp_ref.at[z, yl, core]
    second_own = wq_ref.at[z, yl, core]
    ring, cross, relay, beside = {}, {}, {}, {t: [] for t in range(6)}
    for sign in (1, -1):
        ring[sign, 1, 0] = send(first_own, first_own, z_next[sign])
    cross = send(first_own, first_own, y_pair)
    for sign in (1, -1):
        ring[sign, 1, 2] = send(second_own, second_own, z_next[sign])
    relay[0] = [send(second_own, second_own, y_pair)]
    beside[0].append(send(first_own, first_own, sibling))
    beside[0].append(send(second_own, second_own, sibling))
    load_x.wait()

    def split_columns(dst, rows, wide):
        for k in range(8):
            low = wide[:, CHIP_ROWS * k : CHIP_ROWS * (k + 1)]
            high = wide[:, 896 + CHIP_ROWS * k : 896 + CHIP_ROWS * (k + 1)]
            dst[k, rows, 0 : 2 * CHIP_ROWS] = jnp.concatenate([low, high], axis=1).astype(BF16)

    def split_rows(start):
        rows = slice(start, start + 32)
        split_columns(gob_ref, rows, go_ref[rows].astype(F32))

    def norm_rows(start):
        rows = slice(start, start + 32)
        wide = x_ref[rows].astype(F32)
        mean = jnp.mean(wide, axis=-1, keepdims=True)
        center = wide - mean
        inv_std = lax.rsqrt(jnp.mean(center * center, axis=-1, keepdims=True) + 1e-06)
        split_columns(xb_ref, rows, center * inv_std)

    def transpose_block(src, dst, k):
        dst[k] = src[k].T[: 2 * CHIP_ROWS]

    work = [functools.partial(norm_rows, 32 * i) for i in range(16)]
    work += [functools.partial(split_rows, 32 * i) for i in range(16)]
    later = []
    for source, target in ((gob_ref, got_ref), (xb_ref, xt_ref)):
        for k in range(8):
            later.append(functools.partial(transpose_block, source, target, k))
    work.reverse()
    later.reverse()

    def do_some(count):
        for _ in range(count):
            if work or later:
                (work or later).pop()()

    def unpack(k):
        first = wp_ref[k].astype(F32).reshape(2 * CHIP_ROWS, PACK)
        second = wq_ref[k].astype(F32).reshape(2 * CHIP_ROWS, 8 * HD - PACK)
        packed = jnp.concatenate([first, second], axis=1)
        gap = jnp.zeros((2 * CHIP_ROWS, 128 - HD), F32)
        for g in range(4):
            low = packed[:, 2 * HD * g : 2 * HD * g + HD]
            high = packed[:, 2 * HD * g + HD : 2 * HD * (g + 1)]
            wide = jnp.concatenate([low, gap, high, gap], axis=1).astype(BF16)
            w_ref[g, k] = wide.reshape(2, CHIP_ROWS, LANES)

    def project(blocks, first=False):
        for k in blocks:
            unpack(k)
        for g, src in ((0, xb_ref), (1, xb_ref), (2, xb_ref), (3, gob_ref)):
            total = 0.0 if first else acc_ref[g]
            for k in blocks:
                block = w_ref[g, k].reshape(2 * CHIP_ROWS, LANES)
                total += dot(src[k, :, 0 : 2 * CHIP_ROWS], block)
            acc_ref[g] = total

    block = wp_ref.at[z, other, core]
    cross.wait_recv()
    for sign in (1, -1):
        ring[sign, 1, 1] = send(block, block, z_next[sign])
    beside[0].append(send(block, block, sibling))
    load_go.wait()
    do_some(4)

    def piece(kind, k):
        ref = wq_ref if kind == 2 else wp_ref
        return ref.at[k, other if kind == 1 else yl, core]

    turn = 1 - 2 * core
    turned = device(yl, at_z(turn), core)
    for t in (1, 2, 3, 4):
        relay[t] = []
        for kind in (0, 2, 1):
            for sign in (1, -1):
                if (sign, t, kind) not in ring:
                    continue
                ring[sign, t, kind].wait_recv()
                block = piece(kind, at_z(-sign * t))
                if t < 3 or (t == 3 and kind < 2 and sign == (1, -1)[kind]):
                    ring[sign, t + 1, kind] = send(block, block, z_next[sign])
                if t == 3 and kind == 2 and sign == -1:
                    farthest = piece(kind, at_z(-turn * t))
                    ring[1, 4, 2] = send(farthest, farthest, turned)
                if kind == 2:
                    relay[t].append(send(block, block, y_pair))
                beside[t].append(send(block, block, sibling))
            do_some(3)
        spots = [z] if t == 1 else [at_z(1 - t), at_z(t - 1)]
        for copy, k in zip(relay[t - 1], spots):
            copy.wait_recv()
            block = wq_ref.at[k, other, core]
            beside[t - 1].append(send(block, block, sibling))
        if t == 2:
            do_some(len(work))
            for copy in beside[0]:
                copy.wait_recv()
            project([z], True)
        if t > 2:
            for copy in beside[t - 2]:
                copy.wait_recv()
            project([at_z(2 - t), at_z(t - 2)])
    relay[4][0].wait_recv()
    block = wq_ref.at[at_z(4), other, core]
    beside[4].append(send(block, block, sibling))
    for copy in beside[3]:
        copy.wait_recv()
    project([at_z(-3), at_z(3)])
    do_some(len(later))
    for copy in beside[4]:
        copy.wait_recv()
    unpack(at_z(4))

    def weights(g):
        return jnp.concatenate([w_ref[g, :, y].reshape(896, LANES) for y in (0, 1)], axis=0)

    halo = []
    def finished(g):
        src = gob_ref if g == 3 else xb_ref
        k = at_z(4)
        block = w_ref[g, k].reshape(2 * CHIP_ROWS, LANES)
        return (acc_ref[g] + dot(src[k, :, 0 : 2 * CHIP_ROWS], block)).astype(BF16)

    for g, ref in ((0, kp_ref), (1, vp_ref)):
        ref[HALO : HALO + TOK] = finished(g)
        halo.append(send(ref.at[pl.ds(HALO, HALO)], ref.at[pl.ds(HALO + TOK, HALO)], previous))
        halo.append(send(ref.at[pl.ds(TOK, HALO)], ref.at[pl.ds(0, HALO)], following))
    q_ref[...] = finished(2)
    u_ref[...] = finished(3)

    def tile_id(tile):
        inside = jnp.logical_and(tile >= 0, tile < 128)
        value = ids_ref[jnp.clip(tile, 0, 127)]
        return jnp.where(inside, value, -1)

    key_ids = [tile_id(4 * seq - 2 + k) for k in range(8)]
    lane = lax.broadcasted_iota(jnp.int32, (1, 256), 1)
    for copy in halo:
        copy.wait_recv()

    back = []
    for h in (0, 1):
        lanes = slice(128 * h, 128 * h + 128)
        key_t = kp_ref[:, lanes].T
        value_t = vp_ref[:, lanes].T
        for half in (0, 1):
            keys = slice(256 * half, 256 * half + WINDOW)
            rows = slice(256 * half, 256 * half + 256)
            query = q_ref[rows, lanes]
            up = u_ref[rows, lanes]
            key = kp_ref[keys, lanes]
            value = vp_ref[keys, lanes]
            scores = dot_nt(key, query) * FACTOR
            query_id = jnp.where(lane < 128, key_ids[2 + 2 * half], key_ids[3 + 2 * half])
            parts = []
            for k in range(6):
                allowed = query_id == key_ids[2 * half + k]
                parts.append(jnp.where(allowed, jnp.exp(scores[128 * k : 128 * k + 128]), 0.0))
            exponent = jnp.concatenate(parts, axis=0)
            prob = exponent * (1.0 / jnp.sum(exponent, axis=0, keepdims=True))
            prob_low = prob.astype(BF16)
            attended = dot(value_t[:, keys], prob_low)
            delta = jnp.sum(up.astype(F32).T * attended, axis=0, keepdims=True)
            dprob = dot_nt(value, up)
            dscore = (prob * (dprob - delta) * FACTOR).astype(BF16)
            dquery = dot(key_t[:, keys], dscore)
            gp_ref[2, rows, lanes] = dquery.T.astype(BF16)
            gp_ref[3, rows, lanes] = attended.T.astype(BF16)
            dkey = dot(dscore, query)
            dvalue = dot(prob_low, up)
            for ref, grad in ((dk_ref, dkey), (dv_ref, dvalue)):
                if half == 0:
                    ref[0:WINDOW, lanes] = grad
                else:
                    ref[256:WINDOW, lanes] += grad[: WINDOW - 256]
                    ref[WINDOW:PAD_TOK, lanes] = grad[WINDOW - 256 :]
        for j, ref in ((0, dk_ref), (1, dv_ref)):
            hs_ref[h, j, 0] = ref[0:HALO, lanes].astype(BF16)
            hs_ref[h, j, 1] = ref[HALO + TOK : PAD_TOK, lanes].astype(BF16)
            back.append(send(hs_ref.at[h, j, 0], hr_ref.at[h, j, 0], previous))
            back.append(send(hs_ref.at[h, j, 1], hr_ref.at[h, j, 1], following))

    def weight_grad(g):
        src = got_ref if g == 3 else xt_ref

        def body(i, _):
            blocks = pl.ds(i * 4, 4)
            grad = dot(src[blocks].reshape(896, TOK), gp_ref[g]).astype(BF16)
            part_ref[g, blocks] = grad.reshape(4, 2, CHIP_ROWS, LANES)
            return 0

        lax.fori_loop(0, 2, body, 0)

    weight_grad(2)
    weight_grad(3)
    swap = {1: send(part_ref.at[3 - core], ps_ref.at[1], sibling)}
    for copy in back:
        copy.wait_recv()
    for h in (0, 1):
        lanes = slice(128 * h, 128 * h + 128)
        for j, ref in ((0, dk_ref), (1, dv_ref)):
            low = ref[HALO : 2 * HALO, lanes] + hr_ref[h, j, 1].astype(F32)
            high = ref[2 * HALO : 3 * HALO, lanes] + hr_ref[h, j, 0].astype(F32)
            gp_ref[j, 0:HALO, lanes] = low.astype(BF16)
            gp_ref[j, HALO:TOK, lanes] = high.astype(BF16)

    yh, xx = tp // 4, lax.rem(tp, 4)
    y_other = (seq, (1 - yh) * 4 + xx)

    def x_at(e):
        return lax.rem(xx + e, 4)

    def x_peer(e):
        return (seq, yh * 4 + x_at(e))

    def block_at(e, p):
        return pl.ds(pl.multiple_of(x_at(e) * BLOCK + p * PART, PART), PART)

    def part_of(p):
        return pl.ds(p * PART, PART)

    def partial_norm(half, start, stop):
        rows = pl.ds(pl.multiple_of(half * 256, 256), 256)
        total = dot_nt(gp_ref[0, rows], weights(0)[start:stop])
        total += dot_nt(gp_ref[1, rows], weights(1)[start:stop])
        total += dot_nt(gp_ref[2, rows], weights(2)[start:stop])
        return total.astype(BF16)

    gb_ref[1 - yh] = partial_norm(1 - yh, CUT, D)
    y_first = {}
    for p in (0, 1):
        for e in (1, 3, 2, 0):
            src, dst = gb_ref.at[1 - yh, block_at(e, p)], rb1_ref.at[e, part_of(p)]
            y_first[e, p] = send(src, dst, y_other)
    for half in (0, 1):
        ga_ref[half] = partial_norm(half, 0, CUT)
    x_first = {}
    for p in (0, 1):
        for e in (1, 3, 2):
            src, dst = ga_ref.at[:, block_at(e, p)], ra1_ref.at[e - 1, :, part_of(p)]
            x_first[e, p] = send(src, dst, x_peer(e))
    gb_ref[yh] = partial_norm(yh, CUT, D)


    chain = {}

    def ring_step(t, i):
        g = groups[i]
        if t == 4:
            swap[i].wait_recv()
        for side in (0, 1):
            y = (yl, other)[side]
            for sign in (1, -1):
                if t == 4 and side != (0 if sign == 1 else 1):
                    continue
                zz = at_z(sign * t)
                total = part_ref[g, zz, y].astype(F32) + ps_ref[i, zz, y].astype(F32)
                if (sign, t + 1, i, side) in chain:
                    chain[sign, t + 1, i, side].wait_recv()
                    total += rb_ref[(sign + 1) // 2, t, i, side].astype(F32)
                part_ref[g, zz, y] = total.astype(BF16)
                chain[sign, t, i, side] = send(
                    part_ref.at[g, zz, y],
                    rb_ref.at[(sign + 1) // 2, t - 1, i, side],
                    z_next[sign],
                )

    y_copies = {}

    def y_stage(i):
        g = groups[i]
        for side in (1, 0):
            y = (yl, other)[side]
            total = part_ref[g, z, y].astype(F32) + ps_ref[i, z, y].astype(F32)
            for sign in (1, -1):
                chain[sign, 1, i, side].wait_recv()
                total += rb_ref[(sign + 1) // 2, 0, i, side].astype(F32)
            if side == 1:
                ys_ref[i] = total.astype(BF16)
                y_copies[i] = send(ys_ref.at[i], yr_ref.at[i], y_pair)
            else:
                fin_ref[i] = total

    ring_step(4, 1)
    weight_grad(0)
    weight_grad(1)
    swap[0] = send(part_ref.at[1 - core], ps_ref.at[0], sibling)

    x_second, y_second = {}, {}

    def second_step(p):
        part = part_of(p)
        for e in (1, 3, 2):
            y_first[e, p].wait_recv()
            total = gb_ref[yh, block_at(e, p)].astype(F32) + rb1_ref[e, part].astype(F32)
            sb2_ref[e - 1, part] = total.astype(BF16)
            src, dst = sb2_ref.at[e - 1, part], rb2_ref.at[e - 1, part]
            x_second[e, p] = send(src, dst, x_peer(e))
        for e in (1, 3, 2):
            x_first[e, p].wait_recv()

        def sum_x(half):
            total = ga_ref[half, block_at(0, p)].astype(F32)
            for e in (1, 2, 3):
                total += ra1_ref[e - 1, half, part].astype(F32)
            return total

        sa2_ref[part] = sum_x(1 - yh).astype(BF16)
        y_second[p] = send(sa2_ref.at[part], ra2_ref.at[part], y_other)
        suma_ref[part] = sum_x(yh)

    def norm_back(i, _):
        rows = pl.ds(pl.multiple_of(tp * BLOCK + i * 16, 16), 16)
        part = pl.ds(pl.multiple_of(i * 16, 16), 16)
        own_part = pl.ds(pl.multiple_of(xx * BLOCK + i * 16, 16), 16)
        first = suma_ref[part] + ra2_ref[part].astype(F32)
        second = gb_ref[yh, own_part].astype(F32) + rb1_ref[0, part].astype(F32)
        for e in range(3):
            second += rb2_ref[e, part].astype(F32)
        total = jnp.concatenate([first, second], axis=1)
        wide = x_ref[rows].astype(F32)
        center = wide - jnp.mean(wide, axis=-1, keepdims=True)
        inv_std = lax.rsqrt(jnp.mean(center * center, axis=-1, keepdims=True) + 1e-06)
        normed = center * inv_std
        grad = inv_std * (
            total
            - jnp.mean(total, axis=-1, keepdims=True)
            - normed * jnp.mean(total * normed, axis=-1, keepdims=True)
        )
        gi_ref[rows] = grad.astype(BF16)
        return 0

    first, second = pl.ds(0, CUT), pl.ds(CUT, D - CUT)
    y_gather, x_gather, gather = {}, {}, []

    def share(y, x, p, columns, to):
        rows = pl.ds(pl.multiple_of((y * 4 + x) * BLOCK + p * PART, PART), PART)
        piece = gi_ref.at[rows, columns]
        return send(piece, piece, to)

    def finish(p):
        y_first[0, p].wait_recv()
        for e in (1, 3, 2):
            x_second[e, p].wait_recv()
        y_second[p].wait_recv()
        lax.fori_loop(2 * p, 2 * p + 2, norm_back, 0)
        y_gather[p] = share(yh, xx, p, first, y_other)
        for e in (1, 3, 2):
            x_gather[e, p] = share(yh, xx, p, second, x_peer(e))
        gather.append(share(yh, xx, p, second, y_other))
        for e in (1, 3, 2):
            gather.append(share(yh, xx, p, first, x_peer(e)))

    def forward(p):
        y_gather[p].wait_recv()
        for e in (1, 3, 2):
            gather.append(share(1 - yh, xx, p, first, x_peer(e)))
        for e in (1, 3, 2):
            x_gather[e, p].wait_recv()
            gather.append(share(yh, x_at(4 - e), p, second, y_other))

    second_step(0)
    ring_step(3, 1)
    ring_step(4, 0)
    second_step(1)
    ring_step(2, 1)
    ring_step(3, 0)
    finish(0)
    finish(1)
    ring_step(1, 1)
    ring_step(2, 0)
    forward(0)
    forward(1)
    ring_step(1, 0)
    y_stage(1)
    y_stage(0)
    own_rows = pl.ds(pl.multiple_of(56 * core, 8), 56)
    sib_rows = pl.ds(pl.multiple_of(56 * (1 - core), 8), 56)
    for i in (0, 1):
        y_copies[i].wait_recv()
        fin_ref[i] += yr_ref[i].astype(F32)
        fs_ref[i] = fin_ref[i, sib_rows]
        og_ref[groups[i]] = fin_ref[i, own_rows]
    last = send(fs_ref, fr_ref, sibling)
    last.wait_recv()
    og_ref[1 - core] = fr_ref[0]
    og_ref[3 - core] = fr_ref[1]
    for c, g in ((0, 2), (1, 0), (2, 1)):
        qkv_grad_ref[c] = close_up(og_ref[g])
    out_grad_ref[...] = close_up(og_ref[3])

    for copy in gather:
        copy.wait_recv()
    send.drain()


def publish(gi, qkv_grad, out_grad, gi_out, qkv_out, out_out, gi_buf, qkv_buf, out_buf, sems):
    moves = []
    for i in range(4):
        rows = pl.ds(i * (TOK // 4), TOK // 4)
        moves.append((gi.at[rows], gi_buf.at[rows], gi_out.at[rows]))
    moves.append((qkv_grad, qkv_buf, qkv_out))
    moves.append((out_grad, out_buf, out_out))
    loads, stores = [], []
    for i, (src, buf, dst) in enumerate(moves):
        loads.append(pltpu.make_async_copy(src, buf, sems.at[0, i]))
        stores.append(pltpu.make_async_copy(buf, dst, sems.at[1, i]))
        loads[-1].start()
    for load, store in zip(loads, stores):
        load.wait()
        store.start()
    for store in stores:
        store.wait()


def per_device(layer_input, grad_output, tile_image, qkv_weight, out_weight):
    vmem = pltpu.VMEM
    shapes = (
        jax.ShapeDtypeStruct((TOK, D), BF16),
        jax.ShapeDtypeStruct((3, 56, 2 * HD), F32),
        jax.ShapeDtypeStruct((56, 2 * HD), F32),
    )
    results = pl.pallas_call(
        kernel,
        out_shape=shapes,
        in_specs=[
            pl.BlockSpec(memory_space=pl.ANY),
            pl.BlockSpec(memory_space=pl.ANY),
            pl.BlockSpec(memory_space=pltpu.VMEM),
            pl.BlockSpec(memory_space=pltpu.VMEM),
            pl.BlockSpec(memory_space=pltpu.SMEM),
        ],
        out_specs=(
            pl.BlockSpec(memory_space=pltpu.VMEM),
            pl.BlockSpec(memory_space=pltpu.VMEM),
            pl.BlockSpec(memory_space=pltpu.VMEM),
        ),
        scratch_shapes=[
            vmem((4, 56, LANES), F32),
            vmem((TOK, D), BF16),
            vmem((TOK, D), BF16),
            vmem((8, 2, 2, 56, PACK), BF16),
            vmem((8, 2, 2, 56, 8 * HD - PACK), BF16),
            vmem((4, 8, 2, CHIP_ROWS, LANES), BF16),
            vmem((8, TOK, LANES), BF16),
            vmem((8, TOK, LANES), BF16),
            vmem((4, TOK, LANES), F32),
            vmem((8, 2 * CHIP_ROWS, TOK), BF16),
            vmem((8, 2 * CHIP_ROWS, TOK), BF16),
            vmem((PAD_TOK, LANES), BF16),
            vmem((PAD_TOK, LANES), BF16),
            vmem((TOK, LANES), BF16),
            vmem((TOK, LANES), BF16),
            vmem((PAD_TOK, LANES), F32),
            vmem((PAD_TOK, LANES), F32),
            vmem((2, 2, 2, HALO, 128), BF16),
            vmem((2, 2, 2, HALO, 128), BF16),
            vmem((4, TOK, LANES), BF16),
            vmem((4, 8, 2, CHIP_ROWS, LANES), BF16),
            vmem((2, 8, 2, CHIP_ROWS, LANES), BF16),
            vmem((2, 4, 2, 2, CHIP_ROWS, LANES), BF16),
            vmem((2, CHIP_ROWS, LANES), BF16),
            vmem((2, CHIP_ROWS, LANES), BF16),
            vmem((2, CHIP_ROWS, LANES), F32),
            vmem((2, 56, LANES), F32),
            vmem((2, 56, LANES), F32),
            vmem((2, 256, CUT), BF16),
            vmem((2, 256, D - CUT), BF16),
            vmem((3, 2, BLOCK, CUT), BF16),
            vmem((4, BLOCK, D - CUT), BF16),
            vmem((BLOCK, CUT), BF16),
            vmem((BLOCK, CUT), BF16),
            vmem((3, BLOCK, D - CUT), BF16),
            vmem((3, BLOCK, D - CUT), BF16),
            vmem((BLOCK, CUT), F32),
            pltpu.SemaphoreType.DMA((N_COPIES,)),
            pltpu.SemaphoreType.DMA((N_COPIES,)),
            pltpu.SemaphoreType.DMA((2,)),
        ],
        compiler_params=pltpu.CompilerParams(
            collective_id=0, has_side_effects=True, vmem_limit_bytes=56 << 20
        ),
        name="attention_backward",
    )(layer_input, grad_output, qkv_weight.transpose(1, 0, 2), out_weight, tile_image)
    grad_input, qkv_grad, out_grad = pl.pallas_call(
        publish,
        out_shape=shapes,
        in_specs=[pl.BlockSpec(memory_space=pl.ANY)] * 3,
        out_specs=[pl.BlockSpec(memory_space=pl.ANY)] * 3,
        scratch_shapes=[
            vmem((TOK, D), BF16),
            vmem((3, 56, 2 * HD), F32),
            vmem((56, 2 * HD), F32),
            pltpu.SemaphoreType.DMA((2, 6)),
        ],
        name="publish",
    )(*results)
    return (grad_input, qkv_grad.transpose(1, 0, 2), out_grad)


def solution(mesh):
    placed = (P("seq", None), P("seq", None), P(), P("seq", None, "tp"), P("seq", "tp"))
    return jax.shard_map(
        per_device,
        mesh=mesh,
        in_specs=placed,
        out_specs=(P("seq", None), P("seq", None, "tp"), P("seq", "tp")),
        check_vma=False,
    )
```

```python
import functools

import jax
import jax.numpy as jnp
from jax import lax
from jax.experimental import pallas as pl
from jax.experimental.pallas import tpu as pltpu
from jax.sharding import PartitionSpec as P

HD = 112
TILE = 128
LANES = 256
TOK = 512
D = 1792
CHIP_ROWS = 112
HALO = 256
PAD_TOK = TOK + 2 * HALO
WINDOW = 768
BLOCK = 64
PART = 32
CUT = 768
PACK = 512
FACTOR = float(HD) ** (-0.5)
F32 = jnp.float32
BF16 = jnp.bfloat16
MESH = pl.DeviceIdType.MESH
N_COPIES = 176

NT = (((1,), (1,)), ((), ()))


def dot(a, b):
    return jnp.dot(a, b, preferred_element_type=F32)


def dot_nt(a, b):
    return lax.dot_general(a, b, NT, preferred_element_type=F32)


class Sender:
    def __init__(self, send_sems, recv_sems):
        self.send_sems, self.recv_sems = send_sems, recv_sems
        self.copies = []

    def __call__(self, src, dst, device):
        index = len(self.copies)
        copy = pltpu.make_async_remote_copy(
            src_ref=src,
            dst_ref=dst,
            send_sem=self.send_sems.at[index],
            recv_sem=self.recv_sems.at[index],
            device_id=device,
            device_id_type=MESH,
        )
        copy.start()
        self.copies.append(copy)
        return copy

    def drain(self):
        for copy in self.copies:
            copy.wait_send()


def kernel(
    x_hbm,
    go_hbm,
    qkv_ref,
    out_ref,
    ids_ref,
    gi_ref,
    qkv_grad_ref,
    out_grad_ref,
    og_ref,
    x_ref,
    go_ref,
    wp_ref,
    wq_ref,
    w_ref,
    xb_ref,
    gob_ref,
    acc_ref,
    xt_ref,
    got_ref,
    kp_ref,
    vp_ref,
    q_ref,
    u_ref,
    dk_ref,
    dv_ref,
    hs_ref,
    hr_ref,
    gp_ref,
    part_ref,
    ps_ref,
    rb_ref,
    ys_ref,
    yr_ref,
    fin_ref,
    fs_ref,
    fr_ref,
    ga_ref,
    gb_ref,
    ra1_ref,
    rb1_ref,
    sa2_ref,
    ra2_ref,
    sb2_ref,
    rb2_ref,
    suma_ref,
    send_sems,
    recv_sems,
    load_sems,
):
    seq = lax.axis_index("seq")
    tp = lax.axis_index("tp")
    core = lax.rem(seq, 2)
    z = lax.rem(seq // 2, 8)
    yl = seq // 16
    other = 1 - yl

    def at_z(offset):
        return lax.rem(z + 8 + offset, 8)

    def device(yl_, z_, core_):
        return (yl_ * 16 + z_ * 2 + core_, tp)

    sibling = device(yl, z, 1 - core)
    z_next = {1: device(yl, at_z(1), core), -1: device(yl, at_z(-1), core)}
    y_pair = device(other, z, core)
    following = (lax.rem(seq + 1, 32), tp)
    previous = (lax.rem(seq + 31, 32), tp)

    def tp_peer(d):
        return jnp.bitwise_xor(tp, d)

    load_x = pltpu.make_async_copy(x_hbm, x_ref, load_sems.at[0])
    load_go = pltpu.make_async_copy(go_hbm, go_ref, load_sems.at[1])
    load_x.start()
    load_go.start()

    barrier = pltpu.get_barrier_semaphore()
    peers = [sibling, z_next[1], z_next[-1], y_pair, following, previous]
    peers += [(seq, tp_peer(d)) for d in range(1, 8)]

    def close_up(wide):
        return jnp.concatenate([wide[:, :HD], wide[:, 128 : 128 + HD]], axis=1)

    own = [qkv_ref[1], qkv_ref[2], qkv_ref[0], out_ref[...]]
    own = jnp.concatenate([rows.astype(F32) for rows in own], axis=1).astype(BF16)
    wp_ref[z, yl, core] = own[:, :PACK]
    wq_ref[z, yl, core] = own[:, PACK:]
    for peer in peers:
        pl.semaphore_signal(barrier, inc=1, device_id=peer, device_id_type=MESH)
    pl.semaphore_wait(barrier, len(peers))

    send = Sender(send_sems, recv_sems)
    groups = (core, 2 + core)

    first_own = wp_ref.at[z, yl, core]
    second_own = wq_ref.at[z, yl, core]
    ring, cross, relay, beside = {}, {}, {}, {t: [] for t in range(6)}
    for sign in (1, -1):
        ring[sign, 1, 0] = send(first_own, first_own, z_next[sign])
    cross = send(first_own, first_own, y_pair)
    for sign in (1, -1):
        ring[sign, 1, 2] = send(second_own, second_own, z_next[sign])
    relay[0] = [send(second_own, second_own, y_pair)]
    beside[0].append(send(first_own, first_own, sibling))
    beside[0].append(send(second_own, second_own, sibling))
    load_x.wait()

    def split_columns(dst, rows, wide):
        for k in range(8):
            low = wide[:, CHIP_ROWS * k : CHIP_ROWS * (k + 1)]
            high = wide[:, 896 + CHIP_ROWS * k : 896 + CHIP_ROWS * (k + 1)]
            dst[k, rows, 0 : 2 * CHIP_ROWS] = jnp.concatenate([low, high], axis=1).astype(BF16)

    def split_rows(start):
        rows = slice(start, start + 32)
        split_columns(gob_ref, rows, go_ref[rows].astype(F32))

    def norm_rows(start):
        rows = slice(start, start + 32)
        wide = x_ref[rows].astype(F32)
        mean = jnp.mean(wide, axis=-1, keepdims=True)
        center = wide - mean
        inv_std = lax.rsqrt(jnp.mean(center * center, axis=-1, keepdims=True) + 1e-06)
        split_columns(xb_ref, rows, center * inv_std)

    def transpose_block(src, dst, k):
        dst[k] = src[k].T[: 2 * CHIP_ROWS]

    work = [functools.partial(norm_rows, 32 * i) for i in range(16)]
    work += [functools.partial(split_rows, 32 * i) for i in range(16)]
    later = []
    for source, target in ((gob_ref, got_ref), (xb_ref, xt_ref)):
        for k in range(8):
            later.append(functools.partial(transpose_block, source, target, k))
    work.reverse()
    later.reverse()

    def do_some(count):
        for _ in range(count):
            if work or later:
                (work or later).pop()()

    def unpack(k):
        first = wp_ref[k].astype(F32).reshape(2 * CHIP_ROWS, PACK)
        second = wq_ref[k].astype(F32).reshape(2 * CHIP_ROWS, 8 * HD - PACK)
        packed = jnp.concatenate([first, second], axis=1)
        gap = jnp.zeros((2 * CHIP_ROWS, 128 - HD), F32)
        for g in range(4):
            low = packed[:, 2 * HD * g : 2 * HD * g + HD]
            high = packed[:, 2 * HD * g + HD : 2 * HD * (g + 1)]
            wide = jnp.concatenate([low, gap, high, gap], axis=1).astype(BF16)
            w_ref[g, k] = wide.reshape(2, CHIP_ROWS, LANES)

    def project(blocks, first=False):
        for k in blocks:
            unpack(k)
        for g, src in ((0, xb_ref), (1, xb_ref), (2, xb_ref), (3, gob_ref)):
            total = 0.0 if first else acc_ref[g]
            for k in blocks:
                block = w_ref[g, k].reshape(2 * CHIP_ROWS, LANES)
                total += dot(src[k, :, 0 : 2 * CHIP_ROWS], block)
            acc_ref[g] = total

    block = wp_ref.at[z, other, core]
    cross.wait_recv()
    for sign in (1, -1):
        ring[sign, 1, 1] = send(block, block, z_next[sign])
    beside[0].append(send(block, block, sibling))
    load_go.wait()
    do_some(4)

    def piece(kind, k):
        ref = wq_ref if kind == 2 else wp_ref
        return ref.at[k, other if kind == 1 else yl, core]

    turn = 1 - 2 * core
    turned = device(yl, at_z(turn), core)
    for t in (1, 2, 3, 4):
        relay[t] = []
        for kind in (0, 2, 1):
            for sign in (1, -1):
                if (sign, t, kind) not in ring:
                    continue
                ring[sign, t, kind].wait_recv()
                block = piece(kind, at_z(-sign * t))
                if t < 3 or (t == 3 and kind < 2 and sign == (1, -1)[kind]):
                    ring[sign, t + 1, kind] = send(block, block, z_next[sign])
                if t == 3 and kind == 2 and sign == -1:
                    farthest = piece(kind, at_z(-turn * t))
                    ring[1, 4, 2] = send(farthest, farthest, turned)
                if kind == 2:
                    relay[t].append(send(block, block, y_pair))
                beside[t].append(send(block, block, sibling))
            do_some(3)
        spots = [z] if t == 1 else [at_z(1 - t), at_z(t - 1)]
        for copy, k in zip(relay[t - 1], spots):
            copy.wait_recv()
            block = wq_ref.at[k, other, core]
            beside[t - 1].append(send(block, block, sibling))
        if t == 2:
            do_some(len(work))
            for copy in beside[0]:
                copy.wait_recv()
            project([z], True)
        if t > 2:
            for copy in beside[t - 2]:
                copy.wait_recv()
            project([at_z(2 - t), at_z(t - 2)])
    relay[4][0].wait_recv()
    block = wq_ref.at[at_z(4), other, core]
    beside[4].append(send(block, block, sibling))
    for copy in beside[3]:
        copy.wait_recv()
    project([at_z(-3), at_z(3)])
    do_some(len(later))
    for copy in beside[4]:
        copy.wait_recv()
    unpack(at_z(4))

    def weights(g):
        return jnp.concatenate([w_ref[g, :, y].reshape(896, LANES) for y in (0, 1)], axis=0)

    halo = []
    def finished(g):
        src = gob_ref if g == 3 else xb_ref
        k = at_z(4)
        block = w_ref[g, k].reshape(2 * CHIP_ROWS, LANES)
        return (acc_ref[g] + dot(src[k, :, 0 : 2 * CHIP_ROWS], block)).astype(BF16)

    for g, ref in ((0, kp_ref), (1, vp_ref)):
        ref[HALO : HALO + TOK] = finished(g)
        halo.append(send(ref.at[pl.ds(HALO, HALO)], ref.at[pl.ds(HALO + TOK, HALO)], previous))
        halo.append(send(ref.at[pl.ds(TOK, HALO)], ref.at[pl.ds(0, HALO)], following))
    q_ref[...] = finished(2)
    u_ref[...] = finished(3)

    def tile_id(tile):
        inside = jnp.logical_and(tile >= 0, tile < 128)
        value = ids_ref[jnp.clip(tile, 0, 127)]
        return jnp.where(inside, value, -1)

    key_ids = [tile_id(4 * seq - 2 + k) for k in range(8)]
    lane = lax.broadcasted_iota(jnp.int32, (1, 256), 1)
    for copy in halo:
        copy.wait_recv()

    back = []
    for h in (0, 1):
        lanes = slice(128 * h, 128 * h + 128)
        key_t = kp_ref[:, lanes].T
        value_t = vp_ref[:, lanes].T
        for half in (0, 1):
            keys = slice(256 * half, 256 * half + WINDOW)
            rows = slice(256 * half, 256 * half + 256)
            query = q_ref[rows, lanes]
            up = u_ref[rows, lanes]
            key = kp_ref[keys, lanes]
            value = vp_ref[keys, lanes]
            scores = dot_nt(key, query) * FACTOR
            query_id = jnp.where(lane < 128, key_ids[2 + 2 * half], key_ids[3 + 2 * half])
            parts = []
            for k in range(6):
                allowed = query_id == key_ids[2 * half + k]
                parts.append(jnp.where(allowed, jnp.exp(scores[128 * k : 128 * k + 128]), 0.0))
            exponent = jnp.concatenate(parts, axis=0)
            prob = exponent * (1.0 / jnp.sum(exponent, axis=0, keepdims=True))
            prob_low = prob.astype(BF16)
            attended = dot(value_t[:, keys], prob_low)
            delta = jnp.sum(up.astype(F32).T * attended, axis=0, keepdims=True)
            dprob = dot_nt(value, up)
            dscore = (prob * (dprob - delta) * FACTOR).astype(BF16)
            dquery = dot(key_t[:, keys], dscore)
            gp_ref[2, rows, lanes] = dquery.T.astype(BF16)
            gp_ref[3, rows, lanes] = attended.T.astype(BF16)
            dkey = dot(dscore, query)
            dvalue = dot(prob_low, up)
            for ref, grad in ((dk_ref, dkey), (dv_ref, dvalue)):
                if half == 0:
                    ref[0:WINDOW, lanes] = grad
                else:
                    ref[256:WINDOW, lanes] += grad[: WINDOW - 256]
                    ref[WINDOW:PAD_TOK, lanes] = grad[WINDOW - 256 :]
        for j, ref in ((0, dk_ref), (1, dv_ref)):
            hs_ref[h, j, 0] = ref[0:HALO, lanes].astype(BF16)
            hs_ref[h, j, 1] = ref[HALO + TOK : PAD_TOK, lanes].astype(BF16)
            back.append(send(hs_ref.at[h, j, 0], hr_ref.at[h, j, 0], previous))
            back.append(send(hs_ref.at[h, j, 1], hr_ref.at[h, j, 1], following))

    def weight_grad(g):
        src = got_ref if g == 3 else xt_ref

        def body(i, _):
            blocks = pl.ds(i * 4, 4)
            grad = dot(src[blocks].reshape(896, TOK), gp_ref[g]).astype(BF16)
            part_ref[g, blocks] = grad.reshape(4, 2, CHIP_ROWS, LANES)
            return 0

        lax.fori_loop(0, 2, body, 0)

    chain = {}

    def ring_step(t, i):
        g = groups[i]
        if t == 4:
            swap[i].wait_recv()
        for side in (0, 1):
            y = (yl, other)[side]
            for sign in (1, -1):
                if t == 4 and side != (0 if sign == 1 else 1):
                    continue
                zz = at_z(sign * t)
                total = part_ref[g, zz, y].astype(F32) + ps_ref[i, zz, y].astype(F32)
                if (sign, t + 1, i, side) in chain:
                    chain[sign, t + 1, i, side].wait_recv()
                    total += rb_ref[(sign + 1) // 2, t, i, side].astype(F32)
                part_ref[g, zz, y] = total.astype(BF16)
                chain[sign, t, i, side] = send(
                    part_ref.at[g, zz, y],
                    rb_ref.at[(sign + 1) // 2, t - 1, i, side],
                    z_next[sign],
                )

    y_copies = {}

    def y_stage(i):
        g = groups[i]
        for side in (1, 0):
            y = (yl, other)[side]
            total = part_ref[g, z, y].astype(F32) + ps_ref[i, z, y].astype(F32)
            for sign in (1, -1):
                chain[sign, 1, i, side].wait_recv()
                total += rb_ref[(sign + 1) // 2, 0, i, side].astype(F32)
            if side == 1:
                ys_ref[i] = total.astype(BF16)
                y_copies[i] = send(ys_ref.at[i], yr_ref.at[i], y_pair)
            else:
                fin_ref[i] = total

    weight_grad(2)
    weight_grad(3)
    swap = {1: send(part_ref.at[3 - core], ps_ref.at[1], sibling)}
    ring_step(4, 1)
    for copy in back:
        copy.wait_recv()
    for h in (0, 1):
        lanes = slice(128 * h, 128 * h + 128)
        for j, ref in ((0, dk_ref), (1, dv_ref)):
            low = ref[HALO : 2 * HALO, lanes] + hr_ref[h, j, 1].astype(F32)
            high = ref[2 * HALO : 3 * HALO, lanes] + hr_ref[h, j, 0].astype(F32)
            gp_ref[j, 0:HALO, lanes] = low.astype(BF16)
            gp_ref[j, HALO:TOK, lanes] = high.astype(BF16)

    yh, xx = tp // 4, lax.rem(tp, 4)
    y_other = (seq, (1 - yh) * 4 + xx)

    def x_at(e):
        return lax.rem(xx + e, 4)

    def x_peer(e):
        return (seq, yh * 4 + x_at(e))

    def block_at(e, p):
        return pl.ds(pl.multiple_of(x_at(e) * BLOCK + p * PART, PART), PART)

    def part_of(p):
        return pl.ds(p * PART, PART)

    def partial_norm(half, start, stop):
        rows = pl.ds(pl.multiple_of(half * 256, 256), 256)
        total = dot_nt(gp_ref[0, rows], weights(0)[start:stop])
        total += dot_nt(gp_ref[1, rows], weights(1)[start:stop])
        total += dot_nt(gp_ref[2, rows], weights(2)[start:stop])
        return total.astype(BF16)

    gb_ref[1 - yh] = partial_norm(1 - yh, CUT, D)
    y_first = {}
    for p in (0, 1):
        for e in (1, 3, 2, 0):
            src, dst = gb_ref.at[1 - yh, block_at(e, p)], rb1_ref.at[e, part_of(p)]
            y_first[e, p] = send(src, dst, y_other)
    for half in (0, 1):
        ga_ref[half] = partial_norm(half, 0, CUT)
    x_first = {}
    for p in (0, 1):
        for e in (1, 3, 2):
            src, dst = ga_ref.at[:, block_at(e, p)], ra1_ref.at[e - 1, :, part_of(p)]
            x_first[e, p] = send(src, dst, x_peer(e))
    gb_ref[yh] = partial_norm(yh, CUT, D)


    weight_grad(0)
    weight_grad(1)
    swap[0] = send(part_ref.at[1 - core], ps_ref.at[0], sibling)

    x_second, y_second = {}, {}

    def second_step(p):
        part = part_of(p)
        for e in (1, 3, 2):
            y_first[e, p].wait_recv()
            total = gb_ref[yh, block_at(e, p)].astype(F32) + rb1_ref[e, part].astype(F32)
            sb2_ref[e - 1, part] = total.astype(BF16)
            src, dst = sb2_ref.at[e - 1, part], rb2_ref.at[e - 1, part]
            x_second[e, p] = send(src, dst, x_peer(e))
        for e in (1, 3, 2):
            x_first[e, p].wait_recv()

        def sum_x(half):
            total = ga_ref[half, block_at(0, p)].astype(F32)
            for e in (1, 2, 3):
                total += ra1_ref[e - 1, half, part].astype(F32)
            return total

        sa2_ref[part] = sum_x(1 - yh).astype(BF16)
        y_second[p] = send(sa2_ref.at[part], ra2_ref.at[part], y_other)
        suma_ref[part] = sum_x(yh)

    def norm_back(i, _):
        rows = pl.ds(pl.multiple_of(tp * BLOCK + i * 16, 16), 16)
        part = pl.ds(pl.multiple_of(i * 16, 16), 16)
        own_part = pl.ds(pl.multiple_of(xx * BLOCK + i * 16, 16), 16)
        first = suma_ref[part] + ra2_ref[part].astype(F32)
        second = gb_ref[yh, own_part].astype(F32) + rb1_ref[0, part].astype(F32)
        for e in range(3):
            second += rb2_ref[e, part].astype(F32)
        total = jnp.concatenate([first, second], axis=1)
        wide = x_ref[rows].astype(F32)
        center = wide - jnp.mean(wide, axis=-1, keepdims=True)
        inv_std = lax.rsqrt(jnp.mean(center * center, axis=-1, keepdims=True) + 1e-06)
        normed = center * inv_std
        grad = inv_std * (
            total
            - jnp.mean(total, axis=-1, keepdims=True)
            - normed * jnp.mean(total * normed, axis=-1, keepdims=True)
        )
        gi_ref[rows] = grad.astype(BF16)
        return 0

    first, second = pl.ds(0, CUT), pl.ds(CUT, D - CUT)
    y_gather, x_gather, gather = {}, {}, []

    def share(y, x, p, columns, to):
        rows = pl.ds(pl.multiple_of((y * 4 + x) * BLOCK + p * PART, PART), PART)
        piece = gi_ref.at[rows, columns]
        return send(piece, piece, to)

    def finish(p):
        y_first[0, p].wait_recv()
        for e in (1, 3, 2):
            x_second[e, p].wait_recv()
        y_second[p].wait_recv()
        lax.fori_loop(2 * p, 2 * p + 2, norm_back, 0)
        y_gather[p] = share(yh, xx, p, first, y_other)
        for e in (1, 3, 2):
            x_gather[e, p] = share(yh, xx, p, second, x_peer(e))
        gather.append(share(yh, xx, p, second, y_other))
        for e in (1, 3, 2):
            gather.append(share(yh, xx, p, first, x_peer(e)))

    def forward(p):
        y_gather[p].wait_recv()
        for e in (1, 3, 2):
            gather.append(share(1 - yh, xx, p, first, x_peer(e)))
        for e in (1, 3, 2):
            x_gather[e, p].wait_recv()
            gather.append(share(yh, x_at(4 - e), p, second, y_other))

    ring_step(3, 1)
    ring_step(4, 0)
    second_step(0)
    ring_step(2, 1)
    second_step(1)
    ring_step(3, 0)
    finish(0)
    ring_step(1, 1)
    ring_step(2, 0)
    finish(1)
    y_stage(1)
    ring_step(1, 0)
    forward(0)
    forward(1)
    y_stage(0)
    own_rows = pl.ds(pl.multiple_of(56 * core, 8), 56)
    sib_rows = pl.ds(pl.multiple_of(56 * (1 - core), 8), 56)
    for i in (0, 1):
        y_copies[i].wait_recv()
        fin_ref[i] += yr_ref[i].astype(F32)
        fs_ref[i] = fin_ref[i, sib_rows]
        og_ref[groups[i]] = fin_ref[i, own_rows]
    last = send(fs_ref, fr_ref, sibling)
    last.wait_recv()
    og_ref[1 - core] = fr_ref[0]
    og_ref[3 - core] = fr_ref[1]
    for c, g in ((0, 2), (1, 0), (2, 1)):
        qkv_grad_ref[c] = close_up(og_ref[g])
    out_grad_ref[...] = close_up(og_ref[3])

    for copy in gather:
        copy.wait_recv()
    send.drain()


def publish(gi, qkv_grad, out_grad, gi_out, qkv_out, out_out, gi_buf, qkv_buf, out_buf, sems):
    moves = []
    for i in range(4):
        rows = pl.ds(i * (TOK // 4), TOK // 4)
        moves.append((gi.at[rows], gi_buf.at[rows], gi_out.at[rows]))
    moves.append((qkv_grad, qkv_buf, qkv_out))
    moves.append((out_grad, out_buf, out_out))
    loads, stores = [], []
    for i, (src, buf, dst) in enumerate(moves):
        loads.append(pltpu.make_async_copy(src, buf, sems.at[0, i]))
        stores.append(pltpu.make_async_copy(buf, dst, sems.at[1, i]))
        loads[-1].start()
    for load, store in zip(loads, stores):
        load.wait()
        store.start()
    for store in stores:
        store.wait()


def per_device(layer_input, grad_output, tile_image, qkv_weight, out_weight):
    vmem = pltpu.VMEM
    shapes = (
        jax.ShapeDtypeStruct((TOK, D), BF16),
        jax.ShapeDtypeStruct((3, 56, 2 * HD), F32),
        jax.ShapeDtypeStruct((56, 2 * HD), F32),
    )
    results = pl.pallas_call(
        kernel,
        out_shape=shapes,
        in_specs=[
            pl.BlockSpec(memory_space=pl.ANY),
            pl.BlockSpec(memory_space=pl.ANY),
            pl.BlockSpec(memory_space=pltpu.VMEM),
            pl.BlockSpec(memory_space=pltpu.VMEM),
            pl.BlockSpec(memory_space=pltpu.SMEM),
        ],
        out_specs=(
            pl.BlockSpec(memory_space=pltpu.VMEM),
            pl.BlockSpec(memory_space=pltpu.VMEM),
            pl.BlockSpec(memory_space=pltpu.VMEM),
        ),
        scratch_shapes=[
            vmem((4, 56, LANES), F32),
            vmem((TOK, D), BF16),
            vmem((TOK, D), BF16),
            vmem((8, 2, 2, 56, PACK), BF16),
            vmem((8, 2, 2, 56, 8 * HD - PACK), BF16),
            vmem((4, 8, 2, CHIP_ROWS, LANES), BF16),
            vmem((8, TOK, LANES), BF16),
            vmem((8, TOK, LANES), BF16),
            vmem((4, TOK, LANES), F32),
            vmem((8, 2 * CHIP_ROWS, TOK), BF16),
            vmem((8, 2 * CHIP_ROWS, TOK), BF16),
            vmem((PAD_TOK, LANES), BF16),
            vmem((PAD_TOK, LANES), BF16),
            vmem((TOK, LANES), BF16),
            vmem((TOK, LANES), BF16),
            vmem((PAD_TOK, LANES), F32),
            vmem((PAD_TOK, LANES), F32),
            vmem((2, 2, 2, HALO, 128), BF16),
            vmem((2, 2, 2, HALO, 128), BF16),
            vmem((4, TOK, LANES), BF16),
            vmem((4, 8, 2, CHIP_ROWS, LANES), BF16),
            vmem((2, 8, 2, CHIP_ROWS, LANES), BF16),
            vmem((2, 4, 2, 2, CHIP_ROWS, LANES), BF16),
            vmem((2, CHIP_ROWS, LANES), BF16),
            vmem((2, CHIP_ROWS, LANES), BF16),
            vmem((2, CHIP_ROWS, LANES), F32),
            vmem((2, 56, LANES), F32),
            vmem((2, 56, LANES), F32),
            vmem((2, 256, CUT), BF16),
            vmem((2, 256, D - CUT), BF16),
            vmem((3, 2, BLOCK, CUT), BF16),
            vmem((4, BLOCK, D - CUT), BF16),
            vmem((BLOCK, CUT), BF16),
            vmem((BLOCK, CUT), BF16),
            vmem((3, BLOCK, D - CUT), BF16),
            vmem((3, BLOCK, D - CUT), BF16),
            vmem((BLOCK, CUT), F32),
            pltpu.SemaphoreType.DMA((N_COPIES,)),
            pltpu.SemaphoreType.DMA((N_COPIES,)),
            pltpu.SemaphoreType.DMA((2,)),
        ],
        compiler_params=pltpu.CompilerParams(
            collective_id=0, has_side_effects=True, vmem_limit_bytes=56 << 20
        ),
        name="attention_backward",
    )(layer_input, grad_output, qkv_weight.transpose(1, 0, 2), out_weight, tile_image)
    grad_input, qkv_grad, out_grad = pl.pallas_call(
        publish,
        out_shape=shapes,
        in_specs=[pl.BlockSpec(memory_space=pl.ANY)] * 3,
        out_specs=[pl.BlockSpec(memory_space=pl.ANY)] * 3,
        scratch_shapes=[
            vmem((TOK, D), BF16),
            vmem((3, 56, 2 * HD), F32),
            vmem((56, 2 * HD), F32),
            pltpu.SemaphoreType.DMA((2, 6)),
        ],
        name="publish",
    )(*results)
    return (grad_input, qkv_grad.transpose(1, 0, 2), out_grad)


def solution(mesh):
    placed = (P("seq", None), P("seq", None), P(), P("seq", None, "tp"), P("seq", "tp"))
    return jax.shard_map(
        per_device,
        mesh=mesh,
        in_specs=placed,
        out_specs=(P("seq", None), P("seq", None, "tp"), P("seq", "tp")),
        check_vma=False,
    )
```

```python
import functools

import jax
import jax.numpy as jnp
from jax import lax
from jax.experimental import pallas as pl
from jax.experimental.pallas import tpu as pltpu
from jax.sharding import PartitionSpec as P

HD = 112
TILE = 128
LANES = 256
TOK = 512
D = 1792
CHIP_ROWS = 112
HALO = 256
PAD_TOK = TOK + 2 * HALO
WINDOW = 768
BLOCK = 64
PART = 32
CUT = 768
PACK = 512
FACTOR = float(HD) ** (-0.5)
F32 = jnp.float32
BF16 = jnp.bfloat16
MESH = pl.DeviceIdType.MESH
N_COPIES = 176

NT = (((1,), (1,)), ((), ()))


def dot(a, b):
    return jnp.dot(a, b, preferred_element_type=F32)


def dot_nt(a, b):
    return lax.dot_general(a, b, NT, preferred_element_type=F32)


class Sender:
    def __init__(self, send_sems, recv_sems):
        self.send_sems, self.recv_sems = send_sems, recv_sems
        self.copies = []

    def __call__(self, src, dst, device):
        index = len(self.copies)
        copy = pltpu.make_async_remote_copy(
            src_ref=src,
            dst_ref=dst,
            send_sem=self.send_sems.at[index],
            recv_sem=self.recv_sems.at[index],
            device_id=device,
            device_id_type=MESH,
        )
        copy.start()
        self.copies.append(copy)
        return copy

    def drain(self):
        for copy in self.copies:
            copy.wait_send()


def kernel(
    x_hbm,
    go_hbm,
    qkv_ref,
    out_ref,
    ids_ref,
    gi_ref,
    qkv_grad_ref,
    out_grad_ref,
    og_ref,
    x_ref,
    go_ref,
    wp_ref,
    wq_ref,
    w_ref,
    xb_ref,
    gob_ref,
    acc_ref,
    xt_ref,
    got_ref,
    kp_ref,
    vp_ref,
    q_ref,
    u_ref,
    dk_ref,
    dv_ref,
    hs_ref,
    hr_ref,
    gp_ref,
    part_ref,
    ps_ref,
    rb_ref,
    ys_ref,
    yr_ref,
    fin_ref,
    fs_ref,
    fr_ref,
    ga_ref,
    gb_ref,
    ra1_ref,
    rb1_ref,
    sa2_ref,
    ra2_ref,
    sb2_ref,
    rb2_ref,
    suma_ref,
    send_sems,
    recv_sems,
    load_sems,
):
    seq = lax.axis_index("seq")
    tp = lax.axis_index("tp")
    core = lax.rem(seq, 2)
    z = lax.rem(seq // 2, 8)
    yl = seq // 16
    other = 1 - yl

    def at_z(offset):
        return lax.rem(z + 8 + offset, 8)

    def device(yl_, z_, core_):
        return (yl_ * 16 + z_ * 2 + core_, tp)

    sibling = device(yl, z, 1 - core)
    z_next = {1: device(yl, at_z(1), core), -1: device(yl, at_z(-1), core)}
    y_pair = device(other, z, core)
    following = (lax.rem(seq + 1, 32), tp)
    previous = (lax.rem(seq + 31, 32), tp)

    def tp_peer(d):
        return jnp.bitwise_xor(tp, d)

    load_x = pltpu.make_async_copy(x_hbm, x_ref, load_sems.at[0])
    load_go = pltpu.make_async_copy(go_hbm, go_ref, load_sems.at[1])
    load_x.start()
    load_go.start()

    barrier = pltpu.get_barrier_semaphore()
    peers = [sibling, z_next[1], z_next[-1], y_pair, following, previous]
    peers += [(seq, tp_peer(d)) for d in range(1, 8)]

    def close_up(wide):
        return jnp.concatenate([wide[:, :HD], wide[:, 128 : 128 + HD]], axis=1)

    own = [qkv_ref[1], qkv_ref[2], qkv_ref[0], out_ref[...]]
    own = jnp.concatenate([rows.astype(F32) for rows in own], axis=1).astype(BF16)
    wp_ref[z, yl, core] = own[:, :PACK]
    wq_ref[z, yl, core] = own[:, PACK:]
    for peer in peers:
        pl.semaphore_signal(barrier, inc=1, device_id=peer, device_id_type=MESH)
    pl.semaphore_wait(barrier, len(peers))

    send = Sender(send_sems, recv_sems)
    groups = (core, 2 + core)

    first_own = wp_ref.at[z, yl, core]
    second_own = wq_ref.at[z, yl, core]
    ring, cross, relay, beside = {}, {}, {}, {t: [] for t in range(6)}
    for sign in (1, -1):
        ring[sign, 1, 0] = send(first_own, first_own, z_next[sign])
    cross = send(first_own, first_own, y_pair)
    for sign in (1, -1):
        ring[sign, 1, 2] = send(second_own, second_own, z_next[sign])
    relay[0] = [send(second_own, second_own, y_pair)]
    beside[0].append(send(first_own, first_own, sibling))
    beside[0].append(send(second_own, second_own, sibling))
    load_x.wait()

    def split_columns(dst, rows, wide):
        for k in range(8):
            low = wide[:, CHIP_ROWS * k : CHIP_ROWS * (k + 1)]
            high = wide[:, 896 + CHIP_ROWS * k : 896 + CHIP_ROWS * (k + 1)]
            dst[k, rows, 0 : 2 * CHIP_ROWS] = jnp.concatenate([low, high], axis=1).astype(BF16)

    def split_rows(start):
        rows = slice(start, start + 32)
        split_columns(gob_ref, rows, go_ref[rows].astype(F32))

    def norm_rows(start):
        rows = slice(start, start + 32)
        wide = x_ref[rows].astype(F32)
        mean = jnp.mean(wide, axis=-1, keepdims=True)
        center = wide - mean
        inv_std = lax.rsqrt(jnp.mean(center * center, axis=-1, keepdims=True) + 1e-06)
        split_columns(xb_ref, rows, center * inv_std)

    def transpose_block(src, dst, k):
        dst[k] = src[k].T[: 2 * CHIP_ROWS]

    work = [functools.partial(norm_rows, 32 * i) for i in range(16)]
    work += [functools.partial(split_rows, 32 * i) for i in range(16)]
    later = []
    for source, target in ((gob_ref, got_ref), (xb_ref, xt_ref)):
        for k in range(8):
            later.append(functools.partial(transpose_block, source, target, k))
    work.reverse()
    later.reverse()

    def do_some(count):
        for _ in range(count):
            if work or later:
                (work or later).pop()()

    def unpack(k):
        first = wp_ref[k].astype(F32).reshape(2 * CHIP_ROWS, PACK)
        second = wq_ref[k].astype(F32).reshape(2 * CHIP_ROWS, 8 * HD - PACK)
        packed = jnp.concatenate([first, second], axis=1)
        gap = jnp.zeros((2 * CHIP_ROWS, 128 - HD), F32)
        for g in range(4):
            low = packed[:, 2 * HD * g : 2 * HD * g + HD]
            high = packed[:, 2 * HD * g + HD : 2 * HD * (g + 1)]
            wide = jnp.concatenate([low, gap, high, gap], axis=1).astype(BF16)
            w_ref[g, k] = wide.reshape(2, CHIP_ROWS, LANES)

    def project(blocks, first=False):
        for k in blocks:
            unpack(k)
        for g, src in ((0, xb_ref), (1, xb_ref), (2, xb_ref), (3, gob_ref)):
            total = 0.0 if first else acc_ref[g]
            for k in blocks:
                block = w_ref[g, k].reshape(2 * CHIP_ROWS, LANES)
                total += dot(src[k, :, 0 : 2 * CHIP_ROWS], block)
            acc_ref[g] = total

    block = wp_ref.at[z, other, core]
    cross.wait_recv()
    for sign in (1, -1):
        ring[sign, 1, 1] = send(block, block, z_next[sign])
    beside[0].append(send(block, block, sibling))
    load_go.wait()
    do_some(4)

    def piece(kind, k):
        ref = wq_ref if kind == 2 else wp_ref
        return ref.at[k, other if kind == 1 else yl, core]

    turn = 1 - 2 * core
    turned = device(yl, at_z(turn), core)
    for t in (1, 2, 3, 4):
        relay[t] = []
        for kind in (0, 2, 1):
            for sign in (1, -1):
                if (sign, t, kind) not in ring:
                    continue
                ring[sign, t, kind].wait_recv()
                block = piece(kind, at_z(-sign * t))
                if t < 3 or (t == 3 and kind < 2 and sign == (1, -1)[kind]):
                    ring[sign, t + 1, kind] = send(block, block, z_next[sign])
                if t == 3 and kind == 2 and sign == -1:
                    farthest = piece(kind, at_z(-turn * t))
                    ring[1, 4, 2] = send(farthest, farthest, turned)
                if kind == 2:
                    relay[t].append(send(block, block, y_pair))
                beside[t].append(send(block, block, sibling))
            do_some(3)
        spots = [z] if t == 1 else [at_z(1 - t), at_z(t - 1)]
        for copy, k in zip(relay[t - 1], spots):
            copy.wait_recv()
            block = wq_ref.at[k, other, core]
            beside[t - 1].append(send(block, block, sibling))
        if t == 2:
            do_some(len(work))
            for copy in beside[0]:
                copy.wait_recv()
            project([z], True)
        if t > 2:
            for copy in beside[t - 2]:
                copy.wait_recv()
            project([at_z(2 - t), at_z(t - 2)])
    relay[4][0].wait_recv()
    block = wq_ref.at[at_z(4), other, core]
    beside[4].append(send(block, block, sibling))
    for copy in beside[3]:
        copy.wait_recv()
    project([at_z(-3), at_z(3)])
    do_some(len(later))
    for copy in beside[4]:
        copy.wait_recv()
    unpack(at_z(4))

    def weights(g):
        return jnp.concatenate([w_ref[g, :, y].reshape(896, LANES) for y in (0, 1)], axis=0)

    halo = []
    def finished(g):
        src = gob_ref if g == 3 else xb_ref
        k = at_z(4)
        block = w_ref[g, k].reshape(2 * CHIP_ROWS, LANES)
        return (acc_ref[g] + dot(src[k, :, 0 : 2 * CHIP_ROWS], block)).astype(BF16)

    for g, ref in ((0, kp_ref), (1, vp_ref)):
        ref[HALO : HALO + TOK] = finished(g)
        halo.append(send(ref.at[pl.ds(HALO, HALO)], ref.at[pl.ds(HALO + TOK, HALO)], previous))
        halo.append(send(ref.at[pl.ds(TOK, HALO)], ref.at[pl.ds(0, HALO)], following))
    q_ref[...] = finished(2)
    u_ref[...] = finished(3)

    def tile_id(tile):
        inside = jnp.logical_and(tile >= 0, tile < 128)
        value = ids_ref[jnp.clip(tile, 0, 127)]
        return jnp.where(inside, value, -1)

    key_ids = [tile_id(4 * seq - 2 + k) for k in range(8)]
    lane = lax.broadcasted_iota(jnp.int32, (1, 256), 1)
    for copy in halo:
        copy.wait_recv()

    back = []
    for h in (0, 1):
        lanes = slice(128 * h, 128 * h + 128)
        key_t = kp_ref[:, lanes].T
        value_t = vp_ref[:, lanes].T
        for half in (0, 1):
            keys = slice(256 * half, 256 * half + WINDOW)
            rows = slice(256 * half, 256 * half + 256)
            query = q_ref[rows, lanes]
            up = u_ref[rows, lanes]
            key = kp_ref[keys, lanes]
            value = vp_ref[keys, lanes]
            scores = dot_nt(key, query) * FACTOR
            query_id = jnp.where(lane < 128, key_ids[2 + 2 * half], key_ids[3 + 2 * half])
            parts = []
            for k in range(6):
                allowed = query_id == key_ids[2 * half + k]
                parts.append(jnp.where(allowed, jnp.exp(scores[128 * k : 128 * k + 128]), 0.0))
            exponent = jnp.concatenate(parts, axis=0)
            prob = exponent * (1.0 / jnp.sum(exponent, axis=0, keepdims=True))
            prob_low = prob.astype(BF16)
            attended = dot(value_t[:, keys], prob_low)
            delta = jnp.sum(up.astype(F32).T * attended, axis=0, keepdims=True)
            dprob = dot_nt(value, up)
            dscore = (prob * (dprob - delta) * FACTOR).astype(BF16)
            dquery = dot(key_t[:, keys], dscore)
            gp_ref[2, rows, lanes] = dquery.T.astype(BF16)
            gp_ref[3, rows, lanes] = attended.T.astype(BF16)
            dkey = dot(dscore, query)
            dvalue = dot(prob_low, up)
            for ref, grad in ((dk_ref, dkey), (dv_ref, dvalue)):
                if half == 0:
                    ref[0:WINDOW, lanes] = grad
                else:
                    ref[256:WINDOW, lanes] += grad[: WINDOW - 256]
                    ref[WINDOW:PAD_TOK, lanes] = grad[WINDOW - 256 :]
        for j, ref in ((0, dk_ref), (1, dv_ref)):
            hs_ref[h, j, 0] = ref[0:HALO, lanes].astype(BF16)
            hs_ref[h, j, 1] = ref[HALO + TOK : PAD_TOK, lanes].astype(BF16)
            back.append(send(hs_ref.at[h, j, 0], hr_ref.at[h, j, 0], previous))
            back.append(send(hs_ref.at[h, j, 1], hr_ref.at[h, j, 1], following))

    def weight_grad(g):
        src = got_ref if g == 3 else xt_ref

        def body(i, _):
            blocks = pl.ds(i * 4, 4)
            grad = dot(src[blocks].reshape(896, TOK), gp_ref[g]).astype(BF16)
            part_ref[g, blocks] = grad.reshape(4, 2, CHIP_ROWS, LANES)
            return 0

        lax.fori_loop(0, 2, body, 0)

    chain = {}

    def ring_step(t, i):
        g = groups[i]
        if t == 4:
            swap[i].wait_recv()
        for sign in (1, -1):
            way = (sign + 1) // 2
            zz = at_z(sign * t)
            half = yl if sign == 1 else other
            if t < 4:
                chain[sign, t + 1, i].wait_recv()
            if t < 3:
                total = part_ref[g, zz].astype(F32) + ps_ref[i, zz].astype(F32)
                total += rb_ref[way, t, i].astype(F32)
                part_ref[g, zz] = total.astype(BF16)
            else:
                total = part_ref[g, zz, half].astype(F32) + ps_ref[i, zz, half].astype(F32)
                if t == 3:
                    total += rb_ref[way, t, i, half].astype(F32)
                    rest = part_ref[g, zz, 1 - half].astype(F32)
                    rest += ps_ref[i, zz, 1 - half].astype(F32)
                    part_ref[g, zz, 1 - half] = rest.astype(BF16)
                part_ref[g, zz, half] = total.astype(BF16)
            if t == 4:
                src, dst = part_ref.at[g, zz, half], rb_ref.at[way, t - 1, i, half]
            else:
                src, dst = part_ref.at[g, zz], rb_ref.at[way, t - 1, i]
            chain[sign, t, i] = send(src, dst, z_next[sign])

    y_copies = {}

    def y_stage(i):
        g = groups[i]
        for sign in (1, -1):
            chain[sign, 1, i].wait_recv()
        for y in (other, yl):
            total = part_ref[g, z, y].astype(F32) + ps_ref[i, z, y].astype(F32)
            for way in (0, 1):
                total += rb_ref[way, 0, i, y].astype(F32)
            if y is other:
                ys_ref[i] = total.astype(BF16)
                y_copies[i] = send(ys_ref.at[i], yr_ref.at[i], y_pair)
            else:
                fin_ref[i] = total

    weight_grad(2)
    weight_grad(3)
    swap = {1: send(part_ref.at[3 - core], ps_ref.at[1], sibling)}
    ring_step(4, 1)
    for copy in back:
        copy.wait_recv()
    for h in (0, 1):
        lanes = slice(128 * h, 128 * h + 128)
        for j, ref in ((0, dk_ref), (1, dv_ref)):
            low = ref[HALO : 2 * HALO, lanes] + hr_ref[h, j, 1].astype(F32)
            high = ref[2 * HALO : 3 * HALO, lanes] + hr_ref[h, j, 0].astype(F32)
            gp_ref[j, 0:HALO, lanes] = low.astype(BF16)
            gp_ref[j, HALO:TOK, lanes] = high.astype(BF16)

    yh, xx = tp // 4, lax.rem(tp, 4)
    y_other = (seq, (1 - yh) * 4 + xx)

    def x_at(e):
        return lax.rem(xx + e, 4)

    def x_peer(e):
        return (seq, yh * 4 + x_at(e))

    def block_at(e, p):
        return pl.ds(pl.multiple_of(x_at(e) * BLOCK + p * PART, PART), PART)

    def part_of(p):
        return pl.ds(p * PART, PART)

    def partial_norm(half, start, stop):
        rows = pl.ds(pl.multiple_of(half * 256, 256), 256)
        total = dot_nt(gp_ref[0, rows], weights(0)[start:stop])
        total += dot_nt(gp_ref[1, rows], weights(1)[start:stop])
        total += dot_nt(gp_ref[2, rows], weights(2)[start:stop])
        return total.astype(BF16)

    gb_ref[1 - yh] = partial_norm(1 - yh, CUT, D)
    y_first = {}
    for p in (0, 1):
        for e in (1, 3, 2, 0):
            src, dst = gb_ref.at[1 - yh, block_at(e, p)], rb1_ref.at[e, part_of(p)]
            y_first[e, p] = send(src, dst, y_other)
    for half in (0, 1):
        ga_ref[half] = partial_norm(half, 0, CUT)
    x_first = {}
    for p in (0, 1):
        for e in (1, 3, 2):
            src, dst = ga_ref.at[:, block_at(e, p)], ra1_ref.at[e - 1, :, part_of(p)]
            x_first[e, p] = send(src, dst, x_peer(e))
    gb_ref[yh] = partial_norm(yh, CUT, D)


    weight_grad(0)
    weight_grad(1)
    swap[0] = send(part_ref.at[1 - core], ps_ref.at[0], sibling)

    x_second, y_second = {}, {}

    def second_step(p):
        part = part_of(p)
        for e in (1, 3, 2):
            y_first[e, p].wait_recv()
            total = gb_ref[yh, block_at(e, p)].astype(F32) + rb1_ref[e, part].astype(F32)
            sb2_ref[e - 1, part] = total.astype(BF16)
            src, dst = sb2_ref.at[e - 1, part], rb2_ref.at[e - 1, part]
            x_second[e, p] = send(src, dst, x_peer(e))
        for e in (1, 3, 2):
            x_first[e, p].wait_recv()

        def sum_x(half):
            total = ga_ref[half, block_at(0, p)].astype(F32)
            for e in (1, 2, 3):
                total += ra1_ref[e - 1, half, part].astype(F32)
            return total

        sa2_ref[part] = sum_x(1 - yh).astype(BF16)
        y_second[p] = send(sa2_ref.at[part], ra2_ref.at[part], y_other)
        suma_ref[part] = sum_x(yh)

    def norm_back(i, _):
        rows = pl.ds(pl.multiple_of(tp * BLOCK + i * 16, 16), 16)
        part = pl.ds(pl.multiple_of(i * 16, 16), 16)
        own_part = pl.ds(pl.multiple_of(xx * BLOCK + i * 16, 16), 16)
        first = suma_ref[part] + ra2_ref[part].astype(F32)
        second = gb_ref[yh, own_part].astype(F32) + rb1_ref[0, part].astype(F32)
        for e in range(3):
            second += rb2_ref[e, part].astype(F32)
        total = jnp.concatenate([first, second], axis=1)
        wide = x_ref[rows].astype(F32)
        center = wide - jnp.mean(wide, axis=-1, keepdims=True)
        inv_std = lax.rsqrt(jnp.mean(center * center, axis=-1, keepdims=True) + 1e-06)
        normed = center * inv_std
        grad = inv_std * (
            total
            - jnp.mean(total, axis=-1, keepdims=True)
            - normed * jnp.mean(total * normed, axis=-1, keepdims=True)
        )
        gi_ref[rows] = grad.astype(BF16)
        return 0

    first, second = pl.ds(0, CUT), pl.ds(CUT, D - CUT)
    y_gather, x_gather, gather = {}, {}, []

    def share(y, x, p, columns, to):
        rows = pl.ds(pl.multiple_of((y * 4 + x) * BLOCK + p * PART, PART), PART)
        piece = gi_ref.at[rows, columns]
        return send(piece, piece, to)

    def finish(p):
        y_first[0, p].wait_recv()
        for e in (1, 3, 2):
            x_second[e, p].wait_recv()
        y_second[p].wait_recv()
        lax.fori_loop(2 * p, 2 * p + 2, norm_back, 0)
        y_gather[p] = share(yh, xx, p, first, y_other)
        for e in (1, 3, 2):
            x_gather[e, p] = share(yh, xx, p, second, x_peer(e))
        gather.append(share(yh, xx, p, second, y_other))
        for e in (1, 3, 2):
            gather.append(share(yh, xx, p, first, x_peer(e)))

    def forward(p):
        y_gather[p].wait_recv()
        for e in (1, 3, 2):
            gather.append(share(1 - yh, xx, p, first, x_peer(e)))
        for e in (1, 3, 2):
            x_gather[e, p].wait_recv()
            gather.append(share(yh, x_at(4 - e), p, second, y_other))

    ring_step(3, 1)
    ring_step(4, 0)
    second_step(0)
    ring_step(2, 1)
    second_step(1)
    ring_step(3, 0)
    finish(0)
    ring_step(1, 1)
    ring_step(2, 0)
    finish(1)
    y_stage(1)
    ring_step(1, 0)
    forward(0)
    forward(1)
    y_stage(0)
    own_rows = pl.ds(pl.multiple_of(56 * core, 8), 56)
    sib_rows = pl.ds(pl.multiple_of(56 * (1 - core), 8), 56)
    for i in (0, 1):
        y_copies[i].wait_recv()
        fin_ref[i] += yr_ref[i].astype(F32)
        fs_ref[i] = fin_ref[i, sib_rows]
        og_ref[groups[i]] = fin_ref[i, own_rows]
    last = send(fs_ref, fr_ref, sibling)
    last.wait_recv()
    og_ref[1 - core] = fr_ref[0]
    og_ref[3 - core] = fr_ref[1]
    for c, g in ((0, 2), (1, 0), (2, 1)):
        qkv_grad_ref[c] = close_up(og_ref[g])
    out_grad_ref[...] = close_up(og_ref[3])

    for copy in gather:
        copy.wait_recv()
    send.drain()


def publish(gi, qkv_grad, out_grad, gi_out, qkv_out, out_out, gi_buf, qkv_buf, out_buf, sems):
    moves = []
    for i in range(4):
        rows = pl.ds(i * (TOK // 4), TOK // 4)
        moves.append((gi.at[rows], gi_buf.at[rows], gi_out.at[rows]))
    moves.append((qkv_grad, qkv_buf, qkv_out))
    moves.append((out_grad, out_buf, out_out))
    loads, stores = [], []
    for i, (src, buf, dst) in enumerate(moves):
        loads.append(pltpu.make_async_copy(src, buf, sems.at[0, i]))
        stores.append(pltpu.make_async_copy(buf, dst, sems.at[1, i]))
        loads[-1].start()
    for load, store in zip(loads, stores):
        load.wait()
        store.start()
    for store in stores:
        store.wait()


def per_device(layer_input, grad_output, tile_image, qkv_weight, out_weight):
    vmem = pltpu.VMEM
    shapes = (
        jax.ShapeDtypeStruct((TOK, D), BF16),
        jax.ShapeDtypeStruct((3, 56, 2 * HD), F32),
        jax.ShapeDtypeStruct((56, 2 * HD), F32),
    )
    results = pl.pallas_call(
        kernel,
        out_shape=shapes,
        in_specs=[
            pl.BlockSpec(memory_space=pl.ANY),
            pl.BlockSpec(memory_space=pl.ANY),
            pl.BlockSpec(memory_space=pltpu.VMEM),
            pl.BlockSpec(memory_space=pltpu.VMEM),
            pl.BlockSpec(memory_space=pltpu.SMEM),
        ],
        out_specs=(
            pl.BlockSpec(memory_space=pltpu.VMEM),
            pl.BlockSpec(memory_space=pltpu.VMEM),
            pl.BlockSpec(memory_space=pltpu.VMEM),
        ),
        scratch_shapes=[
            vmem((4, 56, LANES), F32),
            vmem((TOK, D), BF16),
            vmem((TOK, D), BF16),
            vmem((8, 2, 2, 56, PACK), BF16),
            vmem((8, 2, 2, 56, 8 * HD - PACK), BF16),
            vmem((4, 8, 2, CHIP_ROWS, LANES), BF16),
            vmem((8, TOK, LANES), BF16),
            vmem((8, TOK, LANES), BF16),
            vmem((4, TOK, LANES), F32),
            vmem((8, 2 * CHIP_ROWS, TOK), BF16),
            vmem((8, 2 * CHIP_ROWS, TOK), BF16),
            vmem((PAD_TOK, LANES), BF16),
            vmem((PAD_TOK, LANES), BF16),
            vmem((TOK, LANES), BF16),
            vmem((TOK, LANES), BF16),
            vmem((PAD_TOK, LANES), F32),
            vmem((PAD_TOK, LANES), F32),
            vmem((2, 2, 2, HALO, 128), BF16),
            vmem((2, 2, 2, HALO, 128), BF16),
            vmem((4, TOK, LANES), BF16),
            vmem((4, 8, 2, CHIP_ROWS, LANES), BF16),
            vmem((2, 8, 2, CHIP_ROWS, LANES), BF16),
            vmem((2, 4, 2, 2, CHIP_ROWS, LANES), BF16),
            vmem((2, CHIP_ROWS, LANES), BF16),
            vmem((2, CHIP_ROWS, LANES), BF16),
            vmem((2, CHIP_ROWS, LANES), F32),
            vmem((2, 56, LANES), F32),
            vmem((2, 56, LANES), F32),
            vmem((2, 256, CUT), BF16),
            vmem((2, 256, D - CUT), BF16),
            vmem((3, 2, BLOCK, CUT), BF16),
            vmem((4, BLOCK, D - CUT), BF16),
            vmem((BLOCK, CUT), BF16),
            vmem((BLOCK, CUT), BF16),
            vmem((3, BLOCK, D - CUT), BF16),
            vmem((3, BLOCK, D - CUT), BF16),
            vmem((BLOCK, CUT), F32),
            pltpu.SemaphoreType.DMA((N_COPIES,)),
            pltpu.SemaphoreType.DMA((N_COPIES,)),
            pltpu.SemaphoreType.DMA((2,)),
        ],
        compiler_params=pltpu.CompilerParams(
            collective_id=0, has_side_effects=True, vmem_limit_bytes=56 << 20
        ),
        name="attention_backward",
    )(layer_input, grad_output, qkv_weight.transpose(1, 0, 2), out_weight, tile_image)
    grad_input, qkv_grad, out_grad = pl.pallas_call(
        publish,
        out_shape=shapes,
        in_specs=[pl.BlockSpec(memory_space=pl.ANY)] * 3,
        out_specs=[pl.BlockSpec(memory_space=pl.ANY)] * 3,
        scratch_shapes=[
            vmem((TOK, D), BF16),
            vmem((3, 56, 2 * HD), F32),
            vmem((56, 2 * HD), F32),
            pltpu.SemaphoreType.DMA((2, 6)),
        ],
        name="publish",
    )(*results)
    return (grad_input, qkv_grad.transpose(1, 0, 2), out_grad)


def solution(mesh):
    placed = (P("seq", None), P("seq", None), P(), P("seq", None, "tp"), P("seq", "tp"))
    return jax.shard_map(
        per_device,
        mesh=mesh,
        in_specs=placed,
        out_specs=(P("seq", None), P("seq", None, "tp"), P("seq", "tp")),
        check_vma=False,
    )
```

```python
import functools

import jax
import jax.numpy as jnp
from jax import lax
from jax.experimental import pallas as pl
from jax.experimental.pallas import tpu as pltpu
from jax.sharding import PartitionSpec as P

HD = 112
TILE = 128
LANES = 256
TOK = 512
D = 1792
CHIP_ROWS = 112
HALO = 256
PAD_TOK = TOK + 2 * HALO
WINDOW = 768
BLOCK = 64
PART = 32
CUT = 768
PACK = 512
FACTOR = float(HD) ** (-0.5)
F32 = jnp.float32
BF16 = jnp.bfloat16
MESH = pl.DeviceIdType.MESH
N_COPIES = 176

NT = (((1,), (1,)), ((), ()))


def dot(a, b):
    return jnp.dot(a, b, preferred_element_type=F32)


def dot_nt(a, b):
    return lax.dot_general(a, b, NT, preferred_element_type=F32)


class Sender:
    def __init__(self, send_sems, recv_sems):
        self.send_sems, self.recv_sems = send_sems, recv_sems
        self.copies = []

    def __call__(self, src, dst, device):
        index = len(self.copies)
        copy = pltpu.make_async_remote_copy(
            src_ref=src,
            dst_ref=dst,
            send_sem=self.send_sems.at[index],
            recv_sem=self.recv_sems.at[index],
            device_id=device,
            device_id_type=MESH,
        )
        copy.start()
        self.copies.append(copy)
        return copy

    def drain(self):
        for copy in self.copies:
            copy.wait_send()


def kernel(
    x_hbm,
    go_hbm,
    qkv_ref,
    out_ref,
    ids_ref,
    gi_ref,
    qkv_grad_ref,
    out_grad_ref,
    og_ref,
    x_ref,
    go_ref,
    wp_ref,
    wq_ref,
    w_ref,
    xb_ref,
    gob_ref,
    acc_ref,
    xt_ref,
    got_ref,
    kp_ref,
    vp_ref,
    q_ref,
    u_ref,
    dk_ref,
    dv_ref,
    hs_ref,
    hr_ref,
    gp_ref,
    part_ref,
    ps_ref,
    rb_ref,
    ys_ref,
    yr_ref,
    fin_ref,
    fs_ref,
    fr_ref,
    ga_ref,
    gb_ref,
    ra1_ref,
    rb1_ref,
    sa2_ref,
    ra2_ref,
    sb2_ref,
    rb2_ref,
    suma_ref,
    eo_ref,
    do_ref,
    send_sems,
    recv_sems,
    load_sems,
):
    seq = lax.axis_index("seq")
    tp = lax.axis_index("tp")
    core = lax.rem(seq, 2)
    z = lax.rem(seq // 2, 8)
    yl = seq // 16
    other = 1 - yl

    def at_z(offset):
        return lax.rem(z + 8 + offset, 8)

    def device(yl_, z_, core_):
        return (yl_ * 16 + z_ * 2 + core_, tp)

    sibling = device(yl, z, 1 - core)
    z_next = {1: device(yl, at_z(1), core), -1: device(yl, at_z(-1), core)}
    y_pair = device(other, z, core)
    following = (lax.rem(seq + 1, 32), tp)
    previous = (lax.rem(seq + 31, 32), tp)

    def tp_peer(d):
        return jnp.bitwise_xor(tp, d)

    load_x = pltpu.make_async_copy(x_hbm, x_ref, load_sems.at[0])
    load_go = pltpu.make_async_copy(go_hbm, go_ref, load_sems.at[1])
    load_x.start()
    load_go.start()

    barrier = pltpu.get_barrier_semaphore()
    peers = [sibling, z_next[1], z_next[-1], y_pair, following, previous]
    peers += [(seq, tp_peer(d)) for d in range(1, 8)]

    def close_up(wide):
        return jnp.concatenate([wide[:, :HD], wide[:, 128 : 128 + HD]], axis=1)

    own = [qkv_ref[1], qkv_ref[2], qkv_ref[0], out_ref[...]]
    own = jnp.concatenate([rows.astype(F32) for rows in own], axis=1).astype(BF16)
    wp_ref[z, yl, core] = own[:, :PACK]
    wq_ref[z, yl, core] = own[:, PACK:]
    for peer in peers:
        pl.semaphore_signal(barrier, inc=1, device_id=peer, device_id_type=MESH)
    pl.semaphore_wait(barrier, len(peers))

    send = Sender(send_sems, recv_sems)
    groups = (core, 2 + core)

    first_own = wp_ref.at[z, yl, core]
    second_own = wq_ref.at[z, yl, core]
    ring, cross, relay, beside = {}, {}, {}, {t: [] for t in range(6)}
    for sign in (1, -1):
        ring[sign, 1, 0] = send(first_own, first_own, z_next[sign])
    cross = send(first_own, first_own, y_pair)
    for sign in (1, -1):
        ring[sign, 1, 2] = send(second_own, second_own, z_next[sign])
    relay[0] = [send(second_own, second_own, y_pair)]
    beside[0].append(send(first_own, first_own, sibling))
    beside[0].append(send(second_own, second_own, sibling))
    load_x.wait()

    def split_columns(dst, rows, wide):
        for k in range(8):
            low = wide[:, CHIP_ROWS * k : CHIP_ROWS * (k + 1)]
            high = wide[:, 896 + CHIP_ROWS * k : 896 + CHIP_ROWS * (k + 1)]
            dst[k, rows, 0 : 2 * CHIP_ROWS] = jnp.concatenate([low, high], axis=1).astype(BF16)

    def split_rows(start):
        rows = slice(start, start + 32)
        split_columns(gob_ref, rows, go_ref[rows].astype(F32))

    def norm_rows(start):
        rows = slice(start, start + 32)
        wide = x_ref[rows].astype(F32)
        mean = jnp.mean(wide, axis=-1, keepdims=True)
        center = wide - mean
        inv_std = lax.rsqrt(jnp.mean(center * center, axis=-1, keepdims=True) + 1e-06)
        split_columns(xb_ref, rows, center * inv_std)

    def transpose_block(src, dst, k):
        dst[k] = src[k].T[: 2 * CHIP_ROWS]

    work = [functools.partial(norm_rows, 32 * i) for i in range(16)]
    work += [functools.partial(split_rows, 32 * i) for i in range(16)]
    later = []
    for source, target in ((gob_ref, got_ref), (xb_ref, xt_ref)):
        for k in range(8):
            later.append(functools.partial(transpose_block, source, target, k))
    work.reverse()
    later.reverse()

    def do_some(count):
        for _ in range(count):
            if work or later:
                (work or later).pop()()

    def unpack(k):
        first = wp_ref[k].astype(F32).reshape(2 * CHIP_ROWS, PACK)
        second = wq_ref[k].astype(F32).reshape(2 * CHIP_ROWS, 8 * HD - PACK)
        packed = jnp.concatenate([first, second], axis=1)
        gap = jnp.zeros((2 * CHIP_ROWS, 128 - HD), F32)
        for g in range(4):
            low = packed[:, 2 * HD * g : 2 * HD * g + HD]
            high = packed[:, 2 * HD * g + HD : 2 * HD * (g + 1)]
            wide = jnp.concatenate([low, gap, high, gap], axis=1).astype(BF16)
            w_ref[g, k] = wide.reshape(2, CHIP_ROWS, LANES)

    def project(blocks, first=False):
        for k in blocks:
            unpack(k)
        for g, src in ((0, xb_ref), (1, xb_ref), (2, xb_ref), (3, gob_ref)):
            total = 0.0 if first else acc_ref[g]
            for k in blocks:
                block = w_ref[g, k].reshape(2 * CHIP_ROWS, LANES)
                total += dot(src[k, :, 0 : 2 * CHIP_ROWS], block)
            acc_ref[g] = total

    block = wp_ref.at[z, other, core]
    cross.wait_recv()
    for sign in (1, -1):
        ring[sign, 1, 1] = send(block, block, z_next[sign])
    beside[0].append(send(block, block, sibling))
    load_go.wait()
    do_some(4)

    def piece(kind, k):
        ref = wq_ref if kind == 2 else wp_ref
        return ref.at[k, other if kind == 1 else yl, core]

    turn = 1 - 2 * core
    turned = device(yl, at_z(turn), core)
    for t in (1, 2, 3, 4):
        relay[t] = []
        for kind in (0, 2, 1):
            for sign in (1, -1):
                if (sign, t, kind) not in ring:
                    continue
                ring[sign, t, kind].wait_recv()
                block = piece(kind, at_z(-sign * t))
                if t < 3 or (t == 3 and kind < 2 and sign == (1, -1)[kind]):
                    ring[sign, t + 1, kind] = send(block, block, z_next[sign])
                if t == 3 and kind == 2 and sign == -1:
                    farthest = piece(kind, at_z(-turn * t))
                    ring[1, 4, 2] = send(farthest, farthest, turned)
                if kind == 2:
                    relay[t].append(send(block, block, y_pair))
                beside[t].append(send(block, block, sibling))
            do_some(3)
        spots = [z] if t == 1 else [at_z(1 - t), at_z(t - 1)]
        for copy, k in zip(relay[t - 1], spots):
            copy.wait_recv()
            block = wq_ref.at[k, other, core]
            beside[t - 1].append(send(block, block, sibling))
        if t == 2:
            do_some(len(work))
            for copy in beside[0]:
                copy.wait_recv()
            project([z], True)
        if t > 2:
            for copy in beside[t - 2]:
                copy.wait_recv()
            project([at_z(2 - t), at_z(t - 2)])
    relay[4][0].wait_recv()
    block = wq_ref.at[at_z(4), other, core]
    beside[4].append(send(block, block, sibling))
    for copy in beside[3]:
        copy.wait_recv()
    project([at_z(-3), at_z(3)])
    do_some(len(later))
    for copy in beside[4]:
        copy.wait_recv()
    unpack(at_z(4))

    def weights(g):
        return jnp.concatenate([w_ref[g, :, y].reshape(896, LANES) for y in (0, 1)], axis=0)

    halo = []
    def finished(g):
        src = gob_ref if g == 3 else xb_ref
        k = at_z(4)
        block = w_ref[g, k].reshape(2 * CHIP_ROWS, LANES)
        return (acc_ref[g] + dot(src[k, :, 0 : 2 * CHIP_ROWS], block)).astype(BF16)

    for g, ref in ((0, kp_ref), (1, vp_ref)):
        ref[HALO : HALO + TOK] = finished(g)
        halo.append(send(ref.at[pl.ds(HALO, HALO)], ref.at[pl.ds(HALO + TOK, HALO)], previous))
        halo.append(send(ref.at[pl.ds(TOK, HALO)], ref.at[pl.ds(0, HALO)], following))
    q_ref[...] = finished(2)
    u_ref[...] = finished(3)

    def tile_id(tile):
        inside = jnp.logical_and(tile >= 0, tile < 128)
        value = ids_ref[jnp.clip(tile, 0, 127)]
        return jnp.where(inside, value, -1)

    key_ids = [tile_id(4 * seq - 2 + k) for k in range(8)]
    lane = lax.broadcasted_iota(jnp.int32, (1, 256), 1)
    own_keys = slice(HALO, HALO + TOK)

    def exponents(h, half, start, count):
        lanes = slice(128 * h, 128 * h + 128)
        rows = slice(256 * half, 256 * half + 256)
        keys = slice(128 * start, 128 * (start + count))
        scores = dot_nt(kp_ref[keys, lanes], q_ref[rows, lanes]) * FACTOR
        query_id = jnp.where(lane < 128, key_ids[2 + 2 * half], key_ids[3 + 2 * half])
        parts = []
        for k in range(count):
            allowed = query_id == key_ids[start + k]
            parts.append(jnp.where(allowed, jnp.exp(scores[128 * k : 128 * k + 128]), 0.0))
        return jnp.concatenate(parts, axis=0)

    for h in (0, 1):
        lanes = slice(128 * h, 128 * h + 128)
        for half in (0, 1):
            rows = slice(256 * half, 256 * half + 256)
            eo_ref[h, half] = exponents(h, half, 2, 4)
            do_ref[h, half] = dot_nt(vp_ref[own_keys, lanes], u_ref[rows, lanes])
    for copy in halo:
        copy.wait_recv()

    back = []
    for h in (0, 1):
        lanes = slice(128 * h, 128 * h + 128)
        key_t = kp_ref[:, lanes].T
        value_t = vp_ref[:, lanes].T
        for half in (0, 1):
            keys = slice(256 * half, 256 * half + WINDOW)
            rows = slice(256 * half, 256 * half + 256)
            query = q_ref[rows, lanes]
            up = u_ref[rows, lanes]
            edge = slice(768 * half, 768 * half + HALO)
            edge_exponent = exponents(h, half, 6 * half, 2)
            edge_dprob = dot_nt(vp_ref[edge, lanes], up)
            order = -1 if half else 1
            exponent = jnp.concatenate([edge_exponent, eo_ref[h, half]][::order], axis=0)
            dprob = jnp.concatenate([edge_dprob, do_ref[h, half]][::order], axis=0)
            prob = exponent * (1.0 / jnp.sum(exponent, axis=0, keepdims=True))
            prob_low = prob.astype(BF16)
            attended = dot(value_t[:, keys], prob_low)
            delta = jnp.sum(up.astype(F32).T * attended, axis=0, keepdims=True)
            dscore = (prob * (dprob - delta) * FACTOR).astype(BF16)
            dquery = dot(key_t[:, keys], dscore)
            gp_ref[2, rows, lanes] = dquery.T.astype(BF16)
            gp_ref[3, rows, lanes] = attended.T.astype(BF16)
            dkey = dot(dscore, query)
            dvalue = dot(prob_low, up)
            for ref, grad in ((dk_ref, dkey), (dv_ref, dvalue)):
                if half == 0:
                    ref[0:WINDOW, lanes] = grad
                else:
                    ref[256:WINDOW, lanes] += grad[: WINDOW - 256]
                    ref[WINDOW:PAD_TOK, lanes] = grad[WINDOW - 256 :]
        for j, ref in ((0, dk_ref), (1, dv_ref)):
            hs_ref[h, j, 0] = ref[0:HALO, lanes].astype(BF16)
            hs_ref[h, j, 1] = ref[HALO + TOK : PAD_TOK, lanes].astype(BF16)
            back.append(send(hs_ref.at[h, j, 0], hr_ref.at[h, j, 0], previous))
            back.append(send(hs_ref.at[h, j, 1], hr_ref.at[h, j, 1], following))

    def weight_grad(g):
        src = got_ref if g == 3 else xt_ref

        def body(i, _):
            blocks = pl.ds(i * 4, 4)
            grad = dot(src[blocks].reshape(896, TOK), gp_ref[g]).astype(BF16)
            part_ref[g, blocks] = grad.reshape(4, 2, CHIP_ROWS, LANES)
            return 0

        lax.fori_loop(0, 2, body, 0)

    chain = {}

    def ring_step(t, i):
        g = groups[i]
        if t == 4:
            swap[i].wait_recv()
        for side in (0, 1):
            y = (yl, other)[side]
            for sign in (1, -1):
                if t == 4 and side != (0 if sign == 1 else 1):
                    continue
                zz = at_z(sign * t)
                total = part_ref[g, zz, y].astype(F32) + ps_ref[i, zz, y].astype(F32)
                if (sign, t + 1, i, side) in chain:
                    chain[sign, t + 1, i, side].wait_recv()
                    total += rb_ref[(sign + 1) // 2, t, i, side].astype(F32)
                part_ref[g, zz, y] = total.astype(BF16)
                chain[sign, t, i, side] = send(
                    part_ref.at[g, zz, y],
                    rb_ref.at[(sign + 1) // 2, t - 1, i, side],
                    z_next[sign],
                )

    y_copies = {}

    def y_stage(i):
        g = groups[i]
        for side in (1, 0):
            y = (yl, other)[side]
            total = part_ref[g, z, y].astype(F32) + ps_ref[i, z, y].astype(F32)
            for sign in (1, -1):
                chain[sign, 1, i, side].wait_recv()
                total += rb_ref[(sign + 1) // 2, 0, i, side].astype(F32)
            if side == 1:
                ys_ref[i] = total.astype(BF16)
                y_copies[i] = send(ys_ref.at[i], yr_ref.at[i], y_pair)
            else:
                fin_ref[i] = total

    weight_grad(2)
    weight_grad(3)
    swap = {1: send(part_ref.at[3 - core], ps_ref.at[1], sibling)}
    ring_step(4, 1)
    for copy in back:
        copy.wait_recv()
    for h in (0, 1):
        lanes = slice(128 * h, 128 * h + 128)
        for j, ref in ((0, dk_ref), (1, dv_ref)):
            low = ref[HALO : 2 * HALO, lanes] + hr_ref[h, j, 1].astype(F32)
            high = ref[2 * HALO : 3 * HALO, lanes] + hr_ref[h, j, 0].astype(F32)
            gp_ref[j, 0:HALO, lanes] = low.astype(BF16)
            gp_ref[j, HALO:TOK, lanes] = high.astype(BF16)

    yh, xx = tp // 4, lax.rem(tp, 4)
    y_other = (seq, (1 - yh) * 4 + xx)

    def x_at(e):
        return lax.rem(xx + e, 4)

    def x_peer(e):
        return (seq, yh * 4 + x_at(e))

    def block_at(e, p):
        return pl.ds(pl.multiple_of(x_at(e) * BLOCK + p * PART, PART), PART)

    def part_of(p):
        return pl.ds(p * PART, PART)

    def partial_norm(half, start, stop):
        rows = pl.ds(pl.multiple_of(half * 256, 256), 256)
        total = dot_nt(gp_ref[0, rows], weights(0)[start:stop])
        total += dot_nt(gp_ref[1, rows], weights(1)[start:stop])
        total += dot_nt(gp_ref[2, rows], weights(2)[start:stop])
        return total.astype(BF16)

    gb_ref[1 - yh] = partial_norm(1 - yh, CUT, D)
    y_first = {}
    for p in (0, 1):
        for e in (1, 3, 2, 0):
            src, dst = gb_ref.at[1 - yh, block_at(e, p)], rb1_ref.at[e, part_of(p)]
            y_first[e, p] = send(src, dst, y_other)
    for half in (0, 1):
        ga_ref[half] = partial_norm(half, 0, CUT)
    x_first = {}
    for p in (0, 1):
        for e in (1, 3, 2):
            src, dst = ga_ref.at[:, block_at(e, p)], ra1_ref.at[e - 1, :, part_of(p)]
            x_first[e, p] = send(src, dst, x_peer(e))
    gb_ref[yh] = partial_norm(yh, CUT, D)


    weight_grad(0)
    weight_grad(1)
    swap[0] = send(part_ref.at[1 - core], ps_ref.at[0], sibling)

    x_second, y_second = {}, {}

    def second_step(p):
        part = part_of(p)
        for e in (1, 3, 2):
            y_first[e, p].wait_recv()
            total = gb_ref[yh, block_at(e, p)].astype(F32) + rb1_ref[e, part].astype(F32)
            sb2_ref[e - 1, part] = total.astype(BF16)
            src, dst = sb2_ref.at[e - 1, part], rb2_ref.at[e - 1, part]
            x_second[e, p] = send(src, dst, x_peer(e))
        for e in (1, 3, 2):
            x_first[e, p].wait_recv()

        def sum_x(half):
            total = ga_ref[half, block_at(0, p)].astype(F32)
            for e in (1, 2, 3):
                total += ra1_ref[e - 1, half, part].astype(F32)
            return total

        sa2_ref[part] = sum_x(1 - yh).astype(BF16)
        y_second[p] = send(sa2_ref.at[part], ra2_ref.at[part], y_other)
        suma_ref[part] = sum_x(yh)

    def norm_back(i, _):
        rows = pl.ds(pl.multiple_of(tp * BLOCK + i * 16, 16), 16)
        part = pl.ds(pl.multiple_of(i * 16, 16), 16)
        own_part = pl.ds(pl.multiple_of(xx * BLOCK + i * 16, 16), 16)
        first = suma_ref[part] + ra2_ref[part].astype(F32)
        second = gb_ref[yh, own_part].astype(F32) + rb1_ref[0, part].astype(F32)
        for e in range(3):
            second += rb2_ref[e, part].astype(F32)
        total = jnp.concatenate([first, second], axis=1)
        wide = x_ref[rows].astype(F32)
        center = wide - jnp.mean(wide, axis=-1, keepdims=True)
        inv_std = lax.rsqrt(jnp.mean(center * center, axis=-1, keepdims=True) + 1e-06)
        normed = center * inv_std
        grad = inv_std * (
            total
            - jnp.mean(total, axis=-1, keepdims=True)
            - normed * jnp.mean(total * normed, axis=-1, keepdims=True)
        )
        gi_ref[rows] = grad.astype(BF16)
        return 0

    first, second = pl.ds(0, CUT), pl.ds(CUT, D - CUT)
    y_gather, x_gather, gather = {}, {}, []

    def share(y, x, p, columns, to):
        rows = pl.ds(pl.multiple_of((y * 4 + x) * BLOCK + p * PART, PART), PART)
        piece = gi_ref.at[rows, columns]
        return send(piece, piece, to)

    def finish(p):
        y_first[0, p].wait_recv()
        for e in (1, 3, 2):
            x_second[e, p].wait_recv()
        y_second[p].wait_recv()
        lax.fori_loop(2 * p, 2 * p + 2, norm_back, 0)
        y_gather[p] = share(yh, xx, p, first, y_other)
        for e in (1, 3, 2):
            x_gather[e, p] = share(yh, xx, p, second, x_peer(e))
        gather.append(share(yh, xx, p, second, y_other))
        for e in (1, 3, 2):
            gather.append(share(yh, xx, p, first, x_peer(e)))

    def forward(p):
        y_gather[p].wait_recv()
        for e in (1, 3, 2):
            gather.append(share(1 - yh, xx, p, first, x_peer(e)))
        for e in (1, 3, 2):
            x_gather[e, p].wait_recv()
            gather.append(share(yh, x_at(4 - e), p, second, y_other))

    ring_step(3, 1)
    ring_step(4, 0)
    second_step(0)
    ring_step(2, 1)
    second_step(1)
    ring_step(3, 0)
    finish(0)
    ring_step(1, 1)
    ring_step(2, 0)
    finish(1)
    y_stage(1)
    ring_step(1, 0)
    forward(0)
    forward(1)
    y_stage(0)
    own_rows = pl.ds(pl.multiple_of(56 * core, 8), 56)
    sib_rows = pl.ds(pl.multiple_of(56 * (1 - core), 8), 56)
    for i in (0, 1):
        y_copies[i].wait_recv()
        fin_ref[i] += yr_ref[i].astype(F32)
        fs_ref[i] = fin_ref[i, sib_rows]
        og_ref[groups[i]] = fin_ref[i, own_rows]
    last = send(fs_ref, fr_ref, sibling)
    last.wait_recv()
    og_ref[1 - core] = fr_ref[0]
    og_ref[3 - core] = fr_ref[1]
    for c, g in ((0, 2), (1, 0), (2, 1)):
        qkv_grad_ref[c] = close_up(og_ref[g])
    out_grad_ref[...] = close_up(og_ref[3])

    for copy in gather:
        copy.wait_recv()
    send.drain()


def publish(gi, qkv_grad, out_grad, gi_out, qkv_out, out_out, gi_buf, qkv_buf, out_buf, sems):
    moves = []
    for i in range(4):
        rows = pl.ds(i * (TOK // 4), TOK // 4)
        moves.append((gi.at[rows], gi_buf.at[rows], gi_out.at[rows]))
    moves.append((qkv_grad, qkv_buf, qkv_out))
    moves.append((out_grad, out_buf, out_out))
    loads, stores = [], []
    for i, (src, buf, dst) in enumerate(moves):
        loads.append(pltpu.make_async_copy(src, buf, sems.at[0, i]))
        stores.append(pltpu.make_async_copy(buf, dst, sems.at[1, i]))
        loads[-1].start()
    for load, store in zip(loads, stores):
        load.wait()
        store.start()
    for store in stores:
        store.wait()


def per_device(layer_input, grad_output, tile_image, qkv_weight, out_weight):
    vmem = pltpu.VMEM
    shapes = (
        jax.ShapeDtypeStruct((TOK, D), BF16),
        jax.ShapeDtypeStruct((3, 56, 2 * HD), F32),
        jax.ShapeDtypeStruct((56, 2 * HD), F32),
    )
    results = pl.pallas_call(
        kernel,
        out_shape=shapes,
        in_specs=[
            pl.BlockSpec(memory_space=pl.ANY),
            pl.BlockSpec(memory_space=pl.ANY),
            pl.BlockSpec(memory_space=pltpu.VMEM),
            pl.BlockSpec(memory_space=pltpu.VMEM),
            pl.BlockSpec(memory_space=pltpu.SMEM),
        ],
        out_specs=(
            pl.BlockSpec(memory_space=pltpu.VMEM),
            pl.BlockSpec(memory_space=pltpu.VMEM),
            pl.BlockSpec(memory_space=pltpu.VMEM),
        ),
        scratch_shapes=[
            vmem((4, 56, LANES), F32),
            vmem((TOK, D), BF16),
            vmem((TOK, D), BF16),
            vmem((8, 2, 2, 56, PACK), BF16),
            vmem((8, 2, 2, 56, 8 * HD - PACK), BF16),
            vmem((4, 8, 2, CHIP_ROWS, LANES), BF16),
            vmem((8, TOK, LANES), BF16),
            vmem((8, TOK, LANES), BF16),
            vmem((4, TOK, LANES), F32),
            vmem((8, 2 * CHIP_ROWS, TOK), BF16),
            vmem((8, 2 * CHIP_ROWS, TOK), BF16),
            vmem((PAD_TOK, LANES), BF16),
            vmem((PAD_TOK, LANES), BF16),
            vmem((TOK, LANES), BF16),
            vmem((TOK, LANES), BF16),
            vmem((PAD_TOK, LANES), F32),
            vmem((PAD_TOK, LANES), F32),
            vmem((2, 2, 2, HALO, 128), BF16),
            vmem((2, 2, 2, HALO, 128), BF16),
            vmem((4, TOK, LANES), BF16),
            vmem((4, 8, 2, CHIP_ROWS, LANES), BF16),
            vmem((2, 8, 2, CHIP_ROWS, LANES), BF16),
            vmem((2, 4, 2, 2, CHIP_ROWS, LANES), BF16),
            vmem((2, CHIP_ROWS, LANES), BF16),
            vmem((2, CHIP_ROWS, LANES), BF16),
            vmem((2, CHIP_ROWS, LANES), F32),
            vmem((2, 56, LANES), F32),
            vmem((2, 56, LANES), F32),
            vmem((2, 256, CUT), BF16),
            vmem((2, 256, D - CUT), BF16),
            vmem((3, 2, BLOCK, CUT), BF16),
            vmem((4, BLOCK, D - CUT), BF16),
            vmem((BLOCK, CUT), BF16),
            vmem((BLOCK, CUT), BF16),
            vmem((3, BLOCK, D - CUT), BF16),
            vmem((3, BLOCK, D - CUT), BF16),
            vmem((BLOCK, CUT), F32),
            vmem((2, 2, TOK, 256), F32),
            vmem((2, 2, TOK, 256), F32),
            pltpu.SemaphoreType.DMA((N_COPIES,)),
            pltpu.SemaphoreType.DMA((N_COPIES,)),
            pltpu.SemaphoreType.DMA((2,)),
        ],
        compiler_params=pltpu.CompilerParams(
            collective_id=0, has_side_effects=True, vmem_limit_bytes=56 << 20
        ),
        name="attention_backward",
    )(layer_input, grad_output, qkv_weight.transpose(1, 0, 2), out_weight, tile_image)
    grad_input, qkv_grad, out_grad = pl.pallas_call(
        publish,
        out_shape=shapes,
        in_specs=[pl.BlockSpec(memory_space=pl.ANY)] * 3,
        out_specs=[pl.BlockSpec(memory_space=pl.ANY)] * 3,
        scratch_shapes=[
            vmem((TOK, D), BF16),
            vmem((3, 56, 2 * HD), F32),
            vmem((56, 2 * HD), F32),
            pltpu.SemaphoreType.DMA((2, 6)),
        ],
        name="publish",
    )(*results)
    return (grad_input, qkv_grad.transpose(1, 0, 2), out_grad)


def solution(mesh):
    placed = (P("seq", None), P("seq", None), P(), P("seq", None, "tp"), P("seq", "tp"))
    return jax.shard_map(
        per_device,
        mesh=mesh,
        in_specs=placed,
        out_specs=(P("seq", None), P("seq", None, "tp"), P("seq", "tp")),
        check_vma=False,
    )
```
